512 devices in a mesh: real: 2 (over y_hi), gx: 64 (over z, x), gy: 4 (over y_lo, core).
Axes of the slice: x: 4, y: 4 (y_hi: 2, y_lo: 2; y = y_hi * 2 + y_lo), z: 16, core: 2. Of those that a mesh axis runs over, the one named last changes fastest.
Arguments:
- design: float32 [512, 16, 512], P('gx', 'real', 'gy'), may hold values from 0.05 to 0.95
- load: float32 [512, 16, 512], P('gx', 'real', 'gy'), may hold values from -6 to 6
- void_mask: int32 [512, 16, 512], P('gx', 'real', 'gy'), may hold values 0 or 1
- solid_mask: int32 [512, 16, 512], P('gx', 'real', 'gy'), may hold values 0 or 1
Outputs:
- sensitivity: float32 [512, 16, 512], P('gx', 'real', 'gy')
- compliance: float32 [3], replicated
The draws below stay inside these ranges and needn't reach their ends.
All inputs are finite; a program needn't handle non-finite values. No bound on the sum of `void_mask` or of `solid_mask` on one device may be relied on, other than what follows from the above.
Results may differ from the reference program's by a relative error of at most 0.0003.
Values sent between devices are 32-bit elements; how exact they have to be, the bound alone decides.
No kernel may reach another device: no remote copies, remote signals or barrier semaphores. Data moves between devices by JAX's collectives and lax.ppermute only.
A program may use at most 128 MiB of HBM per device.

```python
import jax
import jax.numpy as jnp

LEVELS = 4
NX = 512
NY = 16
NZ = 512


def touch_ends(drawn, own_key, low, top_value):
    index_at = [jax.random.randint(jax.random.fold_in(own_key, axis), (), 0, length) for axis, length in enumerate(drawn.shape)]
    main_axis = drawn.shape.index(max(drawn.shape))
    neighbour = index_at[:main_axis] + [(index_at[main_axis] + 1) % drawn.shape[main_axis]] + index_at[main_axis + 1:]
    return drawn.at[tuple(index_at)].set(low).at[tuple(neighbour)].set(top_value)


def levels(stream_key, shape, pieces, smallest, top_value):
    level, own = 1.0, jax.random.fold_in(stream_key, 6)
    for axis_at, blocks in pieces:
        draws = jnp.exp(jax.random.uniform(jax.random.fold_in(own, axis_at), (blocks,), jnp.float32, smallest / len(pieces), top_value / len(pieces)))
        level = level * jnp.repeat(draws, shape[axis_at] // blocks).reshape([-1 if axis == axis_at else 1 for axis in range(len(shape))])
    return level


def centred(rng, dims, deviation, most, pieces=(), held_as=jnp.bfloat16):
    drawn = jax.random.normal(rng, dims, jnp.float32) * deviation
    if len(pieces) > 0:
        drawn = levels(rng, dims, pieces, -0.22, 0.18) * drawn
    return jnp.clip(drawn, min=-most, max=most).astype(held_as)


def setup_inputs(seed: int = 0) -> dict:
    arg_keys = jax.random.split(jax.random.key(seed), 5)
    design = jnp.clip(0.05 + 0.9 * jax.random.uniform(arg_keys[0], (NX, NY, NZ), jnp.float32) ** levels(arg_keys[0], (NX, NY, NZ), ((0, 64), (1, 2), (2, 4)), -0.2, 0.2), 0.05, 0.95)
    load = centred(arg_keys[1], (NX, NY, NZ), 1.0, 6.0, ((0, 64), (1, 2), (2, 4)), jnp.float32)
    void_mask = touch_ends((jax.random.randint(arg_keys[2], (NX, NY, NZ), 0, 10) < 1).astype(jnp.int32), jax.random.fold_in(arg_keys[2], 1), 0, 1)
    solid_mask = touch_ends((jax.random.randint(arg_keys[3], (NX, NY, NZ), 0, 10) < 1).astype(jnp.int32), jax.random.fold_in(arg_keys[3], 1), 0, 1)
    return {"design": design, "load": load, "void_mask": void_mask, "solid_mask": solid_mask}


EMIN = 0.01
BETA = 8.0
OMEGA = 0.6
DIRECTIONS = ((-3, 1), (-3, -1), (-2, 1), (-2, -1), (-1, 1), (-1, -1))


def shifted(padded, along, offset):
    picker = [slice(None)] * padded.ndim
    for chosen_dim in (-3, -2, -1):
        extent = padded.shape[chosen_dim]
        if chosen_dim == along:
            picker[chosen_dim] = slice(1 + offset, extent - 1 + offset)
        else:
            picker[chosen_dim] = slice(1, extent - 1)
    return padded[tuple(picker)]


def zero_pad(values, width):
    return jnp.pad(values, [(0, 0)] * (values.ndim - 3) + [(width, width)] * 3)


def filter_apply(padded):
    total = 2.0 * shifted(padded, 0, 0)
    for along, offset in DIRECTIONS:
        total = total + shifted(padded, along, offset)
    return total


def conductances(padded, factor):
    middle = shifted(padded, 0, 0)
    return [factor * 0.5 * (middle + shifted(padded, along, offset)) for along, offset in DIRECTIONS]


def apply_operator(padded, links):
    middle = shifted(padded, 0, 0)
    total = jnp.zeros(middle.shape, jnp.float32)
    for link, (along, offset) in zip(links, DIRECTIONS):
        total = total + link * (middle - shifted(padded, along, offset))
    return total


def pool(values, span):
    shape_now = values.shape
    lead = shape_now[:-3]
    blocks = values.reshape(lead + (shape_now[-3] // span, span, shape_now[-2] // span, span, shape_now[-1] // span, span))
    return jnp.mean(blocks, axis=(-5, -3, -1))


def widen(values):
    return jnp.repeat(jnp.repeat(jnp.repeat(values, 2, -3), 2, -2), 2, -1)


def global_dot(first, second):
    return jnp.sum(first * second, axis=(-3, -2, -1), keepdims=True)


def reference(design, load, void_mask, solid_mask):
    smoothed = filter_apply(zero_pad(jnp.stack([design, jnp.ones_like(design)]), 1))
    weights = smoothed[1]
    filtered = smoothed[0] / weights
    etas = jnp.array([0.7, 0.5, 0.3], jnp.float32).reshape(3, 1, 1, 1)
    tanh_eta = jnp.tanh(BETA * etas)
    denominator = tanh_eta + jnp.tanh(BETA * (1.0 - etas))
    inner_tanh = jnp.tanh(BETA * (filtered[None] - etas))
    projected = (tanh_eta + inner_tanh) / denominator
    slope = BETA * (1.0 - inner_tanh * inner_tanh) / denominator
    voids = void_mask.astype(jnp.float32)
    solids = solid_mask.astype(jnp.float32)
    physical = (1.0 - voids) * (solids + (1.0 - solids) * projected)
    stiffness = EMIN + (1.0 - EMIN) * physical ** 3
    operators = []
    level_field = stiffness
    for depth_level in range(LEVELS):
        if depth_level > 0:
            level_field = pool(level_field, 2)
        links = conductances(zero_pad(level_field, 1), 0.25 ** depth_level)
        diag_sum = links[0]
        for link in links[1:]:
            diag_sum = diag_sum + link
        operators.append((links, diag_sum))

    def precondition(rhs, depth_level):
        links, diag_sum = operators[depth_level]
        approx = OMEGA * rhs / diag_sum
        if depth_level < LEVELS - 1:
            leftover = rhs - apply_operator(zero_pad(approx, 1), links)
            approx = approx + widen(precondition(pool(leftover, 2), depth_level + 1))
        return approx + OMEGA * (rhs - apply_operator(zero_pad(approx, 1), links)) / diag_sum

    fine_links = operators[0][0]
    residual = jnp.broadcast_to(load, (3,) + load.shape)
    state = jnp.zeros(residual.shape, jnp.float32)
    precond = precondition(residual, 0)
    direction = precond
    rz_now = global_dot(residual, precond)
    for step in range(2):
        image = apply_operator(zero_pad(direction, 1), fine_links)
        alpha = rz_now / global_dot(direction, image)
        state = state + alpha * direction
        residual = residual - alpha * image
        if step == 0:
            precond = precondition(residual, 0)
            rz_next = global_dot(residual, precond)
            direction = precond + (rz_next / rz_now) * direction
            rz_now = rz_next
    compliance = global_dot(load[None], state).reshape(3)
    state_pad = zero_pad(state, 1)
    middle = shifted(state_pad, 0, 0)
    dcde = jnp.zeros(state.shape, jnp.float32)
    for along, offset in DIRECTIONS:
        gap = middle - shifted(state_pad, along, offset)
        dcde = dcde - 0.5 * gap * gap
    combined = jnp.sum(dcde * 3.0 * physical * physical * (1.0 - EMIN) * (1.0 - voids) * (1.0 - solids) * slope, axis=0)
    sensitivity = filter_apply(zero_pad(combined / weights, 1))
    return sensitivity, compliance
```

```python
import jax
import jax.numpy as jnp
from jax import lax
from jax.experimental import pallas as pl
from jax.experimental.pallas import tpu as pltpu
from jax.sharding import Mesh
from jax.sharding import PartitionSpec as P

EMIN = 0.01
BETA = 8.0
OMEGA = 0.6
ETAS = (0.7, 0.5, 0.3)
NBX = 64
VMEM_LIMIT = 48 * 1024 * 1024
F32 = jnp.float32
HI = lax.Precision.HIGHEST


def call(body, out_shape, scratch=(), flops=1000000):
    return pl.pallas_call(
        body,
        out_shape=out_shape,
        scratch_shapes=list(scratch),
        compiler_params=pltpu.CompilerParams(vmem_limit_bytes=VMEM_LIMIT),
        cost_estimate=pl.CostEstimate(flops=flops, bytes_accessed=1000000, transcendentals=0),
    )


def shaped(*dims):
    return jax.ShapeDtypeStruct(dims, F32)


def rolled(v, amount, axis):
    return pltpu.roll(v, amount % v.shape[axis], axis)


def iota(shape, axis):
    return lax.broadcasted_iota(jnp.int32, shape, axis)


def pool_matrix():
    return (iota((256, 128), 0) // 2 == iota((256, 128), 1)).astype(F32)


def widen_matrix():
    return (iota((128, 256), 1) // 2 == iota((128, 256), 0)).astype(F32)


def y_edges(rows, stride):
    y = iota((rows, 1), 0)
    low = (y >= stride).astype(F32)
    outer = 0.5 * ((y < stride).astype(F32) + (y >= rows - stride).astype(F32))
    return low, outer


def face_y(e, low, stride):
    return 0.5 * low * (e + rolled(e, stride, e.ndim - 2))


def face_z(e, stride):
    return 0.5 * (e + rolled(e, stride, e.ndim - 1))


def through(c, u, stride, axis):
    flow = c * (u - rolled(u, stride, axis))
    return flow - rolled(flow, -stride, axis)


def operate(prev, u, after, cx, cx_after, cy, cz, side, stride):
    n = u.ndim
    total = cx * (u - prev) - cx_after * (after - u)
    total = total + through(cy, u, stride, n - 2) + through(cz, u, stride, n - 1)
    return total + side * u


def inverse(e, diag):
    return jnp.where(e > 0.0, 1.0 / jnp.where(e > 0.0, diag, 1.0), 0.0)


def prepare(e_ref, cx_ref, cy_ref, cz_ref, inv_ref, first, last):
    low, outer = y_edges(16, 1)

    def step(i, _):
        for r in range(3):
            e = e_ref[r, i]
            cx = 0.5 * (e + e_ref[r, i - 1])
            cx_after = 0.5 * (e + e_ref[r, i + 1])
            cy = face_y(e, low, 1)
            cz = face_z(e, 1)
            diag = cx + cx_after + (cy + rolled(cy, -1, 0)) + (cz + rolled(cz, -1, 1)) + outer * e
            cx_ref[r, i] = cx
            cy_ref[r, i] = cy
            cz_ref[r, i] = cz
            inv_ref[r, i] = inverse(e, diag)
        return 0

    lax.fori_loop(first, last, step, 0)
    for r in range(3):
        cx_ref[r, last] = 0.5 * (e_ref[r, last] + e_ref[r, last - 1])


def operate0(u_ref, i, r, e_ref, cx_ref, cy_ref, cz_ref, outer):
    return operate(
        u_ref[r, i - 1], u_ref[r, i], u_ref[r, i + 1],
        cx_ref[r, i], cx_ref[r, i + 1], cy_ref[r, i], cz_ref[r, i], outer * e_ref[r, i], 1,
    )


def pool_own(src_of, many, big_ref, half_ref, scale):
    for f in range(many):
        for k in range(4):
            at = (f * 4 + k) * 16
            big_ref[at : at + 16, :] = (0.125 * scale) * (src_of(f, 8 + 2 * k) + src_of(f, 9 + 2 * k))
    rows = many * 64
    half_ref[0:rows, :] = jnp.dot(big_ref[0:rows, :], pool_matrix(), precision=HI, preferred_element_type=F32)
    return half_ref[pl.ds(0, rows // 2, stride=2), :] + half_ref[pl.ds(1, rows // 2, stride=2), :]


def stack_level(e, stride):
    low, outer = y_edges(8, stride)
    before = jnp.concatenate([e[:1], e[:-1]], 0)
    cx = 0.5 * (e + before)
    cx_after = jnp.concatenate([cx[1:], cx[:1]], 0)
    cy = face_y(e, low[None], stride)
    cz = face_z(e, stride)
    side = outer[None] * e
    diag = cx + cx_after + (cy + rolled(cy, -stride, 1)) + (cz + rolled(cz, -stride, 2)) + side
    return cx, cx_after, cy, cz, side, inverse(e, diag)


def stack_operate(level, u, stride):
    cx, cx_after, cy, cz, side, _ = level
    before = jnp.concatenate([u[:1], u[:-1]], 0)
    after = jnp.concatenate([u[1:], u[-1:]], 0)
    return operate(before, u, after, cx, cx_after, cy, cz, side, stride)


def stack_pool(v, stride):
    n = v.shape[0] // 2
    v = v.reshape(n, 2, 8, 128)
    v = v[:, 0] + v[:, 1]
    y = iota((1, 8, 1), 1)
    v = v + jnp.where((y // stride) % 2 == 0, rolled(v, -stride, 1), rolled(v, stride, 1))
    z = iota((1, 1, 128), 2)
    v = v + jnp.where((z // stride) % 2 == 0, rolled(v, -stride, 2), rolled(v, stride, 2))
    return 0.125 * v


def twice(v):
    n = v.shape[0]
    return jnp.broadcast_to(v[:, None], (n, 2, 8, 128)).reshape(2 * n, 8, 128)


def coarse(e1, rhs1):
    e2 = 0.25 * stack_pool(e1, 1)
    e3 = 0.25 * stack_pool(e2, 2)
    one, two, three = stack_level(e1, 1), stack_level(e2, 2), stack_level(e3, 4)
    x1 = OMEGA * rhs1 * one[5]
    rhs2 = stack_pool(rhs1 - stack_operate(one, x1, 1), 1)
    x2 = OMEGA * rhs2 * two[5]
    rhs3 = stack_pool(rhs2 - stack_operate(two, x2, 2), 2)
    x3 = OMEGA * rhs3 * three[5]
    x3 = x3 + OMEGA * (rhs3 - stack_operate(three, x3, 4)) * three[5]
    x2 = x2 + twice(x3)
    x2 = x2 + OMEGA * (rhs2 - stack_operate(two, x2, 2)) * two[5]
    x1 = x1 + twice(x2)
    return x1 + OMEGA * (rhs1 - stack_operate(one, x1, 1)) * one[5]


def coarse_all(e1_ref, rhs1_ref, out_ref):
    def step(r, _):
        out_ref[r] = coarse(e1_ref[r], rhs1_ref[r])
        return 0

    lax.fori_loop(0, 3, step, 0)


def widen_into(e1_ref, first, count, wide_ref):
    rows = 3 * count * 8
    src = jnp.concatenate([e1_ref[r, first : first + count].reshape(count * 8, 128) for r in range(3)], 0)
    wide = jnp.dot(src, widen_matrix(), precision=HI, preferred_element_type=F32)
    for h in range(2):
        part = wide[:, 128 * h : 128 * h + 128]
        wide_ref[h, pl.ds(0, rows, stride=2), :] = part
        wide_ref[h, pl.ds(1, rows, stride=2), :] = part


def widened(wide_ref, r, k, count):
    at = pl.multiple_of((r * count + k) * 16, 16)
    return jnp.concatenate([wide_ref[0, pl.ds(at, 16), :], wide_ref[1, pl.ds(at, 16), :]], 1)


REACH = (7, 6, 6, 5)
OFFS = (0, 7, 13, 19)


def select_kernel(c_ref, l_ref, r_ref, own_ref, up_ref, down_ref):
    right = iota((8, 128), 1) < 64
    for f in range(4):
        for i in range(8):
            for h in range(2):
                halo = jnp.where(right, r_ref[h, f, i], l_ref[h, f, i])
                piece = jnp.concatenate([c_ref[h, f, i], halo], 1)
                own_ref[f, i, 8 * h : 8 * h + 8, :] = piece
                if i >= 8 - REACH[f]:
                    up_ref[OFFS[f] + i - (8 - REACH[f]), 8 * h : 8 * h + 8, :] = piece
                if i < REACH[f]:
                    down_ref[OFFS[f] + i, 8 * h : 8 * h + 8, :] = piece


def first_kernel(
    place_ref, own_ref, lo_ref, hi_ref, e_ref, f_ref, load_ref, g_ref,
    d_ref, v_ref, s_ref, cx_ref, cy_ref, cz_ref, inv_ref, x_ref, rest_ref, big_ref, half_ref,
):
    block, gy = place_ref[0], place_ref[1]
    for f, ref in enumerate((d_ref, v_ref, s_ref, load_ref)):
        n = REACH[f]
        for j in range(n):
            ref[8 - n + j] = lo_ref[OFFS[f] + j]
            ref[16 + j] = hi_ref[OFFS[f] + j]
        for j in range(8):
            ref[8 + j] = own_ref[f, j]
    lane = iota((1, 256), 1)
    z = gy * 128 + jnp.where(lane < 192, lane, lane - 256)
    z_in = ((z >= 0) & (z < 512)).astype(F32)
    z_count = ((z >= 1) & (z < 513)).astype(F32) + ((z >= -1) & (z < 511)).astype(F32)
    y = iota((16, 1), 0)
    low, high = (y >= 1).astype(F32), (y < 15).astype(F32)
    yz_count = (low + high) + z_count
    shifts = [(jnp.tanh(jnp.full((1, 1), BETA * eta, F32)), jnp.tanh(jnp.full((1, 1), BETA * (1.0 - eta), F32))) for eta in ETAS]

    def step(i, _):
        x = 8 * block + i - 8
        inside = lambda at: ((at >= 0) & (at < 8 * NBX)).astype(F32)
        d = d_ref[i]
        total = 2.0 * d + d_ref[i + 1] + d_ref[i - 1]
        total = total + low * rolled(d, 1, 0) + high * rolled(d, -1, 0) + rolled(d, 1, 1) + rolled(d, -1, 1)
        weights = yz_count + (2.0 + inside(x - 1) + inside(x + 1))
        here = z_in * inside(x)
        filtered = total / weights
        void, solid = v_ref[i], s_ref[i]
        open_ = 1.0 - void
        free = open_ * (1.0 - solid)
        scale = here * free / weights
        for r, eta in enumerate(ETAS):
            t0, t1 = shifts[r]
            den = t0 + t1
            t = jnp.tanh(BETA * (filtered - eta))
            projected = (t0 + t) / den
            slope = BETA * (1.0 - t * t) / den
            physical = open_ * (solid + (1.0 - solid) * projected)
            square = physical * physical
            e_ref[r, i] = here * (EMIN + (1.0 - EMIN) * (square * physical))
            f_ref[r, i] = (3.0 * (1.0 - EMIN)) * square * scale * slope
        return 0

    lax.fori_loop(2, 22, step, 0)
    prepare(e_ref, cx_ref, cy_ref, cz_ref, inv_ref, 7, 17)

    def start(i, _):
        for r in range(3):
            x_ref[r, i] = OMEGA * load_ref[i] * inv_ref[r, i]
        return 0

    lax.fori_loop(7, 17, start, 0)
    _, outer = y_edges(16, 1)

    def leftover(i, _):
        for r in range(3):
            rest_ref[r, i - 8] = load_ref[i] - operate0(x_ref, i, r, e_ref, cx_ref, cy_ref, cz_ref, outer)
        return 0

    lax.fori_loop(8, 16, leftover, 0)
    g_ref[0:3] = pool_own(lambda f, i: rest_ref[f, i - 8], 3, big_ref, half_ref, 1.0).reshape(3, 4, 8, 128)
    g_ref[3:6] = pool_own(lambda f, i: e_ref[f, i], 3, big_ref, half_ref, 0.25).reshape(3, 4, 8, 128)


def triple_kernel(lo_ref, c_ref, hi_ref, out_ref):
    out_ref[0] = lo_ref[...]
    out_ref[1] = c_ref[...]
    out_ref[2] = hi_ref[...]


def window(refs, block, first, into_ref, index):
    for b in range(9):
        at = block - 4 + b
        keep = ((at >= 0) & (at < NBX)).astype(F32)
        for r in range(3):
            into_ref[r, 4 * b : 4 * b + 4] = keep * refs[b // 3][b % 3, first + r]


def second_kernel(
    place_ref, e_ref, load_ref, lo_ref, c_ref, hi_ref, e1_ref, z0_ref, q0_ref, g_ref,
    cx_ref, cy_ref, cz_ref, inv_ref, x_ref, y_ref, rhs_ref, out1_ref, wide_ref, big_ref, half_ref,
):
    block = place_ref[0]
    refs = (lo_ref, c_ref, hi_ref)
    window(refs, block, 0, rhs_ref, 0)
    window(refs, block, 3, e1_ref, 0)
    prepare(e_ref, cx_ref, cy_ref, cz_ref, inv_ref, 3, 21)
    coarse_all(e1_ref, rhs_ref, out1_ref)
    widen_into(out1_ref, 13, 10, wide_ref)
    _, outer = y_edges(16, 1)

    def start(i, _):
        for r in range(3):
            x_ref[r, i] = OMEGA * load_ref[i] * inv_ref[r, i] + widened(wide_ref, r, (i - 2) // 2, 10)
        return 0

    lax.fori_loop(3, 21, start, 0)

    def smooth(i, _):
        for r in range(3):
            image = operate0(x_ref, i, r, e_ref, cx_ref, cy_ref, cz_ref, outer)
            z0_ref[r, i] = x_ref[r, i] + OMEGA * (load_ref[i] - image) * inv_ref[r, i]
        return 0

    lax.fori_loop(4, 20, smooth, 0)

    def apply(i, _):
        for r in range(3):
            image = operate0(z0_ref, i, r, e_ref, cx_ref, cy_ref, cz_ref, outer)
            q0_ref[r, i] = image
            y_ref[r, i] = OMEGA * image * inv_ref[r, i]
        return 0

    lax.fori_loop(5, 19, apply, 0)

    def leftover(i, _):
        for r in range(3):
            x_ref[r, i] = q0_ref[r, i] - operate0(y_ref, i, r, e_ref, cx_ref, cy_ref, cz_ref, outer)
        return 0

    lax.fori_loop(8, 16, leftover, 0)
    g_ref[...] = pool_own(lambda f, i: x_ref[f, i], 3, big_ref, half_ref, 1.0).reshape(3, 4, 8, 128)


def third_kernel(
    place_ref, e_ref, load_ref, e1_ref, z0_ref, q0_ref, lo_ref, c_ref, hi_ref, w_ref, dots_ref,
    cx_ref, cy_ref, cz_ref, inv_ref, x_ref, rhs_ref, out1_ref, wide_ref,
):
    block = place_ref[0]
    window((lo_ref, c_ref, hi_ref), block, 0, rhs_ref, 0)
    prepare(e_ref, cx_ref, cy_ref, cz_ref, inv_ref, 5, 19)
    coarse_all(e1_ref, rhs_ref, out1_ref)
    widen_into(out1_ref, 14, 8, wide_ref)
    _, outer = y_edges(16, 1)

    def start(i, _):
        for r in range(3):
            x_ref[r, i] = OMEGA * q0_ref[r, i] * inv_ref[r, i] + widened(wide_ref, r, (i - 4) // 2, 8)
        return 0

    lax.fori_loop(5, 19, start, 0)

    def smooth(i, _):
        for r in range(3):
            image = operate0(x_ref, i, r, e_ref, cx_ref, cy_ref, cz_ref, outer)
            w_ref[r, i] = x_ref[r, i] + OMEGA * (q0_ref[r, i] - image) * inv_ref[r, i]
        return 0

    lax.fori_loop(6, 18, smooth, 0)

    def add(i, sums):
        new = []
        for r in range(3):
            image = operate0(w_ref, i, r, e_ref, cx_ref, cy_ref, cz_ref, outer)[:, :128]
            b, z0, q0, w = load_ref[i, :, :128], z0_ref[r, i, :, :128], q0_ref[r, i, :, :128], w_ref[r, i, :, :128]
            for q, term in enumerate((b * z0, z0 * q0, b * w, q0 * w, w * image)):
                new.append(sums[r * 5 + q] + (term[:8] + term[8:]))
        return tuple(new)

    sums = lax.fori_loop(8, 16, add, tuple(jnp.zeros((8, 128), F32) for _ in range(15)))
    rows = [jnp.sum(v, 0, keepdims=True) for v in sums] + [jnp.zeros((1, 128), F32)]
    tile = jnp.concatenate(rows, 0)
    for d in range(16):
        dots_ref[d] = tile


def sum_kernel(in_ref, out_ref):
    tile = jnp.sum(in_ref[...], 0)
    for d in range(16):
        out_ref[d] = tile


def last_kernel(place_ref, f_ref, z0_ref, w_ref, dots_ref, sens_ref, comp_ref, u_ref, comb_ref):
    real = place_ref[2]
    totals = jnp.sum(jnp.sum(dots_ref[...], 0), 1, keepdims=True)
    factors = []
    for r in range(3):
        bz, zq, bw, qw, wa = (totals[r * 5 + q : r * 5 + q + 1] for q in range(5))
        a0 = bz / zq
        rz1 = bz - a0 * bw - a0 * zq + (a0 * a0) * qw
        grow = 1.0 + rz1 / bz
        a1 = rz1 / ((grow * grow) * zq - 2.0 * (a0 * grow) * qw + (a0 * a0) * wa)
        c0, c1 = a0 + a1 * grow, -(a1 * a0)
        factors.append((c0, c1))
        comp_ref[r : r + 1, :] = jnp.broadcast_to(c0 * bz + c1 * bw, (1, 128))
    comp_ref[3:8, :] = jnp.zeros((5, 128), F32)
    y = iota((16, 1), 0)
    low, high = (y >= 1).astype(F32), (y < 15).astype(F32)

    def state(i, _):
        for r in range(3):
            u_ref[r, i] = factors[r][0] * z0_ref[r, i] + factors[r][1] * w_ref[r, i]
        return 0

    lax.fori_loop(6, 18, state, 0)

    def energy(i, _):
        total = jnp.zeros((16, 256), F32)
        for r in range(3):
            u = u_ref[r, i]
            gaps = (
                u - u_ref[r, i - 1],
                u - u_ref[r, i + 1],
                u - low * rolled(u, 1, 0),
                u - high * rolled(u, -1, 0),
                u - rolled(u, 1, 1),
                u - rolled(u, -1, 1),
            )
            square = gaps[0] * gaps[0]
            for gap in gaps[1:]:
                square = square + gap * gap
            total = total - (0.5 * square) * f_ref[r, i]
        comb_ref[i] = total
        return 0

    lax.fori_loop(7, 17, energy, 0)

    def spread(i, _):
        c = comb_ref[i]
        total = 2.0 * c + comb_ref[i + 1] + comb_ref[i - 1]
        total = total + low * rolled(c, 1, 0) + high * rolled(c, -1, 0) + rolled(c, 1, 1) + rolled(c, -1, 1)
        sens_ref[i - 8] = jnp.where(real == 0, total[:8, :128], total[8:, :128])
        return 0

    lax.fori_loop(8, 16, spread, 0)


def kernel_call(body, outs, scratch, place, *args, flops=1000000):
    return pl.pallas_call(
        body,
        out_shape=outs,
        in_specs=[pl.BlockSpec(memory_space=pltpu.SMEM)] + [pl.BlockSpec(memory_space=pltpu.VMEM)] * len(args),
        scratch_shapes=[pltpu.VMEM(dims, F32) for dims in scratch],
        compiler_params=pltpu.CompilerParams(vmem_limit_bytes=VMEM_LIMIT),
    )(place, *args)


X_AXES = ("zc", "xc")
Y_AXES = ("yl", "core")
FIELD = (3, 24, 16, 256)
LEVEL1 = (3, 36, 8, 128)


def neighbours(count, step, wrap):
    return [(i, (i + step) % count) for i in range(count) if wrap or 0 <= i + step < count]


def reach(own):
    lo = lax.ppermute(own, X_AXES, neighbours(NBX, 1, True))
    hi = lax.ppermute(own, X_AXES, neighbours(NBX, -1, True))
    triple = call(triple_kernel, shaped(3, *own.shape))(lo, own, hi)
    return (
        lax.ppermute(triple, X_AXES, neighbours(NBX, 3, True)),
        triple,
        lax.ppermute(triple, X_AXES, neighbours(NBX, -3, True)),
    )


def body(design, load, void_mask, solid_mask):
    place = jnp.stack([lax.axis_index(X_AXES), lax.axis_index(Y_AXES), lax.axis_index("real")]).astype(jnp.int32)
    own = jnp.stack([design, void_mask.astype(F32), solid_mask.astype(F32), load])
    both = lax.all_gather(own, "real")
    left = lax.ppermute(both, Y_AXES, neighbours(4, 1, False))
    right = lax.ppermute(both, Y_AXES, neighbours(4, -1, False))
    mine, up, down = call(select_kernel, (shaped(4, 8, 16, 256), shaped(24, 16, 256), shaped(24, 16, 256)))(both, left, right)
    lo = lax.ppermute(up, X_AXES, neighbours(NBX, 1, False))
    hi = lax.ppermute(down, X_AXES, neighbours(NBX, -1, False))
    one = (24, 16, 256)
    e, f, wide_load, g = kernel_call(
        first_kernel,
        (shaped(*FIELD), shaped(*FIELD), shaped(*one), shaped(6, 4, 8, 128)),
        [one] * 3 + [FIELD] * 5 + [(3, 8, 16, 256), (192, 256), (192, 128)],
        place, mine, lo, hi,
    )
    e1, z0, q0, g2 = kernel_call(
        second_kernel,
        (shaped(*LEVEL1), shaped(*FIELD), shaped(*FIELD), shaped(3, 4, 8, 128)),
        [FIELD] * 6 + [LEVEL1] * 2 + [(2, 480, 128), (192, 256), (192, 128)],
        place, e, wide_load, *reach(g),
    )
    w, dots = kernel_call(
        third_kernel,
        (shaped(*FIELD), shaped(16, 16, 128)),
        [FIELD] * 5 + [LEVEL1] * 2 + [(2, 384, 128)],
        place, e, wide_load, e1, z0, q0, *reach(g2),
    )
    dots = lax.all_to_all(dots, ("xc", "yl", "core"), 0, 0, tiled=True)
    dots = call(sum_kernel, shaped(16, 16, 128))(dots)
    dots = lax.all_to_all(dots, "zc", 0, 0, tiled=True)
    sens, comp = kernel_call(
        last_kernel,
        (shaped(8, 8, 128), shaped(8, 128)),
        [FIELD, one],
        place, f, z0, w, dots,
    )
    return sens, comp[:3, 0]


def solution(mesh):
    split = Mesh(mesh.devices.reshape(2, 16, 4, 2, 2), ("real", "zc", "xc", "yl", "core"))
    spec = P(X_AXES, "real", Y_AXES)
    return jax.shard_map(body, mesh=split, in_specs=(spec,) * 4, out_specs=(spec, P()), check_vma=False)
```

```python
import jax
import jax.numpy as jnp
from jax import lax
from jax.experimental import pallas as pl
from jax.experimental.pallas import tpu as pltpu
from jax.sharding import Mesh
from jax.sharding import PartitionSpec as P

EMIN = 0.01
BETA = 8.0
OMEGA = 0.6
ETAS = (0.7, 0.5, 0.3)
NBX = 64
VMEM_LIMIT = 16 * 1024 * 1024
F32 = jnp.float32
HI = lax.Precision.HIGHEST


GROUP = 4


def loop(first, last, step, group=None):
    group = group or GROUP
    turns = (last - first) // group

    def turn(t, _):
        for j in range(group):
            step(first + t * group + j)
        return 0

    lax.fori_loop(0, turns, turn, 0)
    for i in range(first + turns * group, last):
        step(i)


def shaped(*dims):
    return jax.ShapeDtypeStruct(dims, F32)


def rolled(v, amount, axis):
    return pltpu.roll(v, amount % v.shape[axis], axis)


def iota(shape, axis):
    return lax.broadcasted_iota(jnp.int32, shape, axis)


def pool_matrix():
    return (iota((256, 128), 0) // 2 == iota((256, 128), 1)).astype(F32)


def widen_matrix():
    return (iota((128, 256), 1) // 2 == iota((128, 256), 0)).astype(F32)


def y_edges(rows, stride):
    y = iota((rows, 1), 0)
    low = (y >= stride).astype(F32)
    outer = 0.5 * ((y < stride).astype(F32) + (y >= rows - stride).astype(F32))
    return low, outer


def face_y(e, low, stride):
    return 0.5 * low * (e + rolled(e, stride, e.ndim - 2))


def face_z(e, stride):
    return 0.5 * (e + rolled(e, stride, e.ndim - 1))


def through(c, u, stride, axis):
    flow = c * (u - rolled(u, stride, axis))
    return flow - rolled(flow, -stride, axis)


def operate(prev, u, after, cx, cx_after, cy, cz, side, stride):
    n = u.ndim
    total = cx * (u - prev) - cx_after * (after - u)
    total = total + through(cy, u, stride, n - 2) + through(cz, u, stride, n - 1)
    return total + side * u


def inverse(e, diag):
    return jnp.where(e > 0.0, 1.0 / jnp.where(e > 0.0, diag, 1.0), 0.0)


def prepare(e_ref, cx_ref, cy_ref, cz_ref, inv_ref, first, last):
    low, outer = y_edges(16, 1)

    def step(i):
        for r in range(3):
            e = e_ref[r, i]
            cx = 0.5 * (e + e_ref[r, i - 1])
            cx_after = 0.5 * (e + e_ref[r, i + 1])
            cy = face_y(e, low, 1)
            cz = face_z(e, 1)
            diag = cx + cx_after + (cy + rolled(cy, -1, 0)) + (cz + rolled(cz, -1, 1)) + outer * e
            cx_ref[r, i] = cx
            cy_ref[r, i] = cy
            cz_ref[r, i] = cz
            inv_ref[r, i] = inverse(e, diag)

    loop(first, last, step)
    for r in range(3):
        cx_ref[r, last] = 0.5 * (e_ref[r, last] + e_ref[r, last - 1])


def operate0(u_ref, i, r, e_ref, cx_ref, cy_ref, cz_ref, outer):
    return operate(
        u_ref[r, i - 1], u_ref[r, i], u_ref[r, i + 1],
        cx_ref[r, i], cx_ref[r, i + 1], cy_ref[r, i], cz_ref[r, i], outer * e_ref[r, i], 1,
    )


def pool_own(src_of, many, big_ref, half_ref, scale):
    for f in range(many):
        for k in range(4):
            at = (f * 4 + k) * 16
            big_ref[at : at + 16, :] = (0.125 * scale) * (src_of(f, 8 + 2 * k) + src_of(f, 9 + 2 * k))
    rows = many * 64
    half_ref[0:rows, :] = jnp.dot(big_ref[0:rows, :], pool_matrix(), precision=HI, preferred_element_type=F32)
    return half_ref[pl.ds(0, rows // 2, stride=2), :] + half_ref[pl.ds(1, rows // 2, stride=2), :]


def stack_level(e, stride):
    low, outer = y_edges(8, stride)
    before = jnp.concatenate([e[:1], e[:-1]], 0)
    cx = 0.5 * (e + before)
    cx_after = jnp.concatenate([cx[1:], cx[:1]], 0)
    cy = face_y(e, low[None], stride)
    cz = face_z(e, stride)
    side = outer[None] * e
    diag = cx + cx_after + (cy + rolled(cy, -stride, 1)) + (cz + rolled(cz, -stride, 2)) + side
    return cx, cx_after, cy, cz, side, inverse(e, diag)


def stack_operate(level, u, stride, first, last):
    cx, cx_after, cy, cz, side, _ = (v[first:last] for v in level)
    return operate(u[:-2], u[1:-1], u[2:], cx, cx_after, cy, cz, side, stride)


def stack_pool(v, stride):
    n = v.shape[0] // 2
    v = v.reshape(n, 2, 8, 128)
    v = v[:, 0] + v[:, 1]
    y = iota((1, 8, 1), 1)
    v = v + jnp.where((y // stride) % 2 == 0, rolled(v, -stride, 1), rolled(v, stride, 1))
    z = iota((1, 1, 128), 2)
    v = v + jnp.where((z // stride) % 2 == 0, rolled(v, -stride, 2), rolled(v, stride, 2))
    return 0.125 * v


def twice(v):
    n = v.shape[0]
    return jnp.broadcast_to(v[:, None], (n, 2, 8, 128)).reshape(2 * n, 8, 128)


STRIDES = (1, 2, 4)


def set_levels(e1_ref, level_refs):
    def step(r, _):
        e = e1_ref[r]
        for ref, stride in zip(level_refs, STRIDES):
            for q, v in enumerate(stack_level(e, stride)):
                ref[q, r] = v
            e = 0.25 * stack_pool(e, stride) if stride < 4 else e
        return 0

    lax.fori_loop(0, 3, step, 0)


def coarse(levels, rhs1, first, last):
    one, two, three = levels
    x1 = OMEGA * rhs1 * one[5]
    rest1 = rhs1[2:34] - stack_operate(one, x1[1:35], 1, 2, 34)
    rhs2 = stack_pool(rest1, 1)
    x2 = OMEGA * rhs2 * two[5][1:17]
    rest2 = rhs2[1:15] - stack_operate(two, x2, 2, 2, 16)
    rhs3 = stack_pool(rest2, 2)
    x3 = OMEGA * rhs3 * three[5][1:8]
    x3 = x3[1:6] + OMEGA * (rhs3[1:6] - stack_operate(three, x3, 4, 2, 7)) * three[5][2:7]
    x2 = x2[3:13] + twice(x3)
    x2 = x2[1:9] + OMEGA * (rhs2[4:12] - stack_operate(two, x2, 2, 5, 13)) * two[5][5:13]
    x1 = x1[10:26] + twice(x2)
    x1, at = x1[first - 11 : last - 9], slice(first, last)
    return x1[1:-1] + OMEGA * (rhs1[at] - stack_operate(one, x1, 1, first, last)) * one[5][at]


def coarse_all(level_refs, rhs1_ref, out_ref, first, last):
    def step(r, _):
        levels = [[ref[q, r] for q in range(6)] for ref in level_refs]
        out_ref[r, 0 : last - first] = coarse(levels, rhs1_ref[r], first, last)
        return 0

    lax.fori_loop(0, 3, step, 0)


def widen_into(e1_ref, count, wide_ref):
    rows = 3 * count * 8
    src = jnp.concatenate([e1_ref[r, :count].reshape(count * 8, 128) for r in range(3)], 0)
    wide = jnp.dot(src, widen_matrix(), precision=HI, preferred_element_type=F32)
    for h in range(2):
        part = wide[:, 128 * h : 128 * h + 128]
        wide_ref[h, pl.ds(0, rows, stride=2), :] = part
        wide_ref[h, pl.ds(1, rows, stride=2), :] = part


def widened(wide_ref, r, k, count):
    at = pl.multiple_of((r * count + k) * 16, 16)
    return jnp.concatenate([wide_ref[0, pl.ds(at, 16), :], wide_ref[1, pl.ds(at, 16), :]], 1)


REACH = (7, 6, 6, 5)
OFFS = (0, 7, 13, 19)


def pack_kernel(d_ref, v_ref, s_ref, load_ref, out_ref):
    out_ref[0] = d_ref[...]
    out_ref[1] = v_ref[...].astype(F32)
    out_ref[2] = s_ref[...].astype(F32)
    out_ref[3] = load_ref[...]


def select_kernel(c_ref, l_ref, r_ref, own_ref, up_ref, down_ref):
    right = iota((8, 128), 1) < 64
    for f in range(4):
        for i in range(8):
            for h in range(2):
                halo = jnp.where(right, r_ref[h, f, i], l_ref[h, f, i])
                piece = jnp.concatenate([c_ref[h, f, i], halo], 1)
                own_ref[f, i, 8 * h : 8 * h + 8, :] = piece
                if i >= 8 - REACH[f]:
                    up_ref[OFFS[f] + i - (8 - REACH[f]), 8 * h : 8 * h + 8, :] = piece
                if i < REACH[f]:
                    down_ref[OFFS[f] + i, 8 * h : 8 * h + 8, :] = piece


def spread_out(own_ref, lo_ref, hi_ref, refs):
    for f, ref in enumerate(refs):
        n = REACH[f]
        for j in range(n):
            ref[8 - n + j] = lo_ref[OFFS[f] + j]
            ref[16 + j] = hi_ref[OFFS[f] + j]
        for j in range(8):
            ref[8 + j] = own_ref[f, j]


def stiffness(place_ref, d_ref, v_ref, s_ref, e_ref, f_ref, first, last):
    block, gy = place_ref[0], place_ref[1]
    lane = iota((1, 256), 1)
    z = gy * 128 + jnp.where(lane < 192, lane, lane - 256)
    z_in = ((z >= 0) & (z < 512)).astype(F32)
    z_count = ((z >= 1) & (z < 513)).astype(F32) + ((z >= -1) & (z < 511)).astype(F32)
    y = iota((16, 1), 0)
    low, high = (y >= 1).astype(F32), (y < 15).astype(F32)
    yz_count = (low + high) + z_count
    shifts = [(jnp.tanh(jnp.full((1, 1), BETA * eta, F32)), jnp.tanh(jnp.full((1, 1), BETA * (1.0 - eta), F32))) for eta in ETAS]

    def step(i):
        x = 8 * block + i - 8
        inside = lambda at: ((at >= 0) & (at < 8 * NBX)).astype(F32)
        d = d_ref[i]
        total = 2.0 * d + d_ref[i + 1] + d_ref[i - 1]
        total = total + low * rolled(d, 1, 0) + high * rolled(d, -1, 0) + rolled(d, 1, 1) + rolled(d, -1, 1)
        weights = yz_count + (2.0 + inside(x - 1) + inside(x + 1))
        here = z_in * inside(x)
        filtered = total / weights
        void, solid = v_ref[i], s_ref[i]
        open_ = 1.0 - void
        scale = here * (open_ * (1.0 - solid)) / weights
        for r, eta in enumerate(ETAS):
            t0, t1 = shifts[r]
            den = t0 + t1
            t = jnp.tanh(BETA * (filtered - eta))
            projected = (t0 + t) / den
            physical = open_ * (solid + (1.0 - solid) * projected)
            square = physical * physical
            e_ref[r, i] = here * (EMIN + (1.0 - EMIN) * (square * physical))
            if f_ref is not None:
                slope = BETA * (1.0 - t * t) / den
                f_ref[r, i] = (3.0 * (1.0 - EMIN)) * square * scale * slope

    loop(first, last, step)


def first_kernel(
    place_ref, own_ref, lo_ref, hi_ref, g_ref,
    d_ref, v_ref, s_ref, load_ref, e_ref, cx_ref, cy_ref, cz_ref, inv_ref, x_ref, rest_ref, big_ref, half_ref,
):
    spread_out(own_ref, lo_ref, hi_ref, (d_ref, v_ref, s_ref, load_ref))
    stiffness(place_ref, d_ref, v_ref, s_ref, e_ref, None, 6, 18)
    prepare(e_ref, cx_ref, cy_ref, cz_ref, inv_ref, 7, 17)

    def start(i):
        for r in range(3):
            x_ref[r, i] = OMEGA * load_ref[i] * inv_ref[r, i]

    loop(7, 17, start)
    _, outer = y_edges(16, 1)

    def leftover(i):
        for r in range(3):
            rest_ref[r, i - 8] = load_ref[i] - operate0(x_ref, i, r, e_ref, cx_ref, cy_ref, cz_ref, outer)

    loop(8, 16, leftover)
    g_ref[0:3] = pool_own(lambda f, i: rest_ref[f, i - 8], 3, big_ref, half_ref, 1.0).reshape(3, 4, 8, 128)
    g_ref[3:6] = pool_own(lambda f, i: e_ref[f, i], 3, big_ref, half_ref, 0.25).reshape(3, 4, 8, 128)


def wide_kernel(
    place_ref, own_ref, lo_ref, hi_ref, e_ref, f_ref, load_ref, cx_ref, cy_ref, cz_ref, inv_ref, d_ref, v_ref, s_ref,
):
    spread_out(own_ref, lo_ref, hi_ref, (d_ref, v_ref, s_ref, load_ref))
    stiffness(place_ref, d_ref, v_ref, s_ref, e_ref, f_ref, 2, 22)
    prepare(e_ref, cx_ref, cy_ref, cz_ref, inv_ref, 3, 21)


def mix_kernel(place_ref, lo_ref, c_ref, hi_ref, out_ref):
    mine = place_ref[0] % 4
    for to in range(4):
        out_ref[to, 0] = c_ref[...]
        out_ref[to, 1] = jnp.where(mine > to, lo_ref[...], hi_ref[...])


def window(place_ref, lo_ref, c_ref, hi_ref, mixed_ref, first, into_ref):
    block = place_ref[0]
    mine = block % 4
    for b in range(9):
        at = block - 4 + b
        keep = ((at >= 0) & (at < NBX)).astype(F32)
        source = mine + (b - 4)
        for r in range(3):
            if b == 0:
                piece = lo_ref[first + r]
            elif b == 4:
                piece = c_ref[first + r]
            elif b == 8:
                piece = hi_ref[first + r]
            else:
                far = ((source < 0) | (source > 3)).astype(jnp.int32)
                piece = mixed_ref[(source + 4) % 4, far, first + r]
            into_ref[r, 4 * b : 4 * b + 4] = keep * piece


def second_kernel(
    place_ref, e_ref, load_ref, cx_ref, cy_ref, cz_ref, inv_ref, lo_ref, c_ref, hi_ref, mixed_ref,
    one_ref, two_ref, three_ref, z0_ref, q0_ref, g_ref,
    e1_ref, x_ref, y_ref, rhs_ref, out1_ref, wide_ref, big_ref, half_ref,
):
    got = (place_ref, lo_ref, c_ref, hi_ref, mixed_ref)
    window(*got, 3, e1_ref)
    window(*got, 0, rhs_ref)
    levels = (one_ref, two_ref, three_ref)
    set_levels(e1_ref, levels)
    coarse_all(levels, rhs_ref, out1_ref, 13, 23)
    widen_into(out1_ref, 10, wide_ref)
    _, outer = y_edges(16, 1)

    def start(i):
        for r in range(3):
            x_ref[r, i] = OMEGA * load_ref[i] * inv_ref[r, i] + widened(wide_ref, r, (i - 2) // 2, 10)

    loop(3, 21, start)

    def smooth(i):
        for r in range(3):
            image = operate0(x_ref, i, r, e_ref, cx_ref, cy_ref, cz_ref, outer)
            z0_ref[r, i] = x_ref[r, i] + OMEGA * (load_ref[i] - image) * inv_ref[r, i]

    loop(4, 20, smooth)

    def apply(i):
        for r in range(3):
            image = operate0(z0_ref, i, r, e_ref, cx_ref, cy_ref, cz_ref, outer)
            q0_ref[r, i] = image
            y_ref[r, i] = OMEGA * image * inv_ref[r, i]

    loop(5, 19, apply)

    def leftover(i):
        for r in range(3):
            x_ref[r, i] = q0_ref[r, i] - operate0(y_ref, i, r, e_ref, cx_ref, cy_ref, cz_ref, outer)

    loop(8, 16, leftover)
    g_ref[...] = pool_own(lambda f, i: x_ref[f, i], 3, big_ref, half_ref, 1.0).reshape(3, 4, 8, 128)


def third_kernel(
    place_ref, e_ref, load_ref, cx_ref, cy_ref, cz_ref, inv_ref, one_ref, two_ref, three_ref, z0_ref, q0_ref,
    lo_ref, c_ref, hi_ref, mixed_ref, w_ref, dots_ref, x_ref, rhs_ref, out1_ref, wide_ref,
):
    window(place_ref, lo_ref, c_ref, hi_ref, mixed_ref, 0, rhs_ref)
    coarse_all((one_ref, two_ref, three_ref), rhs_ref, out1_ref, 14, 22)
    widen_into(out1_ref, 8, wide_ref)
    _, outer = y_edges(16, 1)

    def start(i):
        for r in range(3):
            x_ref[r, i] = OMEGA * q0_ref[r, i] * inv_ref[r, i] + widened(wide_ref, r, (i - 4) // 2, 8)

    loop(5, 19, start)

    def smooth(i):
        for r in range(3):
            image = operate0(x_ref, i, r, e_ref, cx_ref, cy_ref, cz_ref, outer)
            w_ref[r, i] = x_ref[r, i] + OMEGA * (q0_ref[r, i] - image) * inv_ref[r, i]

    loop(6, 18, smooth)

    def add(t, sums):
        sums = list(sums)
        for i in (8 + 2 * t, 9 + 2 * t):
            for r in range(3):
                image = operate0(w_ref, i, r, e_ref, cx_ref, cy_ref, cz_ref, outer)[:, :128]
                b, z0, q0, w = load_ref[i, :, :128], z0_ref[r, i, :, :128], q0_ref[r, i, :, :128], w_ref[r, i, :, :128]
                for q, term in enumerate((b * z0, z0 * q0, b * w, q0 * w, w * image)):
                    sums[r * 5 + q] = sums[r * 5 + q] + (term[:8] + term[8:])
        return tuple(sums)

    sums = lax.fori_loop(0, 4, add, tuple(jnp.zeros((8, 128), F32) for _ in range(15)))
    lane = iota((1, 128), 1)
    row = jnp.zeros((1, 128), F32)
    for q, v in enumerate(sums):
        row = row + jnp.where(lane == q, jnp.sum(jnp.sum(v, 0, keepdims=True), 1, keepdims=True), 0.0)
    dots_ref[...] = jnp.broadcast_to(row[None], (16, 1, 128))


def sum_kernel(in_ref, out_ref):
    out_ref[...] = jnp.broadcast_to(jnp.sum(in_ref[...], 0, keepdims=True), (16, 1, 128))


def last_kernel(place_ref, f_ref, z0_ref, w_ref, dots_ref, sens_ref, comp_ref, u_ref, comb_ref):
    real = place_ref[2]
    totals = jnp.sum(dots_ref[...], 0)
    lane = iota((1, 128), 1)
    pick = lambda q: jnp.sum(jnp.where(lane == q, totals, 0.0), 1, keepdims=True)
    factors = []
    for r in range(3):
        bz, zq, bw, qw, wa = (pick(r * 5 + q) for q in range(5))
        a0 = bz / zq
        rz1 = bz - a0 * bw - a0 * zq + (a0 * a0) * qw
        grow = 1.0 + rz1 / bz
        a1 = rz1 / ((grow * grow) * zq - 2.0 * (a0 * grow) * qw + (a0 * a0) * wa)
        c0, c1 = a0 + a1 * grow, -(a1 * a0)
        factors.append((c0, c1))
        comp_ref[r] = jnp.sum(c0 * bz + c1 * bw)
    y = iota((16, 1), 0)
    low, high = (y >= 1).astype(F32), (y < 15).astype(F32)

    def state(i):
        for r in range(3):
            u_ref[r, i] = factors[r][0] * z0_ref[r, i] + factors[r][1] * w_ref[r, i]

    loop(6, 18, state)

    def energy(i):
        total = jnp.zeros((16, 256), F32)
        for r in range(3):
            u = u_ref[r, i]
            gaps = (
                u - u_ref[r, i - 1],
                u - u_ref[r, i + 1],
                u - low * rolled(u, 1, 0),
                u - high * rolled(u, -1, 0),
                u - rolled(u, 1, 1),
                u - rolled(u, -1, 1),
            )
            square = gaps[0] * gaps[0]
            for gap in gaps[1:]:
                square = square + gap * gap
            total = total - (0.5 * square) * f_ref[r, i]
        comb_ref[i] = total

    loop(7, 17, energy)

    def spread(i):
        c = comb_ref[i]
        total = 2.0 * c + comb_ref[i + 1] + comb_ref[i - 1]
        total = total + low * rolled(c, 1, 0) + high * rolled(c, -1, 0) + rolled(c, 1, 1) + rolled(c, -1, 1)
        sens_ref[i - 8] = jnp.where(real == 0, total[:8, :128], total[8:, :128])

    loop(8, 16, spread)


def call(body, outs, scratch, *args, place=None, flops=0, out_specs=None):
    in_specs = [pl.BlockSpec(memory_space=pltpu.VMEM)] * len(args)
    if place is not None:
        in_specs, args = [pl.BlockSpec(memory_space=pltpu.SMEM)] + in_specs, (place, *args)
    return pl.pallas_call(
        body,
        out_shape=outs,
        in_specs=in_specs,
        **({} if out_specs is None else {"out_specs": out_specs}),
        scratch_shapes=[pltpu.VMEM(dims, F32) for dims in scratch],
        compiler_params=pltpu.CompilerParams(vmem_limit_bytes=VMEM_LIMIT),
        cost_estimate=pl.CostEstimate(flops=flops, bytes_accessed=0, transcendentals=0),
    )(*args)


Z_AXES = ("zh", "zl")
X_AXES = ("zh", "zl", "xc")
Y_AXES = ("yl", "core")
FIELD = (3, 24, 16, 256)
LEVEL1 = (3, 36, 8, 128)
SLICES = (24, 16, 256)


def neighbours(count, step, wrap):
    return [(i, (i + step) % count) for i in range(count) if wrap or 0 <= i + step < count]


def fetch(place, own):
    lo = lax.ppermute(own, Z_AXES, neighbours(16, 1, True))
    hi = lax.ppermute(own, Z_AXES, neighbours(16, -1, True))
    mixed = call(mix_kernel, shaped(4, 2, *own.shape), [], lo, own, hi, place=place)
    return lo, own, hi, lax.all_to_all(mixed, "xc", 0, 0)


def body(design, load, void_mask, solid_mask):
    place = jnp.stack([lax.axis_index(X_AXES), lax.axis_index(Y_AXES), lax.axis_index("real")]).astype(jnp.int32)
    own = call(pack_kernel, shaped(4, 8, 8, 128), [], design, void_mask, solid_mask, load)
    both = lax.all_gather(own, "real")
    left = lax.ppermute(both, Y_AXES, neighbours(4, 1, False))
    right = lax.ppermute(both, Y_AXES, neighbours(4, -1, False))
    mine, up, down = call(select_kernel, (shaped(4, 8, 16, 256), shaped(*SLICES), shaped(*SLICES)), [], both, left, right)
    lo = lax.ppermute(up, X_AXES, neighbours(NBX, 1, False))
    hi = lax.ppermute(down, X_AXES, neighbours(NBX, -1, False))
    g = call(
        first_kernel,
        shaped(6, 4, 8, 128),
        [SLICES] * 4 + [FIELD] * 6 + [(3, 8, 16, 256), (192, 256), (192, 128)],
        mine, lo, hi, place=place,
    )
    e, f, wide_load, cx, cy, cz, inv = call(
        wide_kernel,
        (shaped(*FIELD), shaped(*FIELD), shaped(*SLICES)) + (shaped(*FIELD),) * 4,
        [SLICES] * 3,
        mine, lo, hi, place=place, flops=2 * 10**7,
    )
    level0 = (e, wide_load, cx, cy, cz, inv)
    levels = tuple(shaped(6, 3, n, 8, 128) for n in (36, 18, 9))
    *levels, z0, q0, g2 = call(
        second_kernel,
        levels + (shaped(*FIELD), shaped(*FIELD), shaped(3, 4, 8, 128)),
        [LEVEL1, FIELD, FIELD, LEVEL1, (3, 10, 8, 128), (2, 480, 128), (192, 256), (192, 128)],
        *level0, *fetch(place, g), place=place,
    )
    w, dots = call(
        third_kernel,
        (shaped(*FIELD), shaped(16, 1, 128)),
        [FIELD, LEVEL1, (3, 8, 8, 128), (2, 384, 128)],
        *level0, *levels, z0, q0, *fetch(place, g2), place=place,
    )
    dots = lax.all_to_all(dots, ("zl", "xc"), 0, 0, tiled=True)
    dots = call(sum_kernel, shaped(16, 1, 128), [], dots)
    dots = lax.all_to_all(dots, ("zh", "yl", "core"), 0, 0, tiled=True)
    return call(
        last_kernel,
        (shaped(8, 8, 128), shaped(3)),
        [FIELD, SLICES],
        f, z0, w, dots, place=place,
        out_specs=(pl.BlockSpec(memory_space=pltpu.VMEM), pl.BlockSpec(memory_space=pltpu.SMEM)),
    )


def solution(mesh):
    split = Mesh(mesh.devices.reshape(2, 4, 4, 4, 2, 2), ("real", "zh", "zl", "xc", "yl", "core"))
    spec = P(X_AXES, "real", Y_AXES)
    return jax.shard_map(body, mesh=split, in_specs=(spec,) * 4, out_specs=(spec, P()), check_vma=False)
```

```python
import jax
import jax.numpy as jnp
from jax import lax
from jax.experimental import pallas as pl
from jax.experimental.pallas import tpu as pltpu
from jax.sharding import Mesh
from jax.sharding import PartitionSpec as P

EMIN = 0.01
BETA = 8.0
OMEGA = 0.6
ETAS = (0.7, 0.5, 0.3)
NBX = 64
VMEM_LIMIT = 16 * 1024 * 1024
F32 = jnp.float32
HI = lax.Precision.HIGHEST


GROUP = 4


def loop(first, last, step, group=None):
    group = group or GROUP
    turns = (last - first) // group

    def turn(t, _):
        for j in range(group):
            step(first + t * group + j)
        return 0

    lax.fori_loop(0, turns, turn, 0)
    for i in range(first + turns * group, last):
        step(i)


def shaped(*dims):
    return jax.ShapeDtypeStruct(dims, F32)


def rolled(v, amount, axis):
    return pltpu.roll(v, amount % v.shape[axis], axis)


def iota(shape, axis):
    return lax.broadcasted_iota(jnp.int32, shape, axis)


def pool_matrix():
    return (iota((256, 128), 0) // 2 == iota((256, 128), 1)).astype(F32)


def widen_matrix():
    return (iota((128, 256), 1) // 2 == iota((128, 256), 0)).astype(F32)


def y_edges(rows, stride):
    y = iota((rows, 1), 0)
    low = (y >= stride).astype(F32)
    outer = 0.5 * ((y < stride).astype(F32) + (y >= rows - stride).astype(F32))
    return low, outer


def face_y(e, low, stride):
    return 0.5 * low * (e + rolled(e, stride, e.ndim - 2))


def face_z(e, stride):
    return 0.5 * (e + rolled(e, stride, e.ndim - 1))


def through(c, u, stride, axis):
    flow = c * (u - rolled(u, stride, axis))
    return flow - rolled(flow, -stride, axis)


def operate(prev, u, after, cx, cx_after, cy, cz, side, stride):
    n = u.ndim
    total = cx * (u - prev) - cx_after * (after - u)
    total = total + through(cy, u, stride, n - 2) + through(cz, u, stride, n - 1)
    return total + side * u


def inverse(e, diag):
    return jnp.where(e > 0.0, 1.0 / jnp.where(e > 0.0, diag, 1.0), 0.0)


def prepare(e_ref, cx_ref, cy_ref, cz_ref, inv_ref, first, last):
    low, outer = y_edges(16, 1)

    def step(i):
        for r in range(3):
            e = e_ref[r, i]
            cx = 0.5 * (e + e_ref[r, i - 1])
            cx_after = 0.5 * (e + e_ref[r, i + 1])
            cy = face_y(e, low, 1)
            cz = face_z(e, 1)
            diag = cx + cx_after + (cy + rolled(cy, -1, 0)) + (cz + rolled(cz, -1, 1)) + outer * e
            cx_ref[r, i] = cx
            cy_ref[r, i] = cy
            cz_ref[r, i] = cz
            inv_ref[r, i] = inverse(e, diag)

    loop(first, last, step)
    for r in range(3):
        cx_ref[r, last] = 0.5 * (e_ref[r, last] + e_ref[r, last - 1])


def operate0(u_ref, i, r, e_ref, cx_ref, cy_ref, cz_ref, outer):
    return operate(
        u_ref[r, i - 1], u_ref[r, i], u_ref[r, i + 1],
        cx_ref[r, i], cx_ref[r, i + 1], cy_ref[r, i], cz_ref[r, i], outer * e_ref[r, i], 1,
    )


def pool_own(src_of, many, big_ref, half_ref, scale):
    for f in range(many):
        for k in range(4):
            at = (f * 4 + k) * 16
            big_ref[at : at + 16, :] = (0.125 * scale) * (src_of(f, 8 + 2 * k) + src_of(f, 9 + 2 * k))
    rows = many * 64
    half_ref[0:rows, :] = jnp.dot(big_ref[0:rows, :], pool_matrix(), precision=HI, preferred_element_type=F32)
    return half_ref[pl.ds(0, rows // 2, stride=2), :] + half_ref[pl.ds(1, rows // 2, stride=2), :]


def stack_level(e, stride):
    low, outer = y_edges(8, stride)
    before = jnp.concatenate([e[:1], e[:-1]], 0)
    cx = 0.5 * (e + before)
    cx_after = jnp.concatenate([cx[1:], cx[:1]], 0)
    cy = face_y(e, low[None], stride)
    cz = face_z(e, stride)
    side = outer[None] * e
    diag = cx + cx_after + (cy + rolled(cy, -stride, 1)) + (cz + rolled(cz, -stride, 2)) + side
    return cx, cx_after, cy, cz, side, inverse(e, diag)


def stack_operate(level, u, stride, first, last):
    cx, cx_after, cy, cz, side, _ = (v[first:last] for v in level)
    return operate(u[:-2], u[1:-1], u[2:], cx, cx_after, cy, cz, side, stride)


def stack_pool(v, stride):
    n = v.shape[0] // 2
    v = v.reshape(n, 2, 8, 128)
    v = v[:, 0] + v[:, 1]
    y = iota((1, 8, 1), 1)
    v = v + jnp.where((y // stride) % 2 == 0, rolled(v, -stride, 1), rolled(v, stride, 1))
    z = iota((1, 1, 128), 2)
    v = v + jnp.where((z // stride) % 2 == 0, rolled(v, -stride, 2), rolled(v, stride, 2))
    return 0.125 * v


def twice(v):
    n = v.shape[0]
    return jnp.broadcast_to(v[:, None], (n, 2, 8, 128)).reshape(2 * n, 8, 128)


STRIDES = (1, 2, 4)


def set_levels(e1_ref, level_refs):
    def step(r, _):
        e = e1_ref[r]
        for ref, stride in zip(level_refs, STRIDES):
            for q, v in enumerate(stack_level(e, stride)):
                ref[q, r] = v
            e = 0.25 * stack_pool(e, stride) if stride < 4 else e
        return 0

    lax.fori_loop(0, 3, step, 0)


def coarse(levels, rhs1, first, last):
    one, two, three = levels
    x1 = OMEGA * rhs1 * one[5]
    rest1 = rhs1[2:34] - stack_operate(one, x1[1:35], 1, 2, 34)
    rhs2 = stack_pool(rest1, 1)
    x2 = OMEGA * rhs2 * two[5][1:17]
    rest2 = rhs2[1:15] - stack_operate(two, x2, 2, 2, 16)
    rhs3 = stack_pool(rest2, 2)
    x3 = OMEGA * rhs3 * three[5][1:8]
    x3 = x3[1:6] + OMEGA * (rhs3[1:6] - stack_operate(three, x3, 4, 2, 7)) * three[5][2:7]
    x2 = x2[3:13] + twice(x3)
    x2 = x2[1:9] + OMEGA * (rhs2[4:12] - stack_operate(two, x2, 2, 5, 13)) * two[5][5:13]
    x1 = x1[10:26] + twice(x2)
    x1, at = x1[first - 11 : last - 9], slice(first, last)
    return x1[1:-1] + OMEGA * (rhs1[at] - stack_operate(one, x1, 1, first, last)) * one[5][at]


def coarse_all(level_refs, rhs1_ref, out_ref, first, last):
    def step(r, _):
        levels = [[ref[q, r] for q in range(6)] for ref in level_refs]
        out_ref[r, 0 : last - first] = coarse(levels, rhs1_ref[r], first, last)
        return 0

    lax.fori_loop(0, 3, step, 0)


def widen_into(e1_ref, count, wide_ref):
    rows = 3 * count * 8
    src = jnp.concatenate([e1_ref[r, :count].reshape(count * 8, 128) for r in range(3)], 0)
    wide = jnp.dot(src, widen_matrix(), precision=HI, preferred_element_type=F32)
    for h in range(2):
        part = wide[:, 128 * h : 128 * h + 128]
        wide_ref[h, pl.ds(0, rows, stride=2), :] = part
        wide_ref[h, pl.ds(1, rows, stride=2), :] = part


def widened(wide_ref, r, k, count):
    at = pl.multiple_of((r * count + k) * 16, 16)
    return jnp.concatenate([wide_ref[0, pl.ds(at, 16), :], wide_ref[1, pl.ds(at, 16), :]], 1)


REACH = (7, 6, 6, 5)
OFFS = (0, 7, 13, 19)


def pack_kernel(d_ref, v_ref, s_ref, load_ref, out_ref, v_in, s_in, sems):
    pairs = ((d_ref, out_ref.at[0]), (v_ref, v_in), (s_ref, s_in), (load_ref, out_ref.at[3]))
    copies = [pltpu.make_async_copy(src, dst, sems.at[q]) for q, (src, dst) in enumerate(pairs)]
    for copy in copies:
        copy.start()
    copies[1].wait()
    out_ref[1] = v_in[...].astype(F32)
    copies[2].wait()
    out_ref[2] = s_in[...].astype(F32)
    copies[0].wait()
    copies[3].wait()


def select_kernel(c_ref, l_ref, r_ref, own_ref, up_ref, down_ref):
    right = iota((8, 128), 1) < 64
    for f in range(4):
        for i in range(8):
            for h in range(2):
                halo = jnp.where(right, r_ref[h, f, i], l_ref[h, f, i])
                piece = jnp.concatenate([c_ref[h, f, i], halo], 1)
                own_ref[f, i, 8 * h : 8 * h + 8, :] = piece
                if i >= 8 - REACH[f]:
                    up_ref[OFFS[f] + i - (8 - REACH[f]), 8 * h : 8 * h + 8, :] = piece
                if i < REACH[f]:
                    down_ref[OFFS[f] + i, 8 * h : 8 * h + 8, :] = piece


def spread_out(own_ref, lo_ref, hi_ref, refs):
    for f, ref in enumerate(refs):
        n = REACH[f]
        for j in range(n):
            ref[8 - n + j] = lo_ref[OFFS[f] + j]
            ref[16 + j] = hi_ref[OFFS[f] + j]
        for j in range(8):
            ref[8 + j] = own_ref[f, j]


def stiffness(place_ref, d_ref, v_ref, s_ref, e_ref, f_ref, first, last):
    block, gy = place_ref[0], place_ref[1]
    lane = iota((1, 256), 1)
    z = gy * 128 + jnp.where(lane < 192, lane, lane - 256)
    z_in = ((z >= 0) & (z < 512)).astype(F32)
    z_count = ((z >= 1) & (z < 513)).astype(F32) + ((z >= -1) & (z < 511)).astype(F32)
    y = iota((16, 1), 0)
    low, high = (y >= 1).astype(F32), (y < 15).astype(F32)
    yz_count = (low + high) + z_count
    shifts = [(jnp.tanh(jnp.full((1, 1), BETA * eta, F32)), jnp.tanh(jnp.full((1, 1), BETA * (1.0 - eta), F32))) for eta in ETAS]

    def step(i):
        x = 8 * block + i - 8
        inside = lambda at: ((at >= 0) & (at < 8 * NBX)).astype(F32)
        d = d_ref[i]
        total = 2.0 * d + d_ref[i + 1] + d_ref[i - 1]
        total = total + low * rolled(d, 1, 0) + high * rolled(d, -1, 0) + rolled(d, 1, 1) + rolled(d, -1, 1)
        weights = yz_count + (2.0 + inside(x - 1) + inside(x + 1))
        here = z_in * inside(x)
        filtered = total / weights
        void, solid = v_ref[i], s_ref[i]
        open_ = 1.0 - void
        scale = here * (open_ * (1.0 - solid)) / weights
        for r, eta in enumerate(ETAS):
            t0, t1 = shifts[r]
            den = t0 + t1
            t = jnp.tanh(BETA * (filtered - eta))
            projected = (t0 + t) / den
            physical = open_ * (solid + (1.0 - solid) * projected)
            square = physical * physical
            e_ref[r, i] = here * (EMIN + (1.0 - EMIN) * (square * physical))
            if f_ref is not None:
                slope = BETA * (1.0 - t * t) / den
                f_ref[r, i] = (3.0 * (1.0 - EMIN)) * square * scale * slope

    loop(first, last, step)


def first_kernel(
    place_ref, own_ref, lo_ref, hi_ref, g_ref,
    d_ref, v_ref, s_ref, load_ref, e_ref, cx_ref, cy_ref, cz_ref, inv_ref, x_ref, rest_ref, big_ref, half_ref,
):
    spread_out(own_ref, lo_ref, hi_ref, (d_ref, v_ref, s_ref, load_ref))
    stiffness(place_ref, d_ref, v_ref, s_ref, e_ref, None, 6, 18)
    prepare(e_ref, cx_ref, cy_ref, cz_ref, inv_ref, 7, 17)

    def start(i):
        for r in range(3):
            x_ref[r, i] = OMEGA * load_ref[i] * inv_ref[r, i]

    loop(7, 17, start)
    _, outer = y_edges(16, 1)

    def leftover(i):
        for r in range(3):
            rest_ref[r, i - 8] = load_ref[i] - operate0(x_ref, i, r, e_ref, cx_ref, cy_ref, cz_ref, outer)

    loop(8, 16, leftover)
    g_ref[0:3] = pool_own(lambda f, i: rest_ref[f, i - 8], 3, big_ref, half_ref, 1.0).reshape(3, 4, 8, 128)
    g_ref[3:6] = pool_own(lambda f, i: e_ref[f, i], 3, big_ref, half_ref, 0.25).reshape(3, 4, 8, 128)


def wide_kernel(
    place_ref, own_ref, lo_ref, hi_ref, e_ref, f_ref, load_ref, cx_ref, cy_ref, cz_ref, inv_ref, d_ref, v_ref, s_ref,
):
    spread_out(own_ref, lo_ref, hi_ref, (d_ref, v_ref, s_ref, load_ref))
    stiffness(place_ref, d_ref, v_ref, s_ref, e_ref, f_ref, 2, 22)
    prepare(e_ref, cx_ref, cy_ref, cz_ref, inv_ref, 3, 21)


def mix_kernel(place_ref, lo_ref, c_ref, hi_ref, *refs):
    out_ref = refs[-1]
    mine = place_ref[0] % 4
    for to in range(4):
        out_ref[to, 0] = c_ref[...]
        out_ref[to, 1] = jnp.where(mine > to, lo_ref[...], hi_ref[...])


def window(place_ref, lo_ref, c_ref, hi_ref, mixed_ref, first, into_ref):
    block = place_ref[0]
    mine = block % 4
    for b in range(9):
        at = block - 4 + b
        keep = ((at >= 0) & (at < NBX)).astype(F32)
        source = mine + (b - 4)
        for r in range(3):
            if b == 0:
                piece = lo_ref[first + r]
            elif b == 4:
                piece = c_ref[first + r]
            elif b == 8:
                piece = hi_ref[first + r]
            else:
                far = ((source < 0) | (source > 3)).astype(jnp.int32)
                piece = mixed_ref[(source + 4) % 4, far, first + r]
            into_ref[r, 4 * b : 4 * b + 4] = keep * piece


def second_kernel(
    place_ref, e_ref, load_ref, cx_ref, cy_ref, cz_ref, inv_ref, lo_ref, c_ref, hi_ref, mixed_ref,
    one_ref, two_ref, three_ref, z0_ref, q0_ref, g_ref,
    e1_ref, x_ref, y_ref, rhs_ref, out1_ref, wide_ref, big_ref, half_ref,
):
    got = (place_ref, lo_ref, c_ref, hi_ref, mixed_ref)
    window(*got, 3, e1_ref)
    window(*got, 0, rhs_ref)
    levels = (one_ref, two_ref, three_ref)
    set_levels(e1_ref, levels)
    coarse_all(levels, rhs_ref, out1_ref, 13, 23)
    widen_into(out1_ref, 10, wide_ref)
    _, outer = y_edges(16, 1)

    def start(i):
        for r in range(3):
            x_ref[r, i] = OMEGA * load_ref[i] * inv_ref[r, i] + widened(wide_ref, r, (i - 2) // 2, 10)

    loop(3, 21, start)

    def smooth(i):
        for r in range(3):
            image = operate0(x_ref, i, r, e_ref, cx_ref, cy_ref, cz_ref, outer)
            z0_ref[r, i] = x_ref[r, i] + OMEGA * (load_ref[i] - image) * inv_ref[r, i]

    loop(4, 20, smooth)

    def apply(i):
        for r in range(3):
            image = operate0(z0_ref, i, r, e_ref, cx_ref, cy_ref, cz_ref, outer)
            q0_ref[r, i] = image
            y_ref[r, i] = OMEGA * image * inv_ref[r, i]

    loop(5, 19, apply)

    def leftover(i):
        for r in range(3):
            x_ref[r, i] = q0_ref[r, i] - operate0(y_ref, i, r, e_ref, cx_ref, cy_ref, cz_ref, outer)

    loop(8, 16, leftover)
    g_ref[...] = pool_own(lambda f, i: x_ref[f, i], 3, big_ref, half_ref, 1.0).reshape(3, 4, 8, 128)


def third_kernel(
    place_ref, e_ref, load_ref, cx_ref, cy_ref, cz_ref, inv_ref, one_ref, two_ref, three_ref, z0_ref, q0_ref,
    lo_ref, c_ref, hi_ref, mixed_ref, w_ref, dots_ref, x_ref, rhs_ref, out1_ref, wide_ref,
):
    window(place_ref, lo_ref, c_ref, hi_ref, mixed_ref, 0, rhs_ref)
    coarse_all((one_ref, two_ref, three_ref), rhs_ref, out1_ref, 14, 22)
    widen_into(out1_ref, 8, wide_ref)
    _, outer = y_edges(16, 1)

    def start(i):
        for r in range(3):
            x_ref[r, i] = OMEGA * q0_ref[r, i] * inv_ref[r, i] + widened(wide_ref, r, (i - 4) // 2, 8)

    loop(5, 19, start)

    def smooth(i):
        for r in range(3):
            image = operate0(x_ref, i, r, e_ref, cx_ref, cy_ref, cz_ref, outer)
            w_ref[r, i] = x_ref[r, i] + OMEGA * (q0_ref[r, i] - image) * inv_ref[r, i]

    loop(6, 18, smooth)

    def add(t, sums):
        sums = list(sums)
        for i in (8 + 2 * t, 9 + 2 * t):
            for r in range(3):
                image = operate0(w_ref, i, r, e_ref, cx_ref, cy_ref, cz_ref, outer)[:, :128]
                b, z0, q0, w = load_ref[i, :, :128], z0_ref[r, i, :, :128], q0_ref[r, i, :, :128], w_ref[r, i, :, :128]
                for q, term in enumerate((b * z0, z0 * q0, b * w, q0 * w, w * image)):
                    sums[r * 5 + q] = sums[r * 5 + q] + (term[:8] + term[8:])
        return tuple(sums)

    sums = lax.fori_loop(0, 4, add, tuple(jnp.zeros((8, 128), F32) for _ in range(15)))
    lane = iota((1, 128), 1)
    row = jnp.zeros((1, 128), F32)
    for q, v in enumerate(sums):
        row = row + jnp.where(lane == q, jnp.sum(jnp.sum(v, 0, keepdims=True), 1, keepdims=True), 0.0)
    dots_ref[...] = jnp.broadcast_to(row[None], (16, 1, 128))


def sum_kernel(in_ref, out_ref):
    out_ref[...] = jnp.broadcast_to(jnp.sum(in_ref[...], 0, keepdims=True), (16, 1, 128))


def last_kernel(place_ref, f_ref, z0_ref, w_ref, dots_ref, sens_ref, comp_ref, u_ref, comb_ref):
    real = place_ref[2]
    totals = jnp.sum(dots_ref[...], 0)
    lane = iota((1, 128), 1)
    pick = lambda q: jnp.sum(jnp.where(lane == q, totals, 0.0), 1, keepdims=True)
    factors = []
    for r in range(3):
        bz, zq, bw, qw, wa = (pick(r * 5 + q) for q in range(5))
        a0 = bz / zq
        rz1 = bz - a0 * bw - a0 * zq + (a0 * a0) * qw
        grow = 1.0 + rz1 / bz
        a1 = rz1 / ((grow * grow) * zq - 2.0 * (a0 * grow) * qw + (a0 * a0) * wa)
        c0, c1 = a0 + a1 * grow, -(a1 * a0)
        factors.append((c0, c1))
        comp_ref[r] = jnp.sum(c0 * bz + c1 * bw)
    y = iota((16, 1), 0)
    low, high = (y >= 1).astype(F32), (y < 15).astype(F32)

    def state(i):
        for r in range(3):
            u_ref[r, i] = factors[r][0] * z0_ref[r, i] + factors[r][1] * w_ref[r, i]

    loop(6, 18, state)

    def energy(i):
        total = jnp.zeros((16, 256), F32)
        for r in range(3):
            u = u_ref[r, i]
            gaps = (
                u - u_ref[r, i - 1],
                u - u_ref[r, i + 1],
                u - low * rolled(u, 1, 0),
                u - high * rolled(u, -1, 0),
                u - rolled(u, 1, 1),
                u - rolled(u, -1, 1),
            )
            square = gaps[0] * gaps[0]
            for gap in gaps[1:]:
                square = square + gap * gap
            total = total - (0.5 * square) * f_ref[r, i]
        comb_ref[i] = total

    loop(7, 17, energy)

    def spread(i):
        c = comb_ref[i]
        total = 2.0 * c + comb_ref[i + 1] + comb_ref[i - 1]
        total = total + low * rolled(c, 1, 0) + high * rolled(c, -1, 0) + rolled(c, 1, 1) + rolled(c, -1, 1)
        sens_ref[i - 8] = jnp.where(real == 0, total[:8, :128], total[8:, :128])

    loop(8, 16, spread)


def call(body, outs, scratch, *args, place=None, flops=0, out_specs=None):
    in_specs = [pl.BlockSpec(memory_space=pltpu.VMEM)] * len(args)
    if place is not None:
        in_specs, args = [pl.BlockSpec(memory_space=pltpu.SMEM)] + in_specs, (place, *args)
    return pl.pallas_call(
        body,
        out_shape=outs,
        in_specs=in_specs,
        **({} if out_specs is None else {"out_specs": out_specs}),
        scratch_shapes=[pltpu.VMEM(dims, F32) for dims in scratch],
        compiler_params=pltpu.CompilerParams(vmem_limit_bytes=VMEM_LIMIT),
        cost_estimate=pl.CostEstimate(flops=flops, bytes_accessed=0, transcendentals=0),
    )(*args)


Z_AXES = ("zh", "zl")
X_AXES = ("zh", "zl", "xc")
Y_AXES = ("yl", "core")
FIELD = (3, 24, 16, 256)
LEVEL1 = (3, 36, 8, 128)
SLICES = (24, 16, 256)


def neighbours(count, step, wrap):
    return [(i, (i + step) % count) for i in range(count) if wrap or 0 <= i + step < count]


def fetch(place, own, *after):
    lo = lax.ppermute(own, Z_AXES, neighbours(16, 1, True))
    hi = lax.ppermute(own, Z_AXES, neighbours(16, -1, True))
    mixed = call(mix_kernel, shaped(4, 2, *own.shape), [], lo, own, hi, *after, place=place)
    return lo, own, hi, lax.all_to_all(mixed, "xc", 0, 0)


def body(design, load, void_mask, solid_mask):
    place = jnp.stack([lax.axis_index(X_AXES), lax.axis_index(Y_AXES), lax.axis_index("real")]).astype(jnp.int32)
    own = pl.pallas_call(
        pack_kernel,
        out_shape=shaped(4, 8, 8, 128),
        in_specs=[pl.BlockSpec(memory_space=pl.ANY)] * 4,
        scratch_shapes=[pltpu.VMEM((8, 8, 128), jnp.int32)] * 2 + [pltpu.SemaphoreType.DMA((4,))],
    )(design, void_mask, solid_mask, load)
    both = lax.all_gather(own, "real")
    left = lax.ppermute(both, Y_AXES, neighbours(4, 1, False))
    right = lax.ppermute(both, Y_AXES, neighbours(4, -1, False))
    mine, up, down = call(select_kernel, (shaped(4, 8, 16, 256), shaped(*SLICES), shaped(*SLICES)), [], both, left, right)
    lo = lax.ppermute(up, X_AXES, neighbours(NBX, 1, False))
    hi = lax.ppermute(down, X_AXES, neighbours(NBX, -1, False))
    g = call(
        first_kernel,
        shaped(6, 4, 8, 128),
        [SLICES] * 4 + [FIELD] * 6 + [(3, 8, 16, 256), (192, 256), (192, 128)],
        mine, lo, hi, place=place,
    )
    e, f, wide_load, cx, cy, cz, inv = call(
        wide_kernel,
        (shaped(*FIELD), shaped(*FIELD), shaped(*SLICES)) + (shaped(*FIELD),) * 4,
        [SLICES] * 3,
        mine, lo, hi, place=place, flops=2 * 10**7,
    )
    level0 = (e, wide_load, cx, cy, cz, inv)
    levels = tuple(shaped(6, 3, n, 8, 128) for n in (36, 18, 9))
    *levels, z0, q0, g2 = call(
        second_kernel,
        levels + (shaped(*FIELD), shaped(*FIELD), shaped(3, 4, 8, 128)),
        [LEVEL1, FIELD, FIELD, LEVEL1, (3, 10, 8, 128), (2, 480, 128), (192, 256), (192, 128)],
        *level0, *fetch(place, g, wide_load), place=place,
    )
    w, dots = call(
        third_kernel,
        (shaped(*FIELD), shaped(16, 1, 128)),
        [FIELD, LEVEL1, (3, 8, 8, 128), (2, 384, 128)],
        *level0, *levels, z0, q0, *fetch(place, g2), place=place,
    )
    dots = lax.all_to_all(dots, ("xc", "yl", "core"), 0, 0, tiled=True)
    dots = call(sum_kernel, shaped(16, 1, 128), [], dots)
    dots = lax.all_to_all(dots, ("zh", "zl"), 0, 0, tiled=True)
    return call(
        last_kernel,
        (shaped(8, 8, 128), shaped(3)),
        [FIELD, SLICES],
        f, z0, w, dots, place=place,
        out_specs=(pl.BlockSpec(memory_space=pltpu.VMEM), pl.BlockSpec(memory_space=pltpu.SMEM)),
    )


def solution(mesh):
    split = Mesh(mesh.devices.reshape(2, 4, 4, 4, 2, 2), ("real", "zh", "zl", "xc", "yl", "core"))
    spec = P(X_AXES, "real", Y_AXES)
    return jax.shard_map(body, mesh=split, in_specs=(spec,) * 4, out_specs=(spec, P()), check_vma=False)
```

```python
import jax
import jax.numpy as jnp
from jax import lax
from jax.experimental import pallas as pl
from jax.experimental.pallas import tpu as pltpu
from jax.sharding import Mesh
from jax.sharding import PartitionSpec as P

EMIN = 0.01
BETA = 8.0
OMEGA = 0.6
ETAS = (0.7, 0.5, 0.3)
NBX = 64
VMEM_LIMIT = 16 * 1024 * 1024
F32 = jnp.float32
HI = lax.Precision.HIGHEST


GROUP = 4


def loop(first, last, step, group=None):
    group = group or GROUP
    turns = (last - first) // group

    def turn(t, _):
        for j in range(group):
            step(first + t * group + j)
        return 0

    lax.fori_loop(0, turns, turn, 0)
    for i in range(first + turns * group, last):
        step(i)


def shaped(*dims):
    return jax.ShapeDtypeStruct(dims, F32)


def rolled(v, amount, axis):
    return pltpu.roll(v, amount % v.shape[axis], axis)


def iota(shape, axis):
    return lax.broadcasted_iota(jnp.int32, shape, axis)


def pool_matrix():
    return (iota((256, 128), 0) // 2 == iota((256, 128), 1)).astype(F32)


def widen_matrix():
    return (iota((128, 256), 1) // 2 == iota((128, 256), 0)).astype(F32)


def y_edges(rows, stride):
    y = iota((rows, 1), 0)
    low = (y >= stride).astype(F32)
    outer = 0.5 * ((y < stride).astype(F32) + (y >= rows - stride).astype(F32))
    return low, outer


def inverse(e, diag):
    return jnp.where(e > 0.0, 1.0 / jnp.where(e > 0.0, diag, 1.0), 0.0)


def prepare(e_ref, level, first, last):
    cx_ref, cy_ref, cyp_ref, cz_ref, czp_ref, diag_ref, inv_ref = level
    low, outer = y_edges(16, 1)

    def step(i):
        for r in range(3):
            e = e_ref[r, i]
            h = 0.5 * e
            cx, cxp = h + 0.5 * e_ref[r, i - 1], h + 0.5 * e_ref[r, i + 1]
            cy, cz = low * (h + rolled(h, 1, 0)), h + rolled(h, 1, 1)
            cyp, czp = rolled(cy, -1, 0), rolled(cz, -1, 1)
            diag = (cx + cxp) + (cy + cyp) + (cz + czp) + outer * e
            for ref, v in zip(level, (cx, cy, cyp, cz, czp, diag, inverse(e, diag))):
                ref[r, i] = v

    loop(first, last, step)
    for r in range(3):
        cx_ref[r, last] = 0.5 * (e_ref[r, last] + e_ref[r, last - 1])


def pull(u_ref, i, r, level):
    cx_ref, cy_ref, cyp_ref, cz_ref, czp_ref = level[:5]
    u = u_ref[r, i]
    total = cx_ref[r, i] * u_ref[r, i - 1] + cx_ref[r, i + 1] * u_ref[r, i + 1]
    total = total + (cy_ref[r, i] * rolled(u, 1, 0) + cyp_ref[r, i] * rolled(u, -1, 0))
    return total + (cz_ref[r, i] * rolled(u, 1, 1) + czp_ref[r, i] * rolled(u, -1, 1))


KEEP = 1.0 - OMEGA


def pool_own(src_of, many, big_ref, half_ref, scale):
    for f in range(many):
        for k in range(4):
            at = (f * 4 + k) * 16
            big_ref[at : at + 16, :] = (0.125 * scale) * (src_of(f, 8 + 2 * k) + src_of(f, 9 + 2 * k))
    rows = many * 64
    half_ref[0:rows, :] = jnp.dot(big_ref[0:rows, :], pool_matrix(), precision=HI, preferred_element_type=F32)
    return half_ref[pl.ds(0, rows // 2, stride=2), :] + half_ref[pl.ds(1, rows // 2, stride=2), :]


def stack_level(e, stride):
    low, outer = y_edges(8, stride)
    h = 0.5 * e
    mid = h[1:-1]
    cx, cxp = mid + h[:-2], mid + h[2:]
    cy, cz = low * (mid + rolled(mid, stride, 1)), mid + rolled(mid, stride, 2)
    cyp, czp = rolled(cy, -stride, 1), rolled(cz, -stride, 2)
    diag = (cx + cxp) + (cy + cyp) + (cz + czp) + outer * e[1:-1]
    return cx, cxp, cy, cyp, cz, czp, inverse(e[1:-1], diag)


def stack_pull(level, u, stride, first, last):
    cx, cxp, cy, cyp, cz, czp = (v[first:last] for v in level[:6])
    mid = u[1:-1]
    total = cx * u[:-2] + cxp * u[2:]
    total = total + (cy * rolled(mid, stride, 1) + cyp * rolled(mid, -stride, 1))
    return total + (cz * rolled(mid, stride, 2) + czp * rolled(mid, -stride, 2))


def stack_pool(v, stride):
    n = v.shape[0] // 2
    v = v.reshape(n, 2, 8, 128)
    v = v[:, 0] + v[:, 1]
    y = iota((1, 8, 1), 1)
    v = v + jnp.where((y // stride) % 2 == 0, rolled(v, -stride, 1), rolled(v, stride, 1))
    z = iota((1, 1, 128), 2)
    v = v + jnp.where((z // stride) % 2 == 0, rolled(v, -stride, 2), rolled(v, stride, 2))
    return 0.125 * v


def twice(v):
    n = v.shape[0]
    return jnp.broadcast_to(v[:, None], (n, 2, 8, 128)).reshape(2 * n, 8, 128)


STRIDES = (1, 2, 4)


def set_levels(e1_ref, level_refs):
    for r in range(3):
        e = e1_ref[r]
        for ref, stride in zip(level_refs, STRIDES):
            for q, v in enumerate(stack_level(e, stride)):
                ref[q, r, 1 : 1 + v.shape[0]] = v
            e = 0.25 * stack_pool(e, stride) if stride < 4 else e


def coarse(levels, rhs1, first, last):
    one, two, three = levels
    x1 = OMEGA * rhs1[1:35] * one[6][1:35]
    rhs2 = stack_pool(KEEP * rhs1[2:34] + stack_pull(one, x1, 1, 2, 34), 1)
    x2 = OMEGA * rhs2 * two[6][1:17]
    rhs3 = stack_pool(KEEP * rhs2[1:15] + stack_pull(two, x2, 2, 2, 16), 2)
    x3 = OMEGA * rhs3 * three[6][1:8]
    x3 = KEEP * x3[1:6] + OMEGA * three[6][2:7] * (rhs3[1:6] + stack_pull(three, x3, 4, 2, 7))
    x2 = x2[3:13] + twice(x3)
    x2 = KEEP * x2[1:9] + OMEGA * two[6][5:13] * (rhs2[4:12] + stack_pull(two, x2, 2, 5, 13))
    x1 = x1[9:25] + twice(x2)
    x1, at = x1[first - 11 : last - 9], slice(first, last)
    return KEEP * x1[1:-1] + OMEGA * one[6][at] * (rhs1[at] + stack_pull(one, x1, 1, first, last))


def coarse_all(level_refs, rhs1_ref, out_ref, first, last):
    for r in range(3):
        levels = [[ref[q, r] for q in range(7)] for ref in level_refs]
        out_ref[r] = coarse(levels, rhs1_ref[r], first, last)


def widen_into(e1_ref, count, wide_ref):
    rows = 3 * count * 8
    src = jnp.concatenate([e1_ref[r, :count].reshape(count * 8, 128) for r in range(3)], 0)
    wide = jnp.dot(src, widen_matrix(), precision=HI, preferred_element_type=F32)
    for h in range(2):
        part = wide[:, 128 * h : 128 * h + 128]
        wide_ref[h, pl.ds(0, rows, stride=2), :] = part
        wide_ref[h, pl.ds(1, rows, stride=2), :] = part


def widened(wide_ref, r, k, count):
    at = pl.multiple_of((r * count + k) * 16, 16)
    return jnp.concatenate([wide_ref[0, pl.ds(at, 16), :], wide_ref[1, pl.ds(at, 16), :]], 1)


REACH = (7, 6, 6, 5)
OFFS = (0, 7, 13, 19)


def pack_kernel(d_ref, v_ref, s_ref, load_ref, out_ref, v_in, s_in, sems):
    pairs = ((d_ref, out_ref.at[0]), (v_ref, v_in), (s_ref, s_in), (load_ref, out_ref.at[3]))
    copies = [pltpu.make_async_copy(src, dst, sems.at[q]) for q, (src, dst) in enumerate(pairs)]
    for copy in copies:
        copy.start()
    copies[1].wait()
    out_ref[1] = v_in[...].astype(F32)
    copies[2].wait()
    out_ref[2] = s_in[...].astype(F32)
    copies[0].wait()
    copies[3].wait()


def select_kernel(place_ref, c_ref, a_ref, b_ref, own_ref, up_ref, down_ref):
    right = (iota((8, 128), 1) < 64) == (place_ref[1] % 2 == 0)
    for f in range(4):
        for i in range(8):
            for h in range(2):
                halo = jnp.where(right, a_ref[h, f, i], b_ref[h, f, i])
                piece = jnp.concatenate([c_ref[h, f, i], halo], 1)
                own_ref[f, i, 8 * h : 8 * h + 8, :] = piece
                if i >= 8 - REACH[f]:
                    up_ref[OFFS[f] + i - (8 - REACH[f]), 8 * h : 8 * h + 8, :] = piece
                if i < REACH[f]:
                    down_ref[OFFS[f] + i, 8 * h : 8 * h + 8, :] = piece


def spread_out(own_ref, lo_ref, hi_ref, refs):
    for f, (ref, n) in enumerate(zip(refs, REACH)):
        ref[8 - n : 8] = lo_ref[OFFS[f] : OFFS[f] + n]
        ref[8:16] = own_ref[f]
        ref[16 : 16 + n] = hi_ref[OFFS[f] : OFFS[f] + n]


def stiffness(place_ref, d_ref, v_ref, s_ref, e_ref, f_ref, first, last):
    block, gy = place_ref[0], place_ref[1]
    lane = iota((1, 256), 1)
    z = gy * 128 + jnp.where(lane < 192, lane, lane - 256)
    z_in = ((z >= 0) & (z < 512)).astype(F32)
    z_count = ((z >= 1) & (z < 513)).astype(F32) + ((z >= -1) & (z < 511)).astype(F32)
    y = iota((16, 1), 0)
    low, high = (y >= 1).astype(F32), (y < 15).astype(F32)
    yz_count = (low + high) + z_count
    shifts = []
    for eta in ETAS:
        t0 = jnp.tanh(jnp.full((1, 1), BETA * eta, F32))
        shifts.append((t0, 1.0 / (t0 + jnp.tanh(jnp.full((1, 1), BETA * (1.0 - eta), F32)))))

    def step(i):
        x = 8 * block + i - 8
        inside = lambda at: ((at >= 0) & (at < 8 * NBX)).astype(F32)
        d = d_ref[i]
        total = 2.0 * d + d_ref[i + 1] + d_ref[i - 1]
        total = total + low * rolled(d, 1, 0) + high * rolled(d, -1, 0) + rolled(d, 1, 1) + rolled(d, -1, 1)
        weight = 1.0 / (yz_count + (2.0 + inside(x - 1) + inside(x + 1)))
        here = z_in * inside(x)
        filtered = total * weight
        void, solid = v_ref[i], s_ref[i]
        open_ = 1.0 - void
        scale = here * (open_ * (1.0 - solid)) * weight
        for r, eta in enumerate(ETAS):
            t0, den = shifts[r]
            t = jnp.tanh(BETA * (filtered - eta))
            projected = (t0 + t) * den
            physical = open_ * (solid + (1.0 - solid) * projected)
            square = physical * physical
            e_ref[r, i] = here * (EMIN + (1.0 - EMIN) * (square * physical))
            if f_ref is not None:
                slope = BETA * (1.0 - t * t) * den
                f_ref[r, i] = (3.0 * (1.0 - EMIN)) * square * scale * slope

    loop(first, last, step)


def first_kernel(
    place_ref, own_ref, lo_ref, hi_ref, g_ref,
    d_ref, v_ref, s_ref, load_ref, e_ref, x_ref, rest_ref, big_ref, half_ref, *level,
):
    spread_out(own_ref, lo_ref, hi_ref, (d_ref, v_ref, s_ref, load_ref))
    stiffness(place_ref, d_ref, v_ref, s_ref, e_ref, None, 6, 18)
    prepare(e_ref, level, 7, 17)

    def start(i):
        for r in range(3):
            x_ref[r, i] = OMEGA * load_ref[i] * level[6][r, i]

    loop(7, 17, start)

    def leftover(i):
        for r in range(3):
            rest_ref[r, i - 8] = KEEP * load_ref[i] + pull(x_ref, i, r, level)

    loop(8, 16, leftover)
    g_ref[0:3] = pool_own(lambda f, i: rest_ref[f, i - 8], 3, big_ref, half_ref, 1.0).reshape(3, 4, 8, 128)
    g_ref[3:6] = pool_own(lambda f, i: e_ref[f, i], 3, big_ref, half_ref, 0.25).reshape(3, 4, 8, 128)


def wide_kernel(
    place_ref, own_ref, lo_ref, hi_ref, f_ref, load_ref, *refs,
):
    level, (d_ref, v_ref, s_ref, e_ref) = refs[:7], refs[7:]
    spread_out(own_ref, lo_ref, hi_ref, (d_ref, v_ref, s_ref, load_ref))
    stiffness(place_ref, d_ref, v_ref, s_ref, e_ref, f_ref, 2, 22)
    prepare(e_ref, level, 3, 21)


def mix_kernel(place_ref, c_ref, even_ref, odd_ref, *refs):
    out_ref = refs[-1]
    mine, even = place_ref[0] % 4, (place_ref[0] // 4) % 2 == 0
    for to in range(4):
        out_ref[to, 0] = c_ref[...]
        out_ref[to, 1] = jnp.where((mine > to) == even, odd_ref[...], even_ref[...])


def window(place_ref, c_ref, even_ref, odd_ref, mixed_ref, first, into_ref):
    block = place_ref[0]
    mine, even = block % 4, (block // 4) % 2 == 0
    for b in range(9):
        at = block - 4 + b
        keep = ((at >= 0) & (at < NBX)).astype(F32)
        source = mine + (b - 4)
        for r in range(3):
            if b == 0:
                piece = jnp.where(even, odd_ref[first + r], even_ref[first + r])
            elif b == 4:
                piece = c_ref[first + r]
            elif b == 8:
                piece = jnp.where(even, even_ref[first + r], odd_ref[first + r])
            else:
                far = ((source < 0) | (source > 3)).astype(jnp.int32)
                piece = mixed_ref[(source + 4) % 4, far, first + r]
            into_ref[r, 4 * b : 4 * b + 4] = keep * piece


def second_kernel(place_ref, load_ref, *refs):
    level, (c_ref, even_ref, odd_ref, mixed_ref) = refs[:7], refs[7:11]
    one_ref, two_ref, three_ref, z0_ref, q0_ref, g_ref = refs[11:17]
    e1_ref, x_ref, y_ref, rhs_ref, out1_ref, wide_ref, big_ref, half_ref = refs[17:]
    diag_ref, inv_ref = level[5:]
    got = (place_ref, c_ref, even_ref, odd_ref, mixed_ref)
    window(*got, 3, e1_ref)
    window(*got, 0, rhs_ref)
    levels = (one_ref, two_ref, three_ref)
    set_levels(e1_ref, levels)
    coarse_all(levels, rhs_ref, out1_ref, 13, 23)
    widen_into(out1_ref, 10, wide_ref)

    def start(i):
        for r in range(3):
            x_ref[r, i] = OMEGA * load_ref[i] * inv_ref[r, i] + widened(wide_ref, r, (i - 2) // 2, 10)

    loop(3, 21, start)

    def smooth(i):
        for r in range(3):
            near = load_ref[i] + pull(x_ref, i, r, level)
            z0_ref[r, i] = KEEP * x_ref[r, i] + OMEGA * near * inv_ref[r, i]

    loop(4, 20, smooth)

    def apply(i):
        for r in range(3):
            image = diag_ref[r, i] * z0_ref[r, i] - pull(z0_ref, i, r, level)
            q0_ref[r, i] = image
            y_ref[r, i] = OMEGA * image * inv_ref[r, i]

    loop(5, 19, apply)

    def leftover(i):
        for r in range(3):
            x_ref[r, i] = KEEP * q0_ref[r, i] + pull(y_ref, i, r, level)

    loop(8, 16, leftover)
    g_ref[...] = pool_own(lambda f, i: x_ref[f, i], 3, big_ref, half_ref, 1.0).reshape(3, 4, 8, 128)


def third_kernel(place_ref, load_ref, *refs):
    level, (one_ref, two_ref, three_ref, z0_ref, q0_ref, c_ref, even_ref, odd_ref, mixed_ref) = refs[:7], refs[7:16]
    w_ref, dots_ref, x_ref, rhs_ref, out1_ref, wide_ref = refs[16:]
    diag_ref, inv_ref = level[5:]
    window(place_ref, c_ref, even_ref, odd_ref, mixed_ref, 0, rhs_ref)
    coarse_all((one_ref, two_ref, three_ref), rhs_ref, out1_ref, 14, 22)
    widen_into(out1_ref, 8, wide_ref)

    def start(i):
        for r in range(3):
            x_ref[r, i] = OMEGA * q0_ref[r, i] * inv_ref[r, i] + widened(wide_ref, r, (i - 4) // 2, 8)

    loop(5, 19, start)

    def smooth(i):
        for r in range(3):
            near = q0_ref[r, i] + pull(x_ref, i, r, level)
            w_ref[r, i] = KEEP * x_ref[r, i] + OMEGA * near * inv_ref[r, i]

    loop(6, 18, smooth)

    def add(t, sums):
        sums = list(sums)
        for i in (8 + 2 * t, 9 + 2 * t):
            for r in range(3):
                image = (diag_ref[r, i] * w_ref[r, i] - pull(w_ref, i, r, level))[:, :128]
                b, z0, q0, w = load_ref[i, :, :128], z0_ref[r, i, :, :128], q0_ref[r, i, :, :128], w_ref[r, i, :, :128]
                for q, term in enumerate((b * z0, z0 * q0, b * w, q0 * w, w * image)):
                    sums[r * 5 + q] = sums[r * 5 + q] + (term[:8] + term[8:])
        return tuple(sums)

    sums = lax.fori_loop(0, 4, add, tuple(jnp.zeros((8, 128), F32) for _ in range(15)))
    lane = iota((1, 128), 1)
    row = jnp.zeros((1, 128), F32)
    for q, v in enumerate(sums):
        row = row + jnp.where(lane == q, jnp.sum(jnp.sum(v, 0, keepdims=True), 1, keepdims=True), 0.0)
    dots_ref[...] = jnp.broadcast_to(row[None], (16, 1, 128))


def sum_kernel(in_ref, out_ref):
    out_ref[...] = jnp.broadcast_to(jnp.sum(in_ref[...], 0, keepdims=True), (16, 1, 128))


def last_kernel(place_ref, f_ref, z0_ref, w_ref, dots_ref, sens_ref, comp_ref, u_ref, comb_ref):
    real = place_ref[2]
    totals = jnp.sum(dots_ref[...], 0)
    lane = iota((1, 128), 1)
    pick = lambda q: jnp.sum(jnp.where(lane == q, totals, 0.0), 1, keepdims=True)
    factors = []
    for r in range(3):
        bz, zq, bw, qw, wa = (pick(r * 5 + q) for q in range(5))
        a0 = bz / zq
        rz1 = bz - a0 * bw - a0 * zq + (a0 * a0) * qw
        grow = 1.0 + rz1 / bz
        a1 = rz1 / ((grow * grow) * zq - 2.0 * (a0 * grow) * qw + (a0 * a0) * wa)
        c0, c1 = a0 + a1 * grow, -(a1 * a0)
        factors.append((c0, c1))
        comp_ref[r] = jnp.sum(c0 * bz + c1 * bw)
    y = iota((16, 1), 0)
    low, high = (y >= 1).astype(F32), (y < 15).astype(F32)

    def state(i):
        for r in range(3):
            u_ref[r, i] = factors[r][0] * z0_ref[r, i] + factors[r][1] * w_ref[r, i]

    loop(6, 18, state)

    def energy(i):
        total = jnp.zeros((16, 256), F32)
        for r in range(3):
            u = u_ref[r, i]
            gaps = (
                u - u_ref[r, i - 1],
                u - u_ref[r, i + 1],
                u - low * rolled(u, 1, 0),
                u - high * rolled(u, -1, 0),
                u - rolled(u, 1, 1),
                u - rolled(u, -1, 1),
            )
            square = gaps[0] * gaps[0]
            for gap in gaps[1:]:
                square = square + gap * gap
            total = total - (0.5 * square) * f_ref[r, i]
        comb_ref[i] = total

    loop(7, 17, energy)

    def spread(i):
        c = comb_ref[i]
        total = 2.0 * c + comb_ref[i + 1] + comb_ref[i - 1]
        total = total + low * rolled(c, 1, 0) + high * rolled(c, -1, 0) + rolled(c, 1, 1) + rolled(c, -1, 1)
        sens_ref[i - 8] = jnp.where(real == 0, total[:8, :128], total[8:, :128])

    loop(8, 16, spread)


def call(body, outs, scratch, *args, place=False, flops=0, out_specs=None):
    if place:
        inner = body

        def body(*refs):
            return inner((lax.axis_index(X_AXES), lax.axis_index(Y_AXES), lax.axis_index("real")), *refs)

    return pl.pallas_call(
        body,
        out_shape=outs,
        in_specs=[pl.BlockSpec(memory_space=pltpu.VMEM)] * len(args),
        **({} if out_specs is None else {"out_specs": out_specs}),
        scratch_shapes=[pltpu.VMEM(dims, F32) for dims in scratch],
        compiler_params=pltpu.CompilerParams(vmem_limit_bytes=VMEM_LIMIT),
        cost_estimate=pl.CostEstimate(flops=flops, bytes_accessed=0, transcendentals=0),
    )(*args)


Z_AXES = ("zh", "zl")
X_AXES = ("zh", "zl", "xc")
Y_AXES = ("yl", "core")
FIELD = (3, 24, 16, 256)
LEVEL1 = (3, 36, 8, 128)
SLICES = (24, 16, 256)


def swap(to_even, to_odd, axes, count):
    got = []
    for first, v in ((0, to_even), (1, to_odd)):
        pairs = [(i, i + 1) for i in range(first, count - 1, 2)]
        got.append(lax.ppermute(v, axes, pairs + [(j, i) for i, j in pairs]))
    return got


def fetch(own, *after):
    even, odd = swap(own, own, Z_AXES, 16)
    mixed = call(mix_kernel, shaped(4, 2, *own.shape), [], own, even, odd, *after, place=True)
    return own, even, odd, lax.all_to_all(mixed, "xc", 0, 0)


def body(design, load, void_mask, solid_mask):
    own = pl.pallas_call(
        pack_kernel,
        out_shape=shaped(4, 8, 8, 128),
        in_specs=[pl.BlockSpec(memory_space=pl.ANY)] * 4,
        scratch_shapes=[pltpu.VMEM((8, 8, 128), jnp.int32)] * 2 + [pltpu.SemaphoreType.DMA((4,))],
    )(design, void_mask, solid_mask, load)
    both = lax.all_gather(own, "real")
    outs = (shaped(4, 8, 16, 256), shaped(*SLICES), shaped(*SLICES))
    mine, up, down = call(select_kernel, outs, [], both, *swap(both, both, Y_AXES, 4), place=True)
    lo = lax.ppermute(up, X_AXES, [(i, i + 1) for i in range(NBX - 1)])
    hi = lax.ppermute(down, X_AXES, [(i + 1, i) for i in range(NBX - 1)])
    g = call(
        first_kernel,
        shaped(6, 4, 8, 128),
        [SLICES] * 4 + [FIELD] * 2 + [(3, 8, 16, 256), (192, 256), (192, 128)] + [FIELD] * 7,
        mine, lo, hi, place=True,
    )
    f, *level0 = call(
        wide_kernel,
        (shaped(*FIELD), shaped(*SLICES)) + (shaped(*FIELD),) * 7,
        [SLICES] * 3 + [FIELD],
        mine, lo, hi, place=True, flops=2 * 10**7,
    )
    levels = tuple(shaped(7, 3, n, 8, 128) for n in (36, 18, 9))
    *levels, z0, q0, g2 = call(
        second_kernel,
        levels + (shaped(*FIELD), shaped(*FIELD), shaped(3, 4, 8, 128)),
        [LEVEL1, FIELD, FIELD, LEVEL1, (3, 10, 8, 128), (2, 480, 128), (192, 256), (192, 128)],
        *level0, *fetch(g, level0[0]), place=True,
    )
    w, dots = call(
        third_kernel,
        (shaped(*FIELD), shaped(16, 1, 128)),
        [FIELD, LEVEL1, (3, 8, 8, 128), (2, 384, 128)],
        *level0, *levels, z0, q0, *fetch(g2), place=True,
    )
    dots = lax.all_to_all(dots, ("xc", "yl", "core"), 0, 0, tiled=True)
    dots = call(sum_kernel, shaped(16, 1, 128), [], dots)
    dots = lax.all_to_all(dots, ("zh", "zl"), 0, 0, tiled=True)
    return call(
        last_kernel,
        (shaped(8, 8, 128), shaped(3)),
        [FIELD, SLICES],
        f, z0, w, dots, place=True,
        out_specs=(pl.BlockSpec(memory_space=pltpu.VMEM), pl.BlockSpec(memory_space=pltpu.SMEM)),
    )


def solution(mesh):
    split = Mesh(mesh.devices.reshape(2, 4, 4, 4, 2, 2), ("real", "zh", "zl", "xc", "yl", "core"))
    spec = P(X_AXES, "real", Y_AXES)
    return jax.shard_map(body, mesh=split, in_specs=(spec,) * 4, out_specs=(spec, P()), check_vma=False)
```

```python
import jax
import jax.numpy as jnp
from jax import lax
from jax.experimental import pallas as pl
from jax.experimental.pallas import tpu as pltpu
from jax.sharding import Mesh
from jax.sharding import PartitionSpec as P

EMIN = 0.01
BETA = 8.0
OMEGA = 0.6
ETAS = (0.7, 0.5, 0.3)
NBX = 64
VMEM_LIMIT = 16 * 1024 * 1024
F32 = jnp.float32
HI = lax.Precision.HIGHEST


GROUP = 8


def loop(first, last, step, group=None):
    group = group or GROUP
    turns = (last - first) // group

    def turn(t, _):
        for j in range(group):
            step(first + t * group + j)
        return 0

    lax.fori_loop(0, turns, turn, 0)
    for i in range(first + turns * group, last):
        step(i)


def shaped(*dims):
    return jax.ShapeDtypeStruct(dims, F32)


def rolled(v, amount, axis):
    return pltpu.roll(v, amount % v.shape[axis], axis)


def iota(shape, axis):
    return lax.broadcasted_iota(jnp.int32, shape, axis)


def pool_matrix():
    return (iota((256, 128), 0) // 2 == iota((256, 128), 1)).astype(F32)


def widen_matrix():
    return (iota((128, 256), 1) // 2 == iota((128, 256), 0)).astype(F32)


def y_edges(rows, stride):
    y = iota((rows, 1), 0)
    low = (y >= stride).astype(F32)
    outer = 0.5 * ((y < stride).astype(F32) + (y >= rows - stride).astype(F32))
    return low, outer


def inverse(e, diag):
    return jnp.where(e > 0.0, 1.0 / jnp.where(e > 0.0, diag, 1.0), 0.0)


def prepare(e_ref, level, first, last, group=None):
    cx_ref, cy_ref, cyp_ref, cz_ref, czp_ref, diag_ref, inv_ref = level
    low, outer = y_edges(16, 1)

    def step(i):
        for r in range(3):
            e = e_ref[r, i]
            h = 0.5 * e
            cx, cxp = h + 0.5 * e_ref[r, i - 1], h + 0.5 * e_ref[r, i + 1]
            cy, cz = low * (h + rolled(h, 1, 0)), h + rolled(h, 1, 1)
            cyp, czp = rolled(cy, -1, 0), rolled(cz, -1, 1)
            diag = (cx + cxp) + (cy + cyp) + (cz + czp) + outer * e
            for ref, v in zip(level, (cx, cy, cyp, cz, czp, diag, inverse(e, diag))):
                ref[r, i] = v

    loop(first, last, step, group)
    for r in range(3):
        cx_ref[r, last] = 0.5 * (e_ref[r, last] + e_ref[r, last - 1])


def pull(u_ref, i, r, level):
    cx_ref, cy_ref, cyp_ref, cz_ref, czp_ref = level[:5]
    u = u_ref[r, i]
    total = cx_ref[r, i] * u_ref[r, i - 1] + cx_ref[r, i + 1] * u_ref[r, i + 1]
    total = total + (cy_ref[r, i] * rolled(u, 1, 0) + cyp_ref[r, i] * rolled(u, -1, 0))
    return total + (cz_ref[r, i] * rolled(u, 1, 1) + czp_ref[r, i] * rolled(u, -1, 1))


KEEP = 1.0 - OMEGA


def pool_own(src_of, many, big_ref):
    for f in range(many):
        for k in range(4):
            at = (f * 4 + k) * 16
            pair = src_of(f, 8 + 2 * k) + src_of(f, 9 + 2 * k)
            for h in range(2):
                big_ref[h, at : at + 16, :] = 0.125 * pair[:, 128 * h : 128 * h + 128]
    rows = many * 32
    halves = [big_ref[h, pl.ds(0, rows, stride=2), :] + big_ref[h, pl.ds(1, rows, stride=2), :] for h in range(2)]
    return jnp.dot(jnp.concatenate(halves, 1), pool_matrix(), precision=HI, preferred_element_type=F32)


def stack_level(e, stride):
    low, outer = y_edges(8, stride)
    h = 0.5 * e
    mid = h[1:-1]
    cx, cxp = mid + h[:-2], mid + h[2:]
    cy, cz = low * (mid + rolled(mid, stride, 1)), mid + rolled(mid, stride, 2)
    cyp, czp = rolled(cy, -stride, 1), rolled(cz, -stride, 2)
    diag = (cx + cxp) + (cy + cyp) + (cz + czp) + outer * e[1:-1]
    return cx, cxp, cy, cyp, cz, czp, inverse(e[1:-1], diag)


def stack_pull(level, u, stride, first, last):
    cx, cxp, cy, cyp, cz, czp = (v[first:last] for v in level[:6])
    mid = u[1:-1]
    total = cx * u[:-2] + cxp * u[2:]
    total = total + (cy * rolled(mid, stride, 1) + cyp * rolled(mid, -stride, 1))
    return total + (cz * rolled(mid, stride, 2) + czp * rolled(mid, -stride, 2))


def stack_pool(v, stride):
    n = v.shape[0] // 2
    v = v.reshape(n, 2, 8, 128)
    v = v[:, 0] + v[:, 1]
    y = iota((1, 8, 1), 1)
    v = v + jnp.where((y // stride) % 2 == 0, rolled(v, -stride, 1), rolled(v, stride, 1))
    z = iota((1, 1, 128), 2)
    v = v + jnp.where((z // stride) % 2 == 0, rolled(v, -stride, 2), rolled(v, stride, 2))
    return 0.125 * v


def twice(v):
    n = v.shape[0]
    return jnp.broadcast_to(v[:, None], (n, 2, 8, 128)).reshape(2 * n, 8, 128)


STRIDES = (1, 2, 4)


def set_levels(e1, level_refs):
    for r in range(3):
        e = e1[r]
        for ref, stride in zip(level_refs, STRIDES):
            for q, v in enumerate(stack_level(e, stride)):
                ref[q, r, 1 : 1 + v.shape[0]] = v
            e = 0.25 * stack_pool(e, stride) if stride < 4 else e


def coarse(levels, rhs1, first, last):
    one, two, three = levels
    x1 = OMEGA * rhs1[1:35] * one[6][1:35]
    rhs2 = stack_pool(KEEP * rhs1[2:34] + stack_pull(one, x1, 1, 2, 34), 1)
    x2 = OMEGA * rhs2 * two[6][1:17]
    rhs3 = stack_pool(KEEP * rhs2[1:15] + stack_pull(two, x2, 2, 2, 16), 2)
    x3 = OMEGA * rhs3 * three[6][1:8]
    x3 = KEEP * x3[1:6] + OMEGA * three[6][2:7] * (rhs3[1:6] + stack_pull(three, x3, 4, 2, 7))
    x2 = x2[3:13] + twice(x3)
    x2 = KEEP * x2[1:9] + OMEGA * two[6][5:13] * (rhs2[4:12] + stack_pull(two, x2, 2, 5, 13))
    x1 = x1[9:25] + twice(x2)
    x1, at = x1[first - 11 : last - 9], slice(first, last)
    return KEEP * x1[1:-1] + OMEGA * one[6][at] * (rhs1[at] + stack_pull(one, x1, 1, first, last))


def coarse_all(level_refs, rhs1, out_ref, first, last):
    for r in range(3):
        levels = [[ref[q, r] for q in range(7)] for ref in level_refs]
        out_ref[r] = coarse(levels, rhs1[r], first, last)


def widen_into(e1_ref, count, wide_ref):
    rows = 3 * count * 8
    src = jnp.concatenate([e1_ref[r, :count].reshape(count * 8, 128) for r in range(3)], 0)
    wide = jnp.dot(src, widen_matrix(), precision=HI, preferred_element_type=F32)
    for h in range(2):
        part = wide[:, 128 * h : 128 * h + 128]
        wide_ref[h, pl.ds(0, rows, stride=2), :] = part
        wide_ref[h, pl.ds(1, rows, stride=2), :] = part


def widened(wide_ref, r, k, count):
    at = pl.multiple_of((r * count + k) * 16, 16)
    return jnp.concatenate([wide_ref[0, pl.ds(at, 16), :], wide_ref[1, pl.ds(at, 16), :]], 1)


REACH = (7, 6, 6, 5)
OFFS = (0, 7, 13, 19)


def pack_kernel(d_ref, v_ref, s_ref, load_ref, out_ref, v_in, s_in, sems):
    pairs = ((d_ref, out_ref.at[0]), (v_ref, v_in), (s_ref, s_in), (load_ref, out_ref.at[3]))
    copies = [pltpu.make_async_copy(src, dst, sems.at[q]) for q, (src, dst) in enumerate(pairs)]
    for copy in copies:
        copy.start()
    copies[1].wait()
    out_ref[1] = v_in[...].astype(F32)
    copies[2].wait()
    out_ref[2] = s_in[...].astype(F32)
    copies[0].wait()
    copies[3].wait()


def select_kernel(place_ref, c_ref, a_ref, b_ref, own_ref, up_ref, down_ref):
    right = (iota((8, 128), 1) < 64) == (place_ref[1] % 2 == 0)
    for f in range(4):
        for i in range(8):
            for h in range(2):
                halo = jnp.where(right, a_ref[h, f, i], b_ref[h, f, i])
                piece = jnp.concatenate([c_ref[h, f, i], halo], 1)
                own_ref[f, i, 8 * h : 8 * h + 8, :] = piece
                if i >= 8 - REACH[f]:
                    up_ref[OFFS[f] + i - (8 - REACH[f]), 8 * h : 8 * h + 8, :] = piece
                if i < REACH[f]:
                    down_ref[OFFS[f] + i, 8 * h : 8 * h + 8, :] = piece


def spread_out(own_ref, lo_ref, hi_ref, refs):
    for f, (ref, n) in enumerate(zip(refs, REACH)):
        ref[8 - n : 8] = lo_ref[OFFS[f] : OFFS[f] + n]
        ref[8:16] = own_ref[f]
        ref[16 : 16 + n] = hi_ref[OFFS[f] : OFFS[f] + n]


def stiffness(place_ref, d_ref, v_ref, s_ref, e_ref, f_ref, first, last, group=None):
    block, gy = place_ref[0], place_ref[1]
    lane = iota((1, 256), 1)
    z = gy * 128 + jnp.where(lane < 192, lane, lane - 256)
    z_in = ((z >= 0) & (z < 512)).astype(F32)
    z_count = ((z >= 1) & (z < 513)).astype(F32) + ((z >= -1) & (z < 511)).astype(F32)
    y = iota((16, 1), 0)
    low, high = (y >= 1).astype(F32), (y < 15).astype(F32)
    yz_count = (low + high) + z_count
    shifts = []
    for eta in ETAS:
        t0 = jnp.tanh(jnp.full((1, 1), BETA * eta, F32))
        shifts.append((t0, 1.0 / (t0 + jnp.tanh(jnp.full((1, 1), BETA * (1.0 - eta), F32)))))

    def step(i):
        x = 8 * block + i - 8
        inside = lambda at: ((at >= 0) & (at < 8 * NBX)).astype(F32)
        d = d_ref[i]
        total = 2.0 * d + d_ref[i + 1] + d_ref[i - 1]
        total = total + low * rolled(d, 1, 0) + high * rolled(d, -1, 0) + rolled(d, 1, 1) + rolled(d, -1, 1)
        weight = 1.0 / (yz_count + (2.0 + inside(x - 1) + inside(x + 1)))
        here = z_in * inside(x)
        filtered = total * weight
        void, solid = v_ref[i], s_ref[i]
        open_ = 1.0 - void
        scale = here * (open_ * (1.0 - solid)) * weight
        for r, eta in enumerate(ETAS):
            t0, den = shifts[r]
            t = jnp.tanh(BETA * (filtered - eta))
            projected = (t0 + t) * den
            physical = open_ * (solid + (1.0 - solid) * projected)
            square = physical * physical
            e_ref[r, i] = here * (EMIN + (1.0 - EMIN) * (square * physical))
            if f_ref is not None:
                slope = BETA * (1.0 - t * t) * den
                f_ref[r, i] = (3.0 * (1.0 - EMIN)) * square * scale * slope

    loop(first, last, step, group)


def inner_kernel(place_ref, own_ref, load_ref, f_ref, e_ref, *refs):
    level, (d_ref, v_ref, s_ref) = refs[:7], refs[7:]
    for f, ref in enumerate((d_ref, v_ref, s_ref, load_ref)):
        ref[8:16] = own_ref[f]
    stiffness(place_ref, d_ref, v_ref, s_ref, e_ref, f_ref, 9, 15, 3)
    prepare(e_ref, level, 10, 14)


def first_kernel(place_ref, own_ref, lo_ref, hi_ref, *refs):
    g_ref, load_ref, f_ref, e_ref = refs[10:14]
    level, (d_ref, v_ref, s_ref, x_ref, rest_ref, big_ref) = refs[14:21], refs[21:]
    inv_ref = level[6]
    spread_out(own_ref, lo_ref, hi_ref, (d_ref, v_ref, s_ref, load_ref))
    for first in (6, 15):
        stiffness(place_ref, d_ref, v_ref, s_ref, e_ref, f_ref, first, first + 3, 3)
    for first in (7, 14):
        prepare(e_ref, level, first, first + 3, 3)

    def start(i):
        for r in range(3):
            x_ref[r, i] = OMEGA * load_ref[i] * inv_ref[r, i]

    loop(7, 17, start)

    def leftover(i):
        for r in range(3):
            rest_ref[r, i - 8] = KEEP * load_ref[i] + pull(x_ref, i, r, level)

    loop(8, 16, leftover)
    source = lambda f, i: rest_ref[f, i - 8] if f < 3 else 0.25 * e_ref[f - 3, i]
    g_ref[...] = pool_own(source, 6, big_ref).reshape(6, 4, 8, 128)


def wide_kernel(place_ref, own_ref, lo_ref, hi_ref, *refs):
    load_ref, f_ref, e_ref = refs[10:13]
    level, (d_ref, v_ref, s_ref) = refs[13:20], refs[20:]
    spread_out(own_ref, lo_ref, hi_ref, (d_ref, v_ref, s_ref, load_ref))
    for first in (2, 18):
        stiffness(place_ref, d_ref, v_ref, s_ref, e_ref, None, first, first + 4)
    for first in (3, 17):
        prepare(e_ref, level, first, first + 4)


def mix_kernel(place_ref, c_ref, even_ref, odd_ref, *refs):
    out_ref = refs[-1]
    mine, even = place_ref[0] % 4, (place_ref[0] // 4) % 2 == 0
    for to in range(4):
        out_ref[to, 0] = c_ref[...]
        out_ref[to, 1] = jnp.where((mine > to) == even, odd_ref[...], even_ref[...])


def window(place_ref, c_ref, even_ref, odd_ref, mixed_ref, field):
    mine, even = place_ref[0] % 4, (place_ref[0] // 4) % 2 == 0
    pieces = []
    for b in range(9):
        source = mine + (b - 4)
        if b == 0:
            piece = jnp.where(even, odd_ref[field], even_ref[field])
        elif b == 4:
            piece = c_ref[field]
        elif b == 8:
            piece = jnp.where(even, even_ref[field], odd_ref[field])
        else:
            far = ((source < 0) | (source > 3)).astype(jnp.int32)
            piece = mixed_ref[(source + 4) % 4, far, field]
        pieces.append(piece)
    return jnp.concatenate(pieces, 0)


def second_kernel(place_ref, load_ref, *refs):
    level, (c_ref, even_ref, odd_ref, mixed_ref) = refs[:7], refs[7:11]
    one_ref, two_ref, three_ref, z0_ref, q0_ref, g_ref = refs[11:17]
    x_ref, y_ref, out1_ref, wide_ref, big_ref = refs[17:]
    diag_ref, inv_ref = level[5:]
    got = (place_ref, c_ref, even_ref, odd_ref, mixed_ref)
    levels = (one_ref, two_ref, three_ref)
    set_levels([window(*got, 3 + r) for r in range(3)], levels)
    coarse_all(levels, [window(*got, r) for r in range(3)], out1_ref, 13, 23)
    widen_into(out1_ref, 10, wide_ref)

    def start(i):
        for r in range(3):
            x_ref[r, i] = OMEGA * load_ref[i] * inv_ref[r, i] + widened(wide_ref, r, (i - 2) // 2, 10)

    loop(3, 21, start)

    def smooth(i):
        for r in range(3):
            near = load_ref[i] + pull(x_ref, i, r, level)
            z0_ref[r, i] = KEEP * x_ref[r, i] + OMEGA * near * inv_ref[r, i]

    loop(4, 20, smooth)

    def apply(i):
        for r in range(3):
            image = diag_ref[r, i] * z0_ref[r, i] - pull(z0_ref, i, r, level)
            q0_ref[r, i] = image
            y_ref[r, i] = OMEGA * image * inv_ref[r, i]

    loop(5, 19, apply)

    def leftover(i):
        for r in range(3):
            x_ref[r, i] = KEEP * q0_ref[r, i] + pull(y_ref, i, r, level)

    loop(8, 16, leftover)
    g_ref[...] = pool_own(lambda f, i: x_ref[f, i], 3, big_ref).reshape(3, 4, 8, 128)


def third_kernel(place_ref, load_ref, *refs):
    level, (one_ref, two_ref, three_ref, z0_ref, q0_ref, c_ref, even_ref, odd_ref, mixed_ref) = refs[:7], refs[7:16]
    w_ref, dots_ref, x_ref, out1_ref, wide_ref = refs[16:]
    diag_ref, inv_ref = level[5:]
    rhs1 = [window(place_ref, c_ref, even_ref, odd_ref, mixed_ref, r) for r in range(3)]
    coarse_all((one_ref, two_ref, three_ref), rhs1, out1_ref, 14, 22)
    widen_into(out1_ref, 8, wide_ref)

    def start(i):
        for r in range(3):
            x_ref[r, i] = OMEGA * q0_ref[r, i] * inv_ref[r, i] + widened(wide_ref, r, (i - 4) // 2, 8)

    loop(5, 19, start, 7)

    def smooth(i):
        for r in range(3):
            near = q0_ref[r, i] + pull(x_ref, i, r, level)
            w_ref[r, i] = KEEP * x_ref[r, i] + OMEGA * near * inv_ref[r, i]

    loop(6, 18, smooth, 6)

    def add(t, sums):
        sums = list(sums)
        for i in (8 + 2 * t, 9 + 2 * t):
            for r in range(3):
                image = (diag_ref[r, i] * w_ref[r, i] - pull(w_ref, i, r, level))[:, :128]
                b, z0, q0, w = load_ref[i, :, :128], z0_ref[r, i, :, :128], q0_ref[r, i, :, :128], w_ref[r, i, :, :128]
                for q, term in enumerate((b * z0, z0 * q0, b * w, q0 * w, w * image)):
                    sums[r * 5 + q] = sums[r * 5 + q] + (term[:8] + term[8:])
        return tuple(sums)

    sums = lax.fori_loop(0, 4, add, tuple(jnp.zeros((8, 128), F32) for _ in range(15)))
    lane = iota((1, 128), 1)
    row = jnp.zeros((1, 128), F32)
    for q, v in enumerate(sums):
        row = row + jnp.where(lane == q, jnp.sum(jnp.sum(v, 0, keepdims=True), 1, keepdims=True), 0.0)
    dots_ref[...] = jnp.broadcast_to(row[None], (16, 1, 128))


def sum_kernel(in_ref, out_ref):
    out_ref[...] = jnp.broadcast_to(jnp.sum(in_ref[...], 0, keepdims=True), (16, 1, 128))


def last_kernel(place_ref, f_ref, z0_ref, w_ref, dots_ref, sens_ref, comp_ref, u_ref, comb_ref):
    real = place_ref[2]
    totals = jnp.sum(dots_ref[...], 0)
    lane = iota((1, 128), 1)
    pick = lambda q: jnp.sum(jnp.where(lane == q, totals, 0.0), 1, keepdims=True)
    factors = []
    for r in range(3):
        bz, zq, bw, qw, wa = (pick(r * 5 + q) for q in range(5))
        a0 = bz / zq
        rz1 = bz - a0 * bw - a0 * zq + (a0 * a0) * qw
        grow = 1.0 + rz1 / bz
        a1 = rz1 / ((grow * grow) * zq - 2.0 * (a0 * grow) * qw + (a0 * a0) * wa)
        c0, c1 = a0 + a1 * grow, -(a1 * a0)
        factors.append((c0, c1))
        comp_ref[r] = jnp.sum(c0 * bz + c1 * bw)
    y = iota((16, 1), 0)
    low, high = (y >= 1).astype(F32), (y < 15).astype(F32)

    def state(i):
        for r in range(3):
            u_ref[r, i] = factors[r][0] * z0_ref[r, i] + factors[r][1] * w_ref[r, i]

    loop(6, 18, state)

    def energy(i):
        total = jnp.zeros((16, 256), F32)
        for r in range(3):
            u = u_ref[r, i]
            gaps = (
                u - u_ref[r, i - 1],
                u - u_ref[r, i + 1],
                u - low * rolled(u, 1, 0),
                u - high * rolled(u, -1, 0),
                u - rolled(u, 1, 1),
                u - rolled(u, -1, 1),
            )
            square = gaps[0] * gaps[0]
            for gap in gaps[1:]:
                square = square + gap * gap
            total = total - (0.5 * square) * f_ref[r, i]
        comb_ref[i] = total

    loop(7, 17, energy)

    def spread(i):
        c = comb_ref[i]
        total = 2.0 * c + comb_ref[i + 1] + comb_ref[i - 1]
        total = total + low * rolled(c, 1, 0) + high * rolled(c, -1, 0) + rolled(c, 1, 1) + rolled(c, -1, 1)
        sens_ref[i - 8] = jnp.where(real == 0, total[:8, :128], total[8:, :128])

    loop(8, 16, spread)


def call(body, outs, scratch, *args, place=False, flops=0, out_specs=None, aliases=None):
    if place:
        inner = body

        def body(*refs):
            return inner((lax.axis_index(X_AXES), lax.axis_index(Y_AXES), lax.axis_index("real")), *refs)

    if aliases:
        out_specs = (pl.BlockSpec(memory_space=pltpu.VMEM),) * len(outs)
    return pl.pallas_call(
        body,
        out_shape=outs,
        in_specs=[pl.BlockSpec(memory_space=pltpu.VMEM)] * len(args),
        **({} if out_specs is None else {"out_specs": out_specs}),
        input_output_aliases=aliases or {},
        scratch_shapes=[pltpu.VMEM(dims, F32) for dims in scratch],
        compiler_params=pltpu.CompilerParams(vmem_limit_bytes=VMEM_LIMIT),
        cost_estimate=pl.CostEstimate(flops=flops, bytes_accessed=0, transcendentals=0),
    )(*args)


Z_AXES = ("zh", "zl")
X_AXES = ("zh", "zl", "xc")
Y_AXES = ("yl", "core")
FIELD = (3, 24, 16, 256)
SLICES = (24, 16, 256)


def swap(to_even, to_odd, axes, count):
    got = []
    for first, v in ((0, to_even), (1, to_odd)):
        pairs = [(i, i + 1) for i in range(first, count - 1, 2)]
        got.append(lax.ppermute(v, axes, pairs + [(j, i) for i, j in pairs]))
    return got


def fetch(own, *after):
    even, odd = swap(own, own, Z_AXES, 16)
    mixed = call(mix_kernel, shaped(4, 2, *own.shape), [], own, even, odd, *after, place=True)
    return own, even, odd, lax.all_to_all(mixed, "xc", 0, 0)


def body(design, load, void_mask, solid_mask):
    own = pl.pallas_call(
        pack_kernel,
        out_shape=shaped(4, 8, 8, 128),
        in_specs=[pl.BlockSpec(memory_space=pl.ANY)] * 4,
        out_specs=pl.BlockSpec(memory_space=pltpu.VMEM),
        scratch_shapes=[pltpu.VMEM((8, 8, 128), jnp.int32)] * 2 + [pltpu.SemaphoreType.DMA((4,))],
    )(design, void_mask, solid_mask, load)
    both = lax.all_gather(own, "real")
    outs = (shaped(4, 8, 16, 256), shaped(*SLICES), shaped(*SLICES))
    mine, up, down = call(select_kernel, outs, [], both, *swap(both, both, Y_AXES, 4), place=True)
    lo = lax.ppermute(up, X_AXES, [(i, i + 1) for i in range(NBX - 1)])
    hi = lax.ppermute(down, X_AXES, [(i + 1, i) for i in range(NBX - 1)])
    fields = (shaped(*SLICES),) + (shaped(*FIELD),) * 9
    kept = call(inner_kernel, fields, [SLICES] * 3, mine, place=True, flops=10**7)
    g, *kept = call(
        first_kernel,
        (shaped(6, 4, 8, 128),) + fields,
        [SLICES] * 3 + [FIELD, (3, 8, 16, 256), (2, 384, 128)],
        mine, lo, hi, *kept, place=True, aliases={3 + q: 1 + q for q in range(10)},
    )
    wide_load, f, _, *level0 = call(
        wide_kernel,
        fields,
        [SLICES] * 3,
        mine, lo, hi, *kept, place=True, flops=2 * 10**7, aliases={3 + q: q for q in range(10)},
    )
    level0 = (wide_load, *level0)
    levels = tuple(shaped(7, 3, n, 8, 128) for n in (36, 18, 9))
    *levels, z0, q0, g2 = call(
        second_kernel,
        levels + (shaped(*FIELD), shaped(*FIELD), shaped(3, 4, 8, 128)),
        [FIELD, FIELD, (3, 10, 8, 128), (2, 480, 128), (2, 192, 128)],
        *level0, *fetch(g, level0[0]), place=True,
    )
    w, dots = call(
        third_kernel,
        (shaped(*FIELD), shaped(16, 1, 128)),
        [FIELD, (3, 8, 8, 128), (2, 384, 128)],
        *level0, *levels, z0, q0, *fetch(g2), place=True,
    )
    dots = lax.all_to_all(dots, ("xc", "yl", "core"), 0, 0, tiled=True)
    dots = call(sum_kernel, shaped(16, 1, 128), [], dots)
    dots = lax.all_to_all(dots, ("zh", "zl"), 0, 0, tiled=True)
    return call(
        last_kernel,
        (shaped(8, 8, 128), shaped(3)),
        [FIELD, SLICES],
        f, z0, w, dots, place=True,
        out_specs=(pl.BlockSpec(memory_space=pltpu.VMEM), pl.BlockSpec(memory_space=pltpu.SMEM)),
    )


def solution(mesh):
    split = Mesh(mesh.devices.reshape(2, 4, 4, 4, 2, 2), ("real", "zh", "zl", "xc", "yl", "core"))
    spec = P(X_AXES, "real", Y_AXES)
    return jax.shard_map(body, mesh=split, in_specs=(spec,) * 4, out_specs=(spec, P()), check_vma=False)
```

```python
import jax
import jax.numpy as jnp
from jax import lax
from jax.experimental import pallas as pl
from jax.experimental.pallas import tpu as pltpu
from jax.sharding import Mesh
from jax.sharding import PartitionSpec as P

EMIN = 0.01
BETA = 8.0
OMEGA = 0.6
ETAS = (0.7, 0.5, 0.3)
NBX = 64
VMEM_LIMIT = 16 * 1024 * 1024
F32 = jnp.float32
HI = lax.Precision.HIGHEST


GROUP = 8


def loop(first, last, step, group=None):
    group = group or GROUP
    turns = (last - first) // group

    def turn(t, _):
        for j in range(group):
            step(first + t * group + j)
        return 0

    lax.fori_loop(0, turns, turn, 0)
    for i in range(first + turns * group, last):
        step(i)


def shaped(*dims):
    return jax.ShapeDtypeStruct(dims, F32)


def rolled(v, amount, axis):
    return pltpu.roll(v, amount % v.shape[axis], axis)


def iota(shape, axis):
    return lax.broadcasted_iota(jnp.int32, shape, axis)


def pool_matrix():
    return (iota((256, 128), 0) // 2 == iota((256, 128), 1)).astype(F32)


def widen_matrix():
    return (iota((128, 256), 1) // 2 == iota((128, 256), 0)).astype(F32)


def y_edges(rows, stride):
    y = iota((rows, 1), 0)
    low = (y >= stride).astype(F32)
    outer = 0.5 * ((y < stride).astype(F32) + (y >= rows - stride).astype(F32))
    return low, outer


def inverse(e, diag):
    return jnp.where(e > 0.0, 1.0 / jnp.where(e > 0.0, diag, 1.0), 0.0)


def prepare(e_ref, level, first, last, group=None):
    cx_ref, cy_ref, cyp_ref, cz_ref, czp_ref, diag_ref, inv_ref = level
    low, outer = y_edges(16, 1)

    def step(i):
        for r in range(3):
            e = e_ref[r, i]
            h = 0.5 * e
            cx, cxp = h + 0.5 * e_ref[r, i - 1], h + 0.5 * e_ref[r, i + 1]
            cy, cz = low * (h + rolled(h, 1, 0)), h + rolled(h, 1, 1)
            cyp, czp = rolled(cy, -1, 0), rolled(cz, -1, 1)
            diag = (cx + cxp) + (cy + cyp) + (cz + czp) + outer * e
            for ref, v in zip(level, (cx, cy, cyp, cz, czp, diag, inverse(e, diag))):
                ref[r, i] = v

    loop(first, last, step, group)
    for r in range(3):
        cx_ref[r, last] = 0.5 * (e_ref[r, last] + e_ref[r, last - 1])


def pull(u_ref, i, r, level):
    cx_ref, cy_ref, cyp_ref, cz_ref, czp_ref = level[:5]
    u = u_ref[r, i]
    total = cx_ref[r, i] * u_ref[r, i - 1] + cx_ref[r, i + 1] * u_ref[r, i + 1]
    total = total + (cy_ref[r, i] * rolled(u, 1, 0) + cyp_ref[r, i] * rolled(u, -1, 0))
    return total + (cz_ref[r, i] * rolled(u, 1, 1) + czp_ref[r, i] * rolled(u, -1, 1))


KEEP = 1.0 - OMEGA


def pool_own(src_of, many, big_ref):
    for f in range(many):
        for k in range(4):
            at = (f * 4 + k) * 16
            pair = src_of(f, 8 + 2 * k) + src_of(f, 9 + 2 * k)
            for h in range(2):
                big_ref[h, at : at + 16, :] = 0.125 * pair[:, 128 * h : 128 * h + 128]
    rows = many * 32
    halves = [big_ref[h, pl.ds(0, rows, stride=2), :] + big_ref[h, pl.ds(1, rows, stride=2), :] for h in range(2)]
    return jnp.dot(jnp.concatenate(halves, 1), pool_matrix(), precision=HI, preferred_element_type=F32)


def stack_level(e, stride):
    low, outer = y_edges(8, stride)
    h = 0.5 * e
    mid = h[1:-1]
    cx, cxp = mid + h[:-2], mid + h[2:]
    cy, cz = low * (mid + rolled(mid, stride, 1)), mid + rolled(mid, stride, 2)
    cyp, czp = rolled(cy, -stride, 1), rolled(cz, -stride, 2)
    diag = (cx + cxp) + (cy + cyp) + (cz + czp) + outer * e[1:-1]
    return cx, cxp, cy, cyp, cz, czp, inverse(e[1:-1], diag)


def stack_pull(level, u, stride, first, last):
    cx, cxp, cy, cyp, cz, czp = (v[first:last] for v in level[:6])
    mid = u[1:-1]
    total = cx * u[:-2] + cxp * u[2:]
    total = total + (cy * rolled(mid, stride, 1) + cyp * rolled(mid, -stride, 1))
    return total + (cz * rolled(mid, stride, 2) + czp * rolled(mid, -stride, 2))


def stack_pool(v, stride):
    n = v.shape[0] // 2
    v = v.reshape(n, 2, 8, 128)
    v = v[:, 0] + v[:, 1]
    y = iota((1, 8, 1), 1)
    v = v + jnp.where((y // stride) % 2 == 0, rolled(v, -stride, 1), rolled(v, stride, 1))
    z = iota((1, 1, 128), 2)
    v = v + jnp.where((z // stride) % 2 == 0, rolled(v, -stride, 2), rolled(v, stride, 2))
    return 0.125 * v


def twice(v):
    n = v.shape[0]
    return jnp.broadcast_to(v[:, None], (n, 2, 8, 128)).reshape(2 * n, 8, 128)


STRIDES = (1, 2, 4)


def set_levels(e1, level_refs):
    for r in range(3):
        e = e1[r]
        for ref, stride in zip(level_refs, STRIDES):
            for q, v in enumerate(stack_level(e, stride)):
                ref[q, r, 1 : 1 + v.shape[0]] = v
            e = 0.25 * stack_pool(e, stride) if stride < 4 else e


def coarse(levels, rhs1, first, last):
    one, two, three = levels
    x1 = OMEGA * rhs1[1:35] * one[6][1:35]
    rhs2 = stack_pool(KEEP * rhs1[2:34] + stack_pull(one, x1, 1, 2, 34), 1)
    x2 = OMEGA * rhs2 * two[6][1:17]
    rhs3 = stack_pool(KEEP * rhs2[1:15] + stack_pull(two, x2, 2, 2, 16), 2)
    x3 = OMEGA * rhs3 * three[6][1:8]
    x3 = KEEP * x3[1:6] + OMEGA * three[6][2:7] * (rhs3[1:6] + stack_pull(three, x3, 4, 2, 7))
    x2 = x2[3:13] + twice(x3)
    x2 = KEEP * x2[1:9] + OMEGA * two[6][5:13] * (rhs2[4:12] + stack_pull(two, x2, 2, 5, 13))
    x1 = x1[9:25] + twice(x2)
    x1, at = x1[first - 11 : last - 9], slice(first, last)
    return KEEP * x1[1:-1] + OMEGA * one[6][at] * (rhs1[at] + stack_pull(one, x1, 1, first, last))


def coarse_all(level_refs, rhs1, out_ref, first, last):
    for r in range(3):
        levels = [[ref[q, r] for q in range(7)] for ref in level_refs]
        out_ref[r] = coarse(levels, rhs1[r], first, last)


def widen_into(e1_ref, count, wide_ref):
    rows = 3 * count * 8
    src = jnp.concatenate([e1_ref[r, :count].reshape(count * 8, 128) for r in range(3)], 0)
    wide = jnp.dot(src, widen_matrix(), precision=HI, preferred_element_type=F32)
    for h in range(2):
        part = wide[:, 128 * h : 128 * h + 128]
        wide_ref[h, pl.ds(0, rows, stride=2), :] = part
        wide_ref[h, pl.ds(1, rows, stride=2), :] = part


def widened(wide_ref, r, k, count):
    at = pl.multiple_of((r * count + k) * 16, 16)
    return jnp.concatenate([wide_ref[0, pl.ds(at, 16), :], wide_ref[1, pl.ds(at, 16), :]], 1)


REACH = (7, 6, 6, 5)
OFFS = (0, 7, 13, 19)


def pack_kernel(d_ref, v_ref, s_ref, load_ref, out_ref, v_in, s_in, sems):
    pairs = ((d_ref, out_ref.at[0]), (v_ref, v_in), (s_ref, s_in), (load_ref, out_ref.at[3]))
    copies = [pltpu.make_async_copy(src, dst, sems.at[q]) for q, (src, dst) in enumerate(pairs)]
    for copy in copies:
        copy.start()
    copies[1].wait()
    out_ref[1] = v_in[...].astype(F32)
    copies[2].wait()
    out_ref[2] = s_in[...].astype(F32)
    copies[0].wait()
    copies[3].wait()


def halve_kernel(place_ref, c_ref, even_ref, odd_ref):
    even = place_ref[1] % 2 == 0
    low = iota((8, 128), 1) < 64
    for f in range(4):
        for i in range(4):
            for h in range(2):
                near, far = c_ref[h, f, i], c_ref[h, f, i + 4]
                begin = jnp.where(low, near, rolled(far, 64, 1))
                end = jnp.where(low, rolled(near, 64, 1), far)
                even_ref[h, f, i] = jnp.where(even, end, begin)
                odd_ref[h, f, i] = jnp.where(even, begin, end)


def select_kernel(place_ref, c_ref, even_ref, odd_ref, own_ref, up_ref, down_ref):
    even = place_ref[1] % 2 == 0
    low = iota((8, 128), 1) < 64
    for f in range(4):
        for h in range(2):
            halos = [None] * 8
            for i in range(4):
                a, b = even_ref[h, f, i], odd_ref[h, f, i]
                after, before = jnp.where(even, a, b), jnp.where(even, b, a)
                halos[i] = jnp.where(low, after, rolled(before, 64, 1))
                halos[i + 4] = jnp.where(low, rolled(after, 64, 1), before)
            for i in range(8):
                piece = jnp.concatenate([c_ref[h, f, i], halos[i]], 1)
                rows = slice(8 * h, 8 * h + 8)
                own_ref[f, i, rows, :] = piece
                if i >= 8 - REACH[f]:
                    up_ref[OFFS[f] + i - (8 - REACH[f]), rows, :] = piece
                if i < REACH[f]:
                    down_ref[OFFS[f] + i, rows, :] = piece


def spread_out(own_ref, lo_ref, hi_ref, refs):
    for f, (ref, n) in enumerate(zip(refs, REACH)):
        ref[8 - n : 8] = lo_ref[OFFS[f] : OFFS[f] + n]
        ref[8:16] = own_ref[f]
        ref[16 : 16 + n] = hi_ref[OFFS[f] : OFFS[f] + n]


def stiffness(place_ref, d_ref, v_ref, s_ref, e_ref, f_ref, first, last, group=None):
    block, gy = place_ref[0], place_ref[1]
    lane = iota((1, 256), 1)
    z = gy * 128 + jnp.where(lane < 192, lane, lane - 256)
    z_in = ((z >= 0) & (z < 512)).astype(F32)
    z_count = ((z >= 1) & (z < 513)).astype(F32) + ((z >= -1) & (z < 511)).astype(F32)
    y = iota((16, 1), 0)
    low, high = (y >= 1).astype(F32), (y < 15).astype(F32)
    yz_count = (low + high) + z_count
    shifts = []
    for eta in ETAS:
        t0 = jnp.tanh(jnp.full((1, 1), BETA * eta, F32))
        shifts.append((t0, 1.0 / (t0 + jnp.tanh(jnp.full((1, 1), BETA * (1.0 - eta), F32)))))

    def step(i):
        x = 8 * block + i - 8
        inside = lambda at: ((at >= 0) & (at < 8 * NBX)).astype(F32)
        d = d_ref[i]
        total = 2.0 * d + d_ref[i + 1] + d_ref[i - 1]
        total = total + low * rolled(d, 1, 0) + high * rolled(d, -1, 0) + rolled(d, 1, 1) + rolled(d, -1, 1)
        weight = 1.0 / (yz_count + (2.0 + inside(x - 1) + inside(x + 1)))
        here = z_in * inside(x)
        filtered = total * weight
        void, solid = v_ref[i], s_ref[i]
        open_ = 1.0 - void
        scale = here * (open_ * (1.0 - solid)) * weight
        for r, eta in enumerate(ETAS):
            t0, den = shifts[r]
            t = jnp.tanh(BETA * (filtered - eta))
            projected = (t0 + t) * den
            physical = open_ * (solid + (1.0 - solid) * projected)
            square = physical * physical
            e_ref[r, i] = here * (EMIN + (1.0 - EMIN) * (square * physical))
            if f_ref is not None:
                slope = BETA * (1.0 - t * t) * den
                f_ref[r, i] = (3.0 * (1.0 - EMIN)) * square * scale * slope

    loop(first, last, step, group)


def inner_kernel(place_ref, own_ref, load_ref, f_ref, e_ref, *refs):
    level, (d_ref, v_ref, s_ref) = refs[:7], refs[7:]
    for f, ref in enumerate((d_ref, v_ref, s_ref, load_ref)):
        ref[8:16] = own_ref[f]
    stiffness(place_ref, d_ref, v_ref, s_ref, e_ref, f_ref, 9, 15, 3)
    prepare(e_ref, level, 10, 14)


def first_kernel(place_ref, own_ref, lo_ref, hi_ref, *refs):
    g_ref, load_ref, f_ref, e_ref = refs[10:14]
    level, (d_ref, v_ref, s_ref, x_ref, rest_ref, big_ref) = refs[14:21], refs[21:]
    inv_ref = level[6]
    spread_out(own_ref, lo_ref, hi_ref, (d_ref, v_ref, s_ref, load_ref))
    for first in (6, 15):
        stiffness(place_ref, d_ref, v_ref, s_ref, e_ref, f_ref, first, first + 3, 3)
    for first in (7, 14):
        prepare(e_ref, level, first, first + 3, 3)

    def start(i):
        for r in range(3):
            x_ref[r, i] = OMEGA * load_ref[i] * inv_ref[r, i]

    loop(7, 17, start)

    def leftover(i):
        for r in range(3):
            rest_ref[r, i - 8] = KEEP * load_ref[i] + pull(x_ref, i, r, level)

    loop(8, 16, leftover)
    source = lambda f, i: rest_ref[f, i - 8] if f < 3 else 0.25 * e_ref[f - 3, i]
    g_ref[...] = pool_own(source, 6, big_ref).reshape(6, 4, 8, 128)


def wide_kernel(place_ref, own_ref, lo_ref, hi_ref, *refs):
    load_ref, f_ref, e_ref = refs[10:13]
    level, (d_ref, v_ref, s_ref) = refs[13:20], refs[20:]
    spread_out(own_ref, lo_ref, hi_ref, (d_ref, v_ref, s_ref, load_ref))
    for first in (2, 18):
        stiffness(place_ref, d_ref, v_ref, s_ref, e_ref, None, first, first + 4)
    for first in (3, 17):
        prepare(e_ref, level, first, first + 4)


def mix_kernel(place_ref, c_ref, even_ref, odd_ref, *refs):
    out_ref = refs[-1]
    mine, even = place_ref[0] % 4, (place_ref[0] // 4) % 2 == 0
    for to in range(4):
        out_ref[to, 0] = c_ref[...]
        out_ref[to, 1] = jnp.where((mine > to) == even, odd_ref[...], even_ref[...])


def window(place_ref, c_ref, even_ref, odd_ref, mixed_ref, field):
    mine, even = place_ref[0] % 4, (place_ref[0] // 4) % 2 == 0
    pieces = []
    for b in range(9):
        source = mine + (b - 4)
        if b == 0:
            piece = jnp.where(even, odd_ref[field], even_ref[field])
        elif b == 4:
            piece = c_ref[field]
        elif b == 8:
            piece = jnp.where(even, even_ref[field], odd_ref[field])
        else:
            far = ((source < 0) | (source > 3)).astype(jnp.int32)
            piece = mixed_ref[(source + 4) % 4, far, field]
        pieces.append(piece)
    return jnp.concatenate(pieces, 0)


def second_kernel(place_ref, load_ref, *refs):
    level, (c_ref, even_ref, odd_ref, mixed_ref) = refs[:7], refs[7:11]
    one_ref, two_ref, three_ref, z0_ref, q0_ref, g_ref = refs[11:17]
    x_ref, y_ref, out1_ref, wide_ref, big_ref = refs[17:]
    diag_ref, inv_ref = level[5:]
    got = (place_ref, c_ref, even_ref, odd_ref, mixed_ref)
    levels = (one_ref, two_ref, three_ref)
    set_levels([window(*got, 3 + r) for r in range(3)], levels)
    coarse_all(levels, [window(*got, r) for r in range(3)], out1_ref, 13, 23)
    widen_into(out1_ref, 10, wide_ref)

    def start(i):
        for r in range(3):
            x_ref[r, i] = OMEGA * load_ref[i] * inv_ref[r, i] + widened(wide_ref, r, (i - 2) // 2, 10)

    loop(3, 21, start)

    def smooth(i):
        for r in range(3):
            near = load_ref[i] + pull(x_ref, i, r, level)
            z0_ref[r, i] = KEEP * x_ref[r, i] + OMEGA * near * inv_ref[r, i]

    loop(4, 20, smooth)

    def apply(i):
        for r in range(3):
            image = diag_ref[r, i] * z0_ref[r, i] - pull(z0_ref, i, r, level)
            q0_ref[r, i] = image
            y_ref[r, i] = OMEGA * image * inv_ref[r, i]

    loop(5, 19, apply)

    def leftover(i):
        for r in range(3):
            x_ref[r, i] = KEEP * q0_ref[r, i] + pull(y_ref, i, r, level)

    loop(8, 16, leftover)
    g_ref[...] = pool_own(lambda f, i: x_ref[f, i], 3, big_ref).reshape(3, 4, 8, 128)


def third_kernel(place_ref, load_ref, *refs):
    level, (one_ref, two_ref, three_ref, z0_ref, q0_ref, c_ref, even_ref, odd_ref, mixed_ref) = refs[:7], refs[7:16]
    w_ref, dots_ref, x_ref, out1_ref, wide_ref = refs[16:]
    diag_ref, inv_ref = level[5:]
    rhs1 = [window(place_ref, c_ref, even_ref, odd_ref, mixed_ref, r) for r in range(3)]
    coarse_all((one_ref, two_ref, three_ref), rhs1, out1_ref, 14, 22)
    widen_into(out1_ref, 8, wide_ref)

    def start(i):
        for r in range(3):
            x_ref[r, i] = OMEGA * q0_ref[r, i] * inv_ref[r, i] + widened(wide_ref, r, (i - 4) // 2, 8)

    loop(5, 19, start, 7)

    def smooth(i):
        for r in range(3):
            near = q0_ref[r, i] + pull(x_ref, i, r, level)
            w_ref[r, i] = KEEP * x_ref[r, i] + OMEGA * near * inv_ref[r, i]

    loop(6, 18, smooth, 6)

    def add(t, sums):
        sums = list(sums)
        for i in (8 + 2 * t, 9 + 2 * t):
            for r in range(3):
                image = (diag_ref[r, i] * w_ref[r, i] - pull(w_ref, i, r, level))[:, :128]
                b, z0, q0, w = load_ref[i, :, :128], z0_ref[r, i, :, :128], q0_ref[r, i, :, :128], w_ref[r, i, :, :128]
                for q, term in enumerate((b * z0, z0 * q0, b * w, q0 * w, w * image)):
                    sums[r * 5 + q] = sums[r * 5 + q] + (term[:8] + term[8:])
        return tuple(sums)

    sums = lax.fori_loop(0, 4, add, tuple(jnp.zeros((8, 128), F32) for _ in range(15)))
    lane = iota((1, 128), 1)
    row = jnp.zeros((1, 128), F32)
    for q, v in enumerate(sums):
        row = row + jnp.where(lane == q, jnp.sum(jnp.sum(v, 0, keepdims=True), 1, keepdims=True), 0.0)
    dots_ref[...] = jnp.broadcast_to(row[None], (16, 1, 128))


def sum_kernel(in_ref, out_ref):
    out_ref[...] = jnp.broadcast_to(jnp.sum(in_ref[...], 0, keepdims=True), (16, 1, 128))


def last_kernel(place_ref, f_ref, z0_ref, w_ref, dots_ref, sens_ref, comp_ref, u_ref, comb_ref):
    real = place_ref[2]
    totals = jnp.sum(dots_ref[...], 0)
    lane = iota((1, 128), 1)
    pick = lambda q: jnp.sum(jnp.where(lane == q, totals, 0.0), 1, keepdims=True)
    factors = []
    for r in range(3):
        bz, zq, bw, qw, wa = (pick(r * 5 + q) for q in range(5))
        a0 = bz / zq
        rz1 = bz - a0 * bw - a0 * zq + (a0 * a0) * qw
        grow = 1.0 + rz1 / bz
        a1 = rz1 / ((grow * grow) * zq - 2.0 * (a0 * grow) * qw + (a0 * a0) * wa)
        c0, c1 = a0 + a1 * grow, -(a1 * a0)
        factors.append((c0, c1))
        comp_ref[r] = jnp.sum(c0 * bz + c1 * bw)
    y = iota((16, 1), 0)
    low, high = (y >= 1).astype(F32), (y < 15).astype(F32)

    def state(i):
        for r in range(3):
            u_ref[r, i] = factors[r][0] * z0_ref[r, i] + factors[r][1] * w_ref[r, i]

    loop(6, 18, state)

    def energy(i):
        total = jnp.zeros((16, 256), F32)
        for r in range(3):
            u = u_ref[r, i]
            gaps = (
                u - u_ref[r, i - 1],
                u - u_ref[r, i + 1],
                u - low * rolled(u, 1, 0),
                u - high * rolled(u, -1, 0),
                u - rolled(u, 1, 1),
                u - rolled(u, -1, 1),
            )
            square = gaps[0] * gaps[0]
            for gap in gaps[1:]:
                square = square + gap * gap
            total = total - (0.5 * square) * f_ref[r, i]
        comb_ref[i] = total

    loop(7, 17, energy)

    def spread(i):
        c = comb_ref[i]
        total = 2.0 * c + comb_ref[i + 1] + comb_ref[i - 1]
        total = total + low * rolled(c, 1, 0) + high * rolled(c, -1, 0) + rolled(c, 1, 1) + rolled(c, -1, 1)
        sens_ref[i - 8] = jnp.where(real == 0, total[:8, :128], total[8:, :128])

    loop(8, 16, spread)


def call(body, outs, scratch, *args, place=False, flops=0, out_specs=None, aliases=None):
    if place:
        inner = body

        def body(*refs):
            return inner((lax.axis_index(X_AXES), lax.axis_index(Y_AXES), lax.axis_index("real")), *refs)

    if aliases:
        out_specs = (pl.BlockSpec(memory_space=pltpu.VMEM),) * len(outs)
    return pl.pallas_call(
        body,
        out_shape=outs,
        in_specs=[pl.BlockSpec(memory_space=pltpu.VMEM)] * len(args),
        **({} if out_specs is None else {"out_specs": out_specs}),
        input_output_aliases=aliases or {},
        scratch_shapes=[pltpu.VMEM(dims, F32) for dims in scratch],
        compiler_params=pltpu.CompilerParams(vmem_limit_bytes=VMEM_LIMIT),
        cost_estimate=pl.CostEstimate(flops=flops, bytes_accessed=0, transcendentals=0),
    )(*args)


Z_AXES = ("zh", "zl")
X_AXES = ("zh", "zl", "xc")
Y_AXES = ("yl", "core")
FIELD = (3, 24, 16, 256)
SLICES = (24, 16, 256)


def swap(to_even, to_odd, axes, count):
    got = []
    for first, v in ((0, to_even), (1, to_odd)):
        pairs = [(i, i + 1) for i in range(first, count - 1, 2)]
        got.append(lax.ppermute(v, axes, pairs + [(j, i) for i, j in pairs]))
    return got


def fetch(own, *after):
    even, odd = swap(own, own, Z_AXES, 16)
    mixed = call(mix_kernel, shaped(4, 2, *own.shape), [], own, even, odd, *after, place=True)
    return own, even, odd, lax.all_to_all(mixed, "xc", 0, 0)


def body(design, load, void_mask, solid_mask):
    own = pl.pallas_call(
        pack_kernel,
        out_shape=shaped(4, 8, 8, 128),
        in_specs=[pl.BlockSpec(memory_space=pl.ANY)] * 4,
        out_specs=pl.BlockSpec(memory_space=pltpu.VMEM),
        scratch_shapes=[pltpu.VMEM((8, 8, 128), jnp.int32)] * 2 + [pltpu.SemaphoreType.DMA((4,))],
    )(design, void_mask, solid_mask, load)
    both = lax.all_gather(own, "real")
    outs = (shaped(4, 8, 16, 256), shaped(*SLICES), shaped(*SLICES))
    halves = call(halve_kernel, (shaped(2, 4, 4, 8, 128),) * 2, [], both, place=True)
    mine, up, down = call(select_kernel, outs, [], both, *swap(*halves, Y_AXES, 4), place=True)
    lo = lax.ppermute(up, X_AXES, [(i, i + 1) for i in range(NBX - 1)])
    hi = lax.ppermute(down, X_AXES, [(i + 1, i) for i in range(NBX - 1)])
    fields = (shaped(*SLICES),) + (shaped(*FIELD),) * 9
    kept = call(inner_kernel, fields, [SLICES] * 3, mine, place=True, flops=10**7)
    g, *kept = call(
        first_kernel,
        (shaped(6, 4, 8, 128),) + fields,
        [SLICES] * 3 + [FIELD, (3, 8, 16, 256), (2, 384, 128)],
        mine, lo, hi, *kept, place=True, aliases={3 + q: 1 + q for q in range(10)},
    )
    wide_load, f, _, *level0 = call(
        wide_kernel,
        fields,
        [SLICES] * 3,
        mine, lo, hi, *kept, place=True, flops=2 * 10**7, aliases={3 + q: q for q in range(10)},
    )
    level0 = (wide_load, *level0)
    levels = tuple(shaped(7, 3, n, 8, 128) for n in (36, 18, 9))
    *levels, z0, q0, g2 = call(
        second_kernel,
        levels + (shaped(*FIELD), shaped(*FIELD), shaped(3, 4, 8, 128)),
        [FIELD, FIELD, (3, 10, 8, 128), (2, 480, 128), (2, 192, 128)],
        *level0, *fetch(g, level0[0]), place=True,
    )
    w, dots = call(
        third_kernel,
        (shaped(*FIELD), shaped(16, 1, 128)),
        [FIELD, (3, 8, 8, 128), (2, 384, 128)],
        *level0, *levels, z0, q0, *fetch(g2), place=True,
    )
    dots = lax.all_to_all(dots, ("xc", "yl", "core"), 0, 0, tiled=True)
    dots = call(sum_kernel, shaped(16, 1, 128), [], dots)
    dots = lax.all_to_all(dots, ("zh", "zl"), 0, 0, tiled=True)
    return call(
        last_kernel,
        (shaped(8, 8, 128), shaped(3)),
        [FIELD, SLICES],
        f, z0, w, dots, place=True,
        out_specs=(pl.BlockSpec(memory_space=pltpu.VMEM), pl.BlockSpec(memory_space=pltpu.SMEM)),
    )


def solution(mesh):
    split = Mesh(mesh.devices.reshape(2, 4, 4, 4, 2, 2), ("real", "zh", "zl", "xc", "yl", "core"))
    spec = P(X_AXES, "real", Y_AXES)
    return jax.shard_map(body, mesh=split, in_specs=(spec,) * 4, out_specs=(spec, P()), check_vma=False)
```

```python
import jax
import jax.numpy as jnp
from jax import lax
from jax.experimental import pallas as pl
from jax.experimental.pallas import tpu as pltpu
from jax.sharding import Mesh
from jax.sharding import PartitionSpec as P

EMIN = 0.01
BETA = 8.0
OMEGA = 0.6
ETAS = (0.7, 0.5, 0.3)
NBX = 64
VMEM_LIMIT = 16 * 1024 * 1024
F32 = jnp.float32
HI = lax.Precision.HIGHEST


GROUP = 8


def loop(first, last, step, group=None):
    group = group or GROUP
    turns = (last - first) // group

    def turn(t, _):
        for j in range(group):
            step(first + t * group + j)
        return 0

    lax.fori_loop(0, turns, turn, 0)
    for i in range(first + turns * group, last):
        step(i)


def shaped(*dims):
    return jax.ShapeDtypeStruct(dims, F32)


def rolled(v, amount, axis):
    return pltpu.roll(v, amount % v.shape[axis], axis)


def iota(shape, axis):
    return lax.broadcasted_iota(jnp.int32, shape, axis)


def pool_matrix():
    return (iota((256, 128), 0) // 2 == iota((256, 128), 1)).astype(F32)


def widen_matrix():
    return (iota((128, 256), 1) // 2 == iota((128, 256), 0)).astype(F32)


def y_edges(rows, stride):
    y = iota((rows, 1), 0)
    low = (y >= stride).astype(F32)
    outer = 0.5 * ((y < stride).astype(F32) + (y >= rows - stride).astype(F32))
    return low, outer


def inverse(e, diag):
    return jnp.where(e > 0.0, 1.0 / jnp.where(e > 0.0, diag, 1.0), 0.0)


def prepare(e_ref, level, first, last, group=None):
    cx_ref, cy_ref, cyp_ref, cz_ref, czp_ref, diag_ref, inv_ref = level
    low, outer = y_edges(16, 1)

    def step(i):
        for r in range(3):
            e = e_ref[r, i]
            h = 0.5 * e
            cx, cxp = h + 0.5 * e_ref[r, i - 1], h + 0.5 * e_ref[r, i + 1]
            cy, cz = low * (h + rolled(h, 1, 0)), h + rolled(h, 1, 1)
            cyp, czp = rolled(cy, -1, 0), rolled(cz, -1, 1)
            diag = (cx + cxp) + (cy + cyp) + (cz + czp) + outer * e
            for ref, v in zip(level, (cx, cy, cyp, cz, czp, diag, inverse(e, diag))):
                ref[r, i] = v

    loop(first, last, step, group)
    for r in range(3):
        cx_ref[r, last] = 0.5 * (e_ref[r, last] + e_ref[r, last - 1])


def pull(u_ref, i, r, level):
    cx_ref, cy_ref, cyp_ref, cz_ref, czp_ref = level[:5]
    u = u_ref[r, i]
    total = cx_ref[r, i] * u_ref[r, i - 1] + cx_ref[r, i + 1] * u_ref[r, i + 1]
    total = total + (cy_ref[r, i] * rolled(u, 1, 0) + cyp_ref[r, i] * rolled(u, -1, 0))
    return total + (cz_ref[r, i] * rolled(u, 1, 1) + czp_ref[r, i] * rolled(u, -1, 1))


KEEP = 1.0 - OMEGA


def pool_own(src_of, many, big_ref):
    for f in range(many):
        for k in range(4):
            at = (f * 4 + k) * 16
            pair = src_of(f, 8 + 2 * k) + src_of(f, 9 + 2 * k)
            for h in range(2):
                big_ref[h, at : at + 16, :] = 0.125 * pair[:, 128 * h : 128 * h + 128]
    rows = many * 32
    halves = [big_ref[h, pl.ds(0, rows, stride=2), :] + big_ref[h, pl.ds(1, rows, stride=2), :] for h in range(2)]
    return jnp.dot(jnp.concatenate(halves, 1), pool_matrix(), precision=HI, preferred_element_type=F32)


def stack_level(e, stride):
    low, outer = y_edges(8, stride)
    h = 0.5 * e
    mid = h[1:-1]
    cx, cxp = mid + h[:-2], mid + h[2:]
    cy, cz = low * (mid + rolled(mid, stride, 1)), mid + rolled(mid, stride, 2)
    cyp, czp = rolled(cy, -stride, 1), rolled(cz, -stride, 2)
    diag = (cx + cxp) + (cy + cyp) + (cz + czp) + outer * e[1:-1]
    return cx, cxp, cy, cyp, cz, czp, inverse(e[1:-1], diag)


def stack_pull(level, u, stride, first, last):
    cx, cxp, cy, cyp, cz, czp = (v[first:last] for v in level[:6])
    mid = u[1:-1]
    total = cx * u[:-2] + cxp * u[2:]
    total = total + (cy * rolled(mid, stride, 1) + cyp * rolled(mid, -stride, 1))
    return total + (cz * rolled(mid, stride, 2) + czp * rolled(mid, -stride, 2))


def stack_pool(v, stride):
    n = v.shape[0] // 2
    v = v.reshape(n, 2, 8, 128)
    v = v[:, 0] + v[:, 1]
    y = iota((1, 8, 1), 1)
    v = v + jnp.where((y // stride) % 2 == 0, rolled(v, -stride, 1), rolled(v, stride, 1))
    z = iota((1, 1, 128), 2)
    v = v + jnp.where((z // stride) % 2 == 0, rolled(v, -stride, 2), rolled(v, stride, 2))
    return 0.125 * v


def twice(v):
    n = v.shape[0]
    return jnp.broadcast_to(v[:, None], (n, 2, 8, 128)).reshape(2 * n, 8, 128)


STRIDES = (1, 2, 4)


def set_levels(e1, level_refs):
    for r in range(3):
        e = e1[r]
        for ref, stride in zip(level_refs, STRIDES):
            for q, v in enumerate(stack_level(e, stride)):
                ref[q, r, 1 : 1 + v.shape[0]] = v
            e = 0.25 * stack_pool(e, stride) if stride < 4 else e


def coarse(levels, rhs1, first, last):
    one, two, three = levels
    x1 = OMEGA * rhs1[1:35] * one[6][1:35]
    rhs2 = stack_pool(KEEP * rhs1[2:34] + stack_pull(one, x1, 1, 2, 34), 1)
    x2 = OMEGA * rhs2 * two[6][1:17]
    rhs3 = stack_pool(KEEP * rhs2[1:15] + stack_pull(two, x2, 2, 2, 16), 2)
    x3 = OMEGA * rhs3 * three[6][1:8]
    x3 = KEEP * x3[1:6] + OMEGA * three[6][2:7] * (rhs3[1:6] + stack_pull(three, x3, 4, 2, 7))
    x2 = x2[3:13] + twice(x3)
    x2 = KEEP * x2[1:9] + OMEGA * two[6][5:13] * (rhs2[4:12] + stack_pull(two, x2, 2, 5, 13))
    x1 = x1[9:25] + twice(x2)
    x1, at = x1[first - 11 : last - 9], slice(first, last)
    return KEEP * x1[1:-1] + OMEGA * one[6][at] * (rhs1[at] + stack_pull(one, x1, 1, first, last))


def coarse_all(level_refs, rhs1, out_ref, first, last):
    for r in range(3):
        levels = [[ref[q, r] for q in range(7)] for ref in level_refs]
        out_ref[r] = coarse(levels, rhs1[r], first, last)


def widen_into(e1_ref, count, wide_ref):
    rows = 3 * count * 8
    src = jnp.concatenate([e1_ref[r, :count].reshape(count * 8, 128) for r in range(3)], 0)
    wide = jnp.dot(src, widen_matrix(), precision=HI, preferred_element_type=F32)
    for h in range(2):
        part = wide[:, 128 * h : 128 * h + 128]
        wide_ref[h, pl.ds(0, rows, stride=2), :] = part
        wide_ref[h, pl.ds(1, rows, stride=2), :] = part


def widened(wide_ref, r, k, count):
    at = pl.multiple_of((r * count + k) * 16, 16)
    return jnp.concatenate([wide_ref[0, pl.ds(at, 16), :], wide_ref[1, pl.ds(at, 16), :]], 1)


REACH = (7, 6, 6, 5)
WIDE = (5, 4, 4, 3)
WIDE_AT = (0, 5, 9, 13)
SENT = (41, 16, 128)


def pack_kernel(d_ref, v_ref, s_ref, load_ref, out_ref, v_in, s_in, sems):
    pairs = ((d_ref, out_ref.at[0]), (v_ref, v_in), (s_ref, s_in), (load_ref, out_ref.at[3]))
    copies = [pltpu.make_async_copy(src, dst, sems.at[q]) for q, (src, dst) in enumerate(pairs)]
    for copy in copies:
        copy.start()
    copies[1].wait()
    out_ref[1] = v_in[...].astype(F32)
    copies[2].wait()
    out_ref[2] = s_in[...].astype(F32)
    copies[0].wait()
    copies[3].wait()


def halve_kernel(place_ref, c_ref, even_ref, odd_ref):
    even = place_ref[1] % 2 == 0
    low = iota((8, 128), 1) < 64
    for f in range(4):
        for i in range(4):
            for h in range(2):
                near, far = c_ref[h, f, i], c_ref[h, f, i + 4]
                begin = jnp.where(low, near, rolled(far, 64, 1))
                end = jnp.where(low, rolled(near, 64, 1), far)
                even_ref[h, f, i] = jnp.where(even, end, begin)
                odd_ref[h, f, i] = jnp.where(even, begin, end)


def select_kernel(place_ref, c_ref, even_ref, odd_ref, own_ref, up_ref, down_ref):
    even = place_ref[1] % 2 == 0
    lane = iota((8, 128), 1)
    low = lane < 64
    for h in range(2):
        rows = slice(8 * h, 8 * h + 8)
        packed = [jnp.zeros((8, 128), F32)] * 2
        for f in range(4):
            halos = [None] * 8
            for i in range(4):
                a, b = even_ref[h, f, i], odd_ref[h, f, i]
                after, before = jnp.where(even, a, b), jnp.where(even, b, a)
                halos[i] = jnp.where(low, after, rolled(before, 64, 1))
                halos[i + 4] = jnp.where(low, rolled(after, 64, 1), before)
            for i in range(8):
                own_ref[f, i, rows, :] = jnp.concatenate([c_ref[h, f, i], halos[i]], 1)
            for depth in range(REACH[f]):
                for side, (i, ref) in enumerate(((7 - depth, up_ref), (depth, down_ref))):
                    if depth < WIDE[f]:
                        at = 2 * (WIDE_AT[f] + depth)
                        ref[at, rows, :] = c_ref[h, f, i]
                        ref[at + 1, rows, :] = halos[i]
                    else:
                        k = 2 * f + depth - WIDE[f]
                        ref[32 + k, rows, :] = c_ref[h, f, i]
                        packed[side] = jnp.where(lane // 16 == k, rolled(halos[i], 16 * k + 8, 1), packed[side])
        up_ref[40, rows, :] = packed[0]
        down_ref[40, rows, :] = packed[1]


def spread_out(own_ref, lo_ref, hi_ref, refs):
    lane = iota((16, 128), 1)
    edge = (lane < 8) | (lane >= 120)
    for f, ref in enumerate(refs):
        ref[8:16] = own_ref[f]
        for depth in range(REACH[f]):
            for i, got in ((7 - depth, lo_ref), (16 + depth, hi_ref)):
                if depth < WIDE[f]:
                    at = 2 * (WIDE_AT[f] + depth)
                    main, halo = got[at], got[at + 1]
                else:
                    k = 2 * f + depth - WIDE[f]
                    main, halo = got[32 + k], jnp.where(edge, rolled(got[40], -(16 * k + 8), 1), 0.0)
                ref[i] = jnp.concatenate([main, halo], 1)


def stiffness(place_ref, d_ref, v_ref, s_ref, e_ref, f_ref, first, last, group=None):
    block, gy = place_ref[0], place_ref[1]
    lane = iota((1, 256), 1)
    z = gy * 128 + jnp.where(lane < 192, lane, lane - 256)
    z_in = ((z >= 0) & (z < 512)).astype(F32)
    z_count = ((z >= 1) & (z < 513)).astype(F32) + ((z >= -1) & (z < 511)).astype(F32)
    y = iota((16, 1), 0)
    low, high = (y >= 1).astype(F32), (y < 15).astype(F32)
    yz_count = (low + high) + z_count
    shifts = []
    for eta in ETAS:
        t0 = jnp.tanh(jnp.full((1, 1), BETA * eta, F32))
        shifts.append((t0, 1.0 / (t0 + jnp.tanh(jnp.full((1, 1), BETA * (1.0 - eta), F32)))))

    def step(i):
        x = 8 * block + i - 8
        inside = lambda at: ((at >= 0) & (at < 8 * NBX)).astype(F32)
        d = d_ref[i]
        total = 2.0 * d + d_ref[i + 1] + d_ref[i - 1]
        total = total + low * rolled(d, 1, 0) + high * rolled(d, -1, 0) + rolled(d, 1, 1) + rolled(d, -1, 1)
        weight = 1.0 / (yz_count + (2.0 + inside(x - 1) + inside(x + 1)))
        here = z_in * inside(x)
        filtered = total * weight
        void, solid = v_ref[i], s_ref[i]
        open_ = 1.0 - void
        scale = here * (open_ * (1.0 - solid)) * weight
        for r, eta in enumerate(ETAS):
            t0, den = shifts[r]
            t = jnp.tanh(BETA * (filtered - eta))
            projected = (t0 + t) * den
            physical = open_ * (solid + (1.0 - solid) * projected)
            square = physical * physical
            e_ref[r, i] = here * (EMIN + (1.0 - EMIN) * (square * physical))
            if f_ref is not None:
                slope = BETA * (1.0 - t * t) * den
                f_ref[r, i] = (3.0 * (1.0 - EMIN)) * square * scale * slope

    loop(first, last, step, group)


def inner_kernel(place_ref, own_ref, load_ref, f_ref, e_ref, *refs):
    level, (d_ref, v_ref, s_ref) = refs[:7], refs[7:]
    for f, ref in enumerate((d_ref, v_ref, s_ref, load_ref)):
        ref[8:16] = own_ref[f]
    stiffness(place_ref, d_ref, v_ref, s_ref, e_ref, f_ref, 9, 15, 3)
    prepare(e_ref, level, 10, 14)


def first_kernel(place_ref, own_ref, lo_ref, hi_ref, *refs):
    g_ref, load_ref, f_ref, e_ref = refs[10:14]
    level, (d_ref, v_ref, s_ref, x_ref, rest_ref, big_ref) = refs[14:21], refs[21:]
    inv_ref = level[6]
    spread_out(own_ref, lo_ref, hi_ref, (d_ref, v_ref, s_ref, load_ref))
    for first in (6, 15):
        stiffness(place_ref, d_ref, v_ref, s_ref, e_ref, f_ref, first, first + 3, 3)
    for first in (7, 14):
        prepare(e_ref, level, first, first + 3, 3)

    def start(i):
        for r in range(3):
            x_ref[r, i] = OMEGA * load_ref[i] * inv_ref[r, i]

    loop(7, 17, start)

    def leftover(i):
        for r in range(3):
            rest_ref[r, i - 8] = KEEP * load_ref[i] + pull(x_ref, i, r, level)

    loop(8, 16, leftover)
    source = lambda f, i: rest_ref[f, i - 8] if f < 3 else 0.25 * e_ref[f - 3, i]
    g_ref[...] = pool_own(source, 6, big_ref).reshape(6, 4, 8, 128)


def wide_kernel(place_ref, own_ref, lo_ref, hi_ref, *refs):
    load_ref, f_ref, e_ref = refs[10:13]
    level, (d_ref, v_ref, s_ref) = refs[13:20], refs[20:]
    spread_out(own_ref, lo_ref, hi_ref, (d_ref, v_ref, s_ref, load_ref))
    for first in (2, 18):
        stiffness(place_ref, d_ref, v_ref, s_ref, e_ref, None, first, first + 4)
    for first in (3, 17):
        prepare(e_ref, level, first, first + 4)


def mix_kernel(place_ref, c_ref, even_ref, odd_ref, *refs):
    out_ref = refs[-1]
    mine, even = place_ref[0] % 4, (place_ref[0] // 4) % 2 == 0
    for to in range(4):
        out_ref[to, 0] = c_ref[...]
        out_ref[to, 1] = jnp.where((mine > to) == even, odd_ref[...], even_ref[...])


def window(place_ref, c_ref, even_ref, odd_ref, mixed_ref, field):
    mine, even = place_ref[0] % 4, (place_ref[0] // 4) % 2 == 0
    pieces = []
    for b in range(9):
        source = mine + (b - 4)
        if b == 0:
            piece = jnp.where(even, odd_ref[field], even_ref[field])
        elif b == 4:
            piece = c_ref[field]
        elif b == 8:
            piece = jnp.where(even, even_ref[field], odd_ref[field])
        else:
            far = ((source < 0) | (source > 3)).astype(jnp.int32)
            piece = mixed_ref[(source + 4) % 4, far, field]
        pieces.append(piece)
    return jnp.concatenate(pieces, 0)


def second_kernel(place_ref, load_ref, *refs):
    level, (c_ref, even_ref, odd_ref, mixed_ref) = refs[:7], refs[7:11]
    one_ref, two_ref, three_ref, z0_ref, q0_ref, g_ref = refs[11:17]
    x_ref, y_ref, out1_ref, wide_ref, big_ref = refs[17:]
    diag_ref, inv_ref = level[5:]
    got = (place_ref, c_ref, even_ref, odd_ref, mixed_ref)
    levels = (one_ref, two_ref, three_ref)
    set_levels([window(*got, 3 + r) for r in range(3)], levels)
    coarse_all(levels, [window(*got, r) for r in range(3)], out1_ref, 13, 23)
    widen_into(out1_ref, 10, wide_ref)

    def start(i):
        for r in range(3):
            x_ref[r, i] = OMEGA * load_ref[i] * inv_ref[r, i] + widened(wide_ref, r, (i - 2) // 2, 10)

    loop(3, 21, start)

    def smooth(i):
        for r in range(3):
            near = load_ref[i] + pull(x_ref, i, r, level)
            z0_ref[r, i] = KEEP * x_ref[r, i] + OMEGA * near * inv_ref[r, i]

    loop(4, 20, smooth)

    def apply(i):
        for r in range(3):
            image = diag_ref[r, i] * z0_ref[r, i] - pull(z0_ref, i, r, level)
            q0_ref[r, i] = image
            y_ref[r, i] = OMEGA * image * inv_ref[r, i]

    loop(5, 19, apply)

    def leftover(i):
        for r in range(3):
            x_ref[r, i] = KEEP * q0_ref[r, i] + pull(y_ref, i, r, level)

    loop(8, 16, leftover)
    g_ref[...] = pool_own(lambda f, i: x_ref[f, i], 3, big_ref).reshape(3, 4, 8, 128)


def third_kernel(place_ref, load_ref, *refs):
    level, (one_ref, two_ref, three_ref, z0_ref, q0_ref, c_ref, even_ref, odd_ref, mixed_ref) = refs[:7], refs[7:16]
    w_ref, dots_ref, x_ref, out1_ref, wide_ref = refs[16:]
    diag_ref, inv_ref = level[5:]
    rhs1 = [window(place_ref, c_ref, even_ref, odd_ref, mixed_ref, r) for r in range(3)]
    coarse_all((one_ref, two_ref, three_ref), rhs1, out1_ref, 14, 22)
    widen_into(out1_ref, 8, wide_ref)

    def start(i):
        for r in range(3):
            x_ref[r, i] = OMEGA * q0_ref[r, i] * inv_ref[r, i] + widened(wide_ref, r, (i - 4) // 2, 8)

    loop(5, 19, start, 7)

    def smooth(i):
        for r in range(3):
            near = q0_ref[r, i] + pull(x_ref, i, r, level)
            w_ref[r, i] = KEEP * x_ref[r, i] + OMEGA * near * inv_ref[r, i]

    loop(6, 18, smooth, 6)

    def add(t, sums):
        sums = list(sums)
        for i in (8 + 2 * t, 9 + 2 * t):
            for r in range(3):
                image = (diag_ref[r, i] * w_ref[r, i] - pull(w_ref, i, r, level))[:, :128]
                b, z0, q0, w = load_ref[i, :, :128], z0_ref[r, i, :, :128], q0_ref[r, i, :, :128], w_ref[r, i, :, :128]
                for q, term in enumerate((b * z0, z0 * q0, b * w, q0 * w, w * image)):
                    sums[r * 5 + q] = sums[r * 5 + q] + (term[:8] + term[8:])
        return tuple(sums)

    sums = lax.fori_loop(0, 4, add, tuple(jnp.zeros((8, 128), F32) for _ in range(15)))
    lane = iota((1, 128), 1)
    row = jnp.zeros((1, 128), F32)
    for q, v in enumerate(sums):
        row = row + jnp.where(lane == q, jnp.sum(jnp.sum(v, 0, keepdims=True), 1, keepdims=True), 0.0)
    dots_ref[...] = jnp.broadcast_to(row[None], (16, 1, 128))


def sum_kernel(in_ref, out_ref):
    out_ref[...] = jnp.broadcast_to(jnp.sum(in_ref[...], 0, keepdims=True), (16, 1, 128))


def last_kernel(place_ref, f_ref, z0_ref, w_ref, dots_ref, sens_ref, comp_ref, u_ref, comb_ref):
    real = place_ref[2]
    totals = jnp.sum(dots_ref[...], 0)
    lane = iota((1, 128), 1)
    pick = lambda q: jnp.sum(jnp.where(lane == q, totals, 0.0), 1, keepdims=True)
    factors = []
    for r in range(3):
        bz, zq, bw, qw, wa = (pick(r * 5 + q) for q in range(5))
        a0 = bz / zq
        rz1 = bz - a0 * bw - a0 * zq + (a0 * a0) * qw
        grow = 1.0 + rz1 / bz
        a1 = rz1 / ((grow * grow) * zq - 2.0 * (a0 * grow) * qw + (a0 * a0) * wa)
        c0, c1 = a0 + a1 * grow, -(a1 * a0)
        factors.append((c0, c1))
        comp_ref[r] = jnp.sum(c0 * bz + c1 * bw)
    y = iota((16, 1), 0)
    low, high = (y >= 1).astype(F32), (y < 15).astype(F32)

    def state(i):
        for r in range(3):
            u_ref[r, i] = factors[r][0] * z0_ref[r, i] + factors[r][1] * w_ref[r, i]

    loop(6, 18, state)

    def energy(i):
        total = jnp.zeros((16, 256), F32)
        for r in range(3):
            u = u_ref[r, i]
            gaps = (
                u - u_ref[r, i - 1],
                u - u_ref[r, i + 1],
                u - low * rolled(u, 1, 0),
                u - high * rolled(u, -1, 0),
                u - rolled(u, 1, 1),
                u - rolled(u, -1, 1),
            )
            square = gaps[0] * gaps[0]
            for gap in gaps[1:]:
                square = square + gap * gap
            total = total - (0.5 * square) * f_ref[r, i]
        comb_ref[i] = total

    loop(7, 17, energy)

    def spread(i):
        c = comb_ref[i]
        total = 2.0 * c + comb_ref[i + 1] + comb_ref[i - 1]
        total = total + low * rolled(c, 1, 0) + high * rolled(c, -1, 0) + rolled(c, 1, 1) + rolled(c, -1, 1)
        sens_ref[i - 8] = jnp.where(real == 0, total[:8, :128], total[8:, :128])

    loop(8, 16, spread)


def call(body, outs, scratch, *args, place=False, flops=0, out_specs=None, aliases=None):
    if place:
        inner = body

        def body(*refs):
            return inner((lax.axis_index(X_AXES), lax.axis_index(Y_AXES), lax.axis_index("real")), *refs)

    if aliases:
        out_specs = (pl.BlockSpec(memory_space=pltpu.VMEM),) * len(outs)
    return pl.pallas_call(
        body,
        out_shape=outs,
        in_specs=[pl.BlockSpec(memory_space=pltpu.VMEM)] * len(args),
        **({} if out_specs is None else {"out_specs": out_specs}),
        input_output_aliases=aliases or {},
        scratch_shapes=[pltpu.VMEM(dims, F32) for dims in scratch],
        compiler_params=pltpu.CompilerParams(vmem_limit_bytes=VMEM_LIMIT),
        cost_estimate=pl.CostEstimate(flops=flops, bytes_accessed=0, transcendentals=0),
    )(*args)


Z_AXES = ("zh", "zl")
X_AXES = ("zh", "zl", "xc")
Y_AXES = ("yl", "core")
FIELD = (3, 24, 16, 256)
SLICES = (24, 16, 256)


def swap(to_even, to_odd, axes, count):
    got = []
    for first, v in ((0, to_even), (1, to_odd)):
        pairs = [(i, i + 1) for i in range(first, count - 1, 2)]
        got.append(lax.ppermute(v, axes, pairs + [(j, i) for i, j in pairs]))
    return got


def fetch(own, *after):
    even, odd = swap(own, own, Z_AXES, 16)
    mixed = call(mix_kernel, shaped(4, 2, *own.shape), [], own, even, odd, *after, place=True)
    return own, even, odd, lax.all_to_all(mixed, "xc", 0, 0)


def body(design, load, void_mask, solid_mask):
    own = pl.pallas_call(
        pack_kernel,
        out_shape=shaped(4, 8, 8, 128),
        in_specs=[pl.BlockSpec(memory_space=pl.ANY)] * 4,
        out_specs=pl.BlockSpec(memory_space=pltpu.VMEM),
        scratch_shapes=[pltpu.VMEM((8, 8, 128), jnp.int32)] * 2 + [pltpu.SemaphoreType.DMA((4,))],
    )(design, void_mask, solid_mask, load)
    both = lax.all_gather(own, "real")
    outs = (shaped(4, 8, 16, 256), shaped(*SENT), shaped(*SENT))
    halves = call(halve_kernel, (shaped(2, 4, 4, 8, 128),) * 2, [], both, place=True)
    mine, up, down = call(select_kernel, outs, [], both, *swap(*halves, Y_AXES, 4), place=True)
    lo = lax.ppermute(up, X_AXES, [(i, i + 1) for i in range(NBX - 1)])
    hi = lax.ppermute(down, X_AXES, [(i + 1, i) for i in range(NBX - 1)])
    fields = (shaped(*SLICES),) + (shaped(*FIELD),) * 9
    kept = call(inner_kernel, fields, [SLICES] * 3, mine, place=True, flops=10**7)
    g, *kept = call(
        first_kernel,
        (shaped(6, 4, 8, 128),) + fields,
        [SLICES] * 3 + [FIELD, (3, 8, 16, 256), (2, 384, 128)],
        mine, lo, hi, *kept, place=True, aliases={3 + q: 1 + q for q in range(10)},
    )
    wide_load, f, _, *level0 = call(
        wide_kernel,
        fields,
        [SLICES] * 3,
        mine, lo, hi, *kept, place=True, flops=2 * 10**7, aliases={3 + q: q for q in range(10)},
    )
    level0 = (wide_load, *level0)
    levels = tuple(shaped(7, 3, n, 8, 128) for n in (36, 18, 9))
    *levels, z0, q0, g2 = call(
        second_kernel,
        levels + (shaped(*FIELD), shaped(*FIELD), shaped(3, 4, 8, 128)),
        [FIELD, FIELD, (3, 10, 8, 128), (2, 480, 128), (2, 192, 128)],
        *level0, *fetch(g, level0[0]), place=True,
    )
    w, dots = call(
        third_kernel,
        (shaped(*FIELD), shaped(16, 1, 128)),
        [FIELD, (3, 8, 8, 128), (2, 384, 128)],
        *level0, *levels, z0, q0, *fetch(g2), place=True,
    )
    dots = lax.all_to_all(dots, ("xc", "yl", "core"), 0, 0, tiled=True)
    dots = call(sum_kernel, shaped(16, 1, 128), [], dots)
    dots = lax.all_to_all(dots, ("zh", "zl"), 0, 0, tiled=True)
    return call(
        last_kernel,
        (shaped(8, 8, 128), shaped(3)),
        [FIELD, SLICES],
        f, z0, w, dots, place=True,
        out_specs=(pl.BlockSpec(memory_space=pltpu.VMEM), pl.BlockSpec(memory_space=pltpu.SMEM)),
    )


def solution(mesh):
    split = Mesh(mesh.devices.reshape(2, 4, 4, 4, 2, 2), ("real", "zh", "zl", "xc", "yl", "core"))
    spec = P(X_AXES, "real", Y_AXES)
    return jax.shard_map(body, mesh=split, in_specs=(spec,) * 4, out_specs=(spec, P()), check_vma=False)
```

```python
import jax
import jax.numpy as jnp
from jax import lax
from jax.experimental import pallas as pl
from jax.experimental.pallas import tpu as pltpu
from jax.sharding import Mesh
from jax.sharding import PartitionSpec as P

EMIN = 0.01
BETA = 8.0
OMEGA = 0.6
ETAS = (0.7, 0.5, 0.3)
NBX = 64
VMEM_LIMIT = 16 * 1024 * 1024
F32 = jnp.float32
HI = lax.Precision.HIGHEST


GROUP = 8


def loop(first, last, step, group=None):
    group = group or GROUP
    turns = (last - first) // group

    def turn(t, _):
        for j in range(group):
            step(first + t * group + j)
        return 0

    lax.fori_loop(0, turns, turn, 0)
    for i in range(first + turns * group, last):
        step(i)


def shaped(*dims):
    return jax.ShapeDtypeStruct(dims, F32)


def rolled(v, amount, axis):
    return pltpu.roll(v, amount % v.shape[axis], axis)


def iota(shape, axis):
    return lax.broadcasted_iota(jnp.int32, shape, axis)


def pool_matrix():
    return (iota((256, 128), 0) // 2 == iota((256, 128), 1)).astype(F32)


def widen_matrix():
    return (iota((128, 256), 1) // 2 == iota((128, 256), 0)).astype(F32)


def y_edges(rows, stride):
    y = iota((rows, 1), 0)
    low = (y >= stride).astype(F32)
    outer = 0.5 * ((y < stride).astype(F32) + (y >= rows - stride).astype(F32))
    return low, outer


def inverse(e, diag):
    return jnp.where(e > 0.0, 1.0 / jnp.where(e > 0.0, diag, 1.0), 0.0)


def prepare(e_ref, level, first, last, group=None):
    cx_ref, cy_ref, cyp_ref, cz_ref, czp_ref, diag_ref, inv_ref = level
    low, outer = y_edges(16, 1)

    def step(i):
        for r in range(3):
            e = e_ref[r, i]
            h = 0.5 * e
            cx, cxp = h + 0.5 * e_ref[r, i - 1], h + 0.5 * e_ref[r, i + 1]
            cy, cz = low * (h + rolled(h, 1, 0)), h + rolled(h, 1, 1)
            cyp, czp = rolled(cy, -1, 0), rolled(cz, -1, 1)
            diag = (cx + cxp) + (cy + cyp) + (cz + czp) + outer * e
            for ref, v in zip(level, (cx, cy, cyp, cz, czp, diag, inverse(e, diag))):
                ref[r, i] = v

    loop(first, last, step, group)
    for r in range(3):
        cx_ref[r, last] = 0.5 * (e_ref[r, last] + e_ref[r, last - 1])


def pull(u_ref, i, r, level):
    cx_ref, cy_ref, cyp_ref, cz_ref, czp_ref = level[:5]
    u = u_ref[r, i]
    total = cx_ref[r, i] * u_ref[r, i - 1] + cx_ref[r, i + 1] * u_ref[r, i + 1]
    total = total + (cy_ref[r, i] * rolled(u, 1, 0) + cyp_ref[r, i] * rolled(u, -1, 0))
    return total + (cz_ref[r, i] * rolled(u, 1, 1) + czp_ref[r, i] * rolled(u, -1, 1))


KEEP = 1.0 - OMEGA


def pool_own(src_of, many, big_ref):
    for f in range(many):
        for k in range(4):
            at = (f * 4 + k) * 16
            pair = src_of(f, 8 + 2 * k) + src_of(f, 9 + 2 * k)
            for h in range(2):
                big_ref[h, at : at + 16, :] = 0.125 * pair[:, 128 * h : 128 * h + 128]
    rows = many * 32
    halves = [big_ref[h, pl.ds(0, rows, stride=2), :] + big_ref[h, pl.ds(1, rows, stride=2), :] for h in range(2)]
    return jnp.dot(jnp.concatenate(halves, 1), pool_matrix(), precision=HI, preferred_element_type=F32)


def stack_level(e, stride):
    low, outer = y_edges(8, stride)
    h = 0.5 * e
    mid = h[1:-1]
    cx, cxp = mid + h[:-2], mid + h[2:]
    cy, cz = low * (mid + rolled(mid, stride, 1)), mid + rolled(mid, stride, 2)
    cyp, czp = rolled(cy, -stride, 1), rolled(cz, -stride, 2)
    diag = (cx + cxp) + (cy + cyp) + (cz + czp) + outer * e[1:-1]
    return cx, cxp, cy, cyp, cz, czp, inverse(e[1:-1], diag)


def stack_pull(level, u, stride, first, last):
    cx, cxp, cy, cyp, cz, czp = (v[first:last] for v in level[:6])
    mid = u[1:-1]
    total = cx * u[:-2] + cxp * u[2:]
    total = total + (cy * rolled(mid, stride, 1) + cyp * rolled(mid, -stride, 1))
    return total + (cz * rolled(mid, stride, 2) + czp * rolled(mid, -stride, 2))


def stack_pool(v, stride):
    n = v.shape[0] // 2
    v = v.reshape(n, 2, 8, 128)
    v = v[:, 0] + v[:, 1]
    y = iota((1, 8, 1), 1)
    v = v + jnp.where((y // stride) % 2 == 0, rolled(v, -stride, 1), rolled(v, stride, 1))
    z = iota((1, 1, 128), 2)
    v = v + jnp.where((z // stride) % 2 == 0, rolled(v, -stride, 2), rolled(v, stride, 2))
    return 0.125 * v


def twice(v):
    n = v.shape[0]
    return jnp.broadcast_to(v[:, None], (n, 2, 8, 128)).reshape(2 * n, 8, 128)


STRIDES = (1, 2, 4)


def set_levels(e1, level_refs):
    for r in range(3):
        e = e1[r]
        for ref, stride in zip(level_refs, STRIDES):
            for q, v in enumerate(stack_level(e, stride)):
                ref[q, r, 1 : 1 + v.shape[0]] = v
            e = 0.25 * stack_pool(e, stride) if stride < 4 else e


def coarse(levels, rhs1, first, last):
    one, two, three = levels
    x1 = OMEGA * rhs1[1:35] * one[6][1:35]
    rhs2 = stack_pool(KEEP * rhs1[2:34] + stack_pull(one, x1, 1, 2, 34), 1)
    x2 = OMEGA * rhs2 * two[6][1:17]
    rhs3 = stack_pool(KEEP * rhs2[1:15] + stack_pull(two, x2, 2, 2, 16), 2)
    x3 = OMEGA * rhs3 * three[6][1:8]
    x3 = KEEP * x3[1:6] + OMEGA * three[6][2:7] * (rhs3[1:6] + stack_pull(three, x3, 4, 2, 7))
    x2 = x2[3:13] + twice(x3)
    x2 = KEEP * x2[1:9] + OMEGA * two[6][5:13] * (rhs2[4:12] + stack_pull(two, x2, 2, 5, 13))
    x1 = x1[9:25] + twice(x2)
    x1, at = x1[first - 11 : last - 9], slice(first, last)
    return KEEP * x1[1:-1] + OMEGA * one[6][at] * (rhs1[at] + stack_pull(one, x1, 1, first, last))


def coarse_all(level_refs, rhs1, out_ref, first, last):
    for r in range(3):
        levels = [[ref[q, r] for q in range(7)] for ref in level_refs]
        out_ref[r] = coarse(levels, rhs1[r], first, last)


def widen_into(e1_ref, count, wide_ref):
    rows = 3 * count * 8
    src = jnp.concatenate([e1_ref[r, :count].reshape(count * 8, 128) for r in range(3)], 0)
    wide = jnp.dot(src, widen_matrix(), precision=HI, preferred_element_type=F32)
    for h in range(2):
        part = wide[:, 128 * h : 128 * h + 128]
        wide_ref[h, pl.ds(0, rows, stride=2), :] = part
        wide_ref[h, pl.ds(1, rows, stride=2), :] = part


def widened(wide_ref, r, k, count):
    at = pl.multiple_of((r * count + k) * 16, 16)
    return jnp.concatenate([wide_ref[0, pl.ds(at, 16), :], wide_ref[1, pl.ds(at, 16), :]], 1)


REACH = (7, 6, 6, 5)
OFFS = (0, 7, 13, 19)


def halve_kernel(place_ref, c_ref, even_ref, odd_ref):
    even = place_ref[1] % 2 == 0
    low = iota((8, 128), 1) < 64
    for f in range(4):
        for i in range(4):
            for h in range(2):
                near, far = c_ref[h, f, i], c_ref[h, f, i + 4]
                begin = jnp.where(low, near, rolled(far, 64, 1))
                end = jnp.where(low, rolled(near, 64, 1), far)
                even_ref[h, f, i] = jnp.where(even, end, begin)
                odd_ref[h, f, i] = jnp.where(even, begin, end)


def select_kernel(place_ref, c_ref, even_ref, odd_ref, own_ref, up_ref, down_ref):
    even = place_ref[1] % 2 == 0
    low = iota((8, 128), 1) < 64
    for f in range(4):
        for h in range(2):
            halos = [None] * 8
            for i in range(4):
                a, b = even_ref[h, f, i], odd_ref[h, f, i]
                after, before = jnp.where(even, a, b), jnp.where(even, b, a)
                halos[i] = jnp.where(low, after, rolled(before, 64, 1))
                halos[i + 4] = jnp.where(low, rolled(after, 64, 1), before)
            for i in range(8):
                piece = jnp.concatenate([c_ref[h, f, i], halos[i]], 1)
                rows = slice(8 * h, 8 * h + 8)
                own_ref[f, i, rows, :] = piece
                if i >= 8 - REACH[f]:
                    up_ref[OFFS[f] + i - (8 - REACH[f]), rows, :] = piece
                if i < REACH[f]:
                    down_ref[OFFS[f] + i, rows, :] = piece


def spread_out(own_ref, lo_ref, hi_ref, refs):
    for f, (ref, n) in enumerate(zip(refs, REACH)):
        ref[8 - n : 8] = lo_ref[OFFS[f] : OFFS[f] + n]
        ref[8:16] = own_ref[f]
        ref[16 : 16 + n] = hi_ref[OFFS[f] : OFFS[f] + n]


def stiffness(place_ref, d_ref, v_ref, s_ref, e_ref, f_ref, first, last, group=None):
    block, gy = place_ref[0], place_ref[1]
    lane = iota((1, 256), 1)
    z = gy * 128 + jnp.where(lane < 192, lane, lane - 256)
    z_in = ((z >= 0) & (z < 512)).astype(F32)
    z_count = ((z >= 1) & (z < 513)).astype(F32) + ((z >= -1) & (z < 511)).astype(F32)
    y = iota((16, 1), 0)
    low, high = (y >= 1).astype(F32), (y < 15).astype(F32)
    yz_count = (low + high) + z_count
    shifts = []
    for eta in ETAS:
        t0 = jnp.tanh(jnp.full((1, 1), BETA * eta, F32))
        shifts.append((t0, 1.0 / (t0 + jnp.tanh(jnp.full((1, 1), BETA * (1.0 - eta), F32)))))

    def step(i):
        x = 8 * block + i - 8
        inside = lambda at: ((at >= 0) & (at < 8 * NBX)).astype(F32)
        d = d_ref[i]
        total = 2.0 * d + d_ref[i + 1] + d_ref[i - 1]
        total = total + low * rolled(d, 1, 0) + high * rolled(d, -1, 0) + rolled(d, 1, 1) + rolled(d, -1, 1)
        weight = 1.0 / (yz_count + (2.0 + inside(x - 1) + inside(x + 1)))
        here = z_in * inside(x)
        filtered = total * weight
        void, solid = v_ref[i], s_ref[i]
        open_ = 1.0 - void
        scale = here * (open_ * (1.0 - solid)) * weight
        for r, eta in enumerate(ETAS):
            t0, den = shifts[r]
            t = jnp.tanh(BETA * (filtered - eta))
            projected = (t0 + t) * den
            physical = open_ * (solid + (1.0 - solid) * projected)
            square = physical * physical
            e_ref[r, i] = here * (EMIN + (1.0 - EMIN) * (square * physical))
            if f_ref is not None:
                slope = BETA * (1.0 - t * t) * den
                f_ref[r, i] = (3.0 * (1.0 - EMIN)) * square * scale * slope

    loop(first, last, step, group)


def inner_kernel(place_ref, own_ref, load_ref, f_ref, e_ref, *refs):
    level, (d_ref, v_ref, s_ref) = refs[:7], refs[7:]
    for f, ref in enumerate((d_ref, v_ref, s_ref, load_ref)):
        ref[8:16] = own_ref[f]
    stiffness(place_ref, d_ref, v_ref, s_ref, e_ref, f_ref, 9, 15, 3)
    prepare(e_ref, level, 10, 14)


def first_kernel(place_ref, own_ref, lo_ref, hi_ref, *refs):
    g_ref, load_ref, f_ref, e_ref = refs[10:14]
    level, (d_ref, v_ref, s_ref, x_ref, rest_ref, big_ref) = refs[14:21], refs[21:]
    inv_ref = level[6]
    spread_out(own_ref, lo_ref, hi_ref, (d_ref, v_ref, s_ref, load_ref))
    for first in (6, 15):
        stiffness(place_ref, d_ref, v_ref, s_ref, e_ref, f_ref, first, first + 3, 3)
    for first in (7, 14):
        prepare(e_ref, level, first, first + 3, 3)

    def start(i):
        for r in range(3):
            x_ref[r, i] = OMEGA * load_ref[i] * inv_ref[r, i]

    loop(7, 17, start)

    def leftover(i):
        for r in range(3):
            rest_ref[r, i - 8] = KEEP * load_ref[i] + pull(x_ref, i, r, level)

    loop(8, 16, leftover)
    source = lambda f, i: rest_ref[f, i - 8] if f < 3 else 0.25 * e_ref[f - 3, i]
    g_ref[...] = pool_own(source, 6, big_ref).reshape(6, 4, 8, 128)


def wide_kernel(place_ref, own_ref, lo_ref, hi_ref, *refs):
    load_ref, f_ref, e_ref = refs[10:13]
    level, (d_ref, v_ref, s_ref) = refs[13:20], refs[20:]
    spread_out(own_ref, lo_ref, hi_ref, (d_ref, v_ref, s_ref, load_ref))
    for first in (2, 18):
        stiffness(place_ref, d_ref, v_ref, s_ref, e_ref, None, first, first + 4)
    for first in (3, 17):
        prepare(e_ref, level, first, first + 4)


def mix_kernel(place_ref, c_ref, even_ref, odd_ref, *refs):
    out_ref = refs[-1]
    mine, even = place_ref[0] % 4, (place_ref[0] // 4) % 2 == 0
    for to in range(4):
        out_ref[to, 0] = c_ref[...]
        out_ref[to, 1] = jnp.where((mine > to) == even, odd_ref[...], even_ref[...])


def window(place_ref, c_ref, even_ref, odd_ref, mixed_ref, field):
    mine, even = place_ref[0] % 4, (place_ref[0] // 4) % 2 == 0
    pieces = []
    for b in range(9):
        source = mine + (b - 4)
        if b == 0:
            piece = jnp.where(even, odd_ref[field], even_ref[field])
        elif b == 4:
            piece = c_ref[field]
        elif b == 8:
            piece = jnp.where(even, even_ref[field], odd_ref[field])
        else:
            far = ((source < 0) | (source > 3)).astype(jnp.int32)
            piece = mixed_ref[(source + 4) % 4, far, field]
        pieces.append(piece)
    return jnp.concatenate(pieces, 0)


def second_kernel(place_ref, load_ref, *refs):
    level, (c_ref, even_ref, odd_ref, mixed_ref) = refs[:7], refs[7:11]
    one_ref, two_ref, three_ref, z0_ref, q0_ref, g_ref = refs[11:17]
    x_ref, y_ref, out1_ref, wide_ref, big_ref = refs[17:]
    diag_ref, inv_ref = level[5:]
    got = (place_ref, c_ref, even_ref, odd_ref, mixed_ref)
    levels = (one_ref, two_ref, three_ref)
    set_levels([window(*got, 3 + r) for r in range(3)], levels)
    coarse_all(levels, [window(*got, r) for r in range(3)], out1_ref, 13, 23)
    widen_into(out1_ref, 10, wide_ref)

    def start(i):
        for r in range(3):
            x_ref[r, i] = OMEGA * load_ref[i] * inv_ref[r, i] + widened(wide_ref, r, (i - 2) // 2, 10)

    loop(3, 21, start)

    def smooth(i):
        for r in range(3):
            near = load_ref[i] + pull(x_ref, i, r, level)
            z0_ref[r, i] = KEEP * x_ref[r, i] + OMEGA * near * inv_ref[r, i]

    loop(4, 20, smooth)

    def apply(i):
        for r in range(3):
            image = diag_ref[r, i] * z0_ref[r, i] - pull(z0_ref, i, r, level)
            q0_ref[r, i] = image
            y_ref[r, i] = OMEGA * image * inv_ref[r, i]

    loop(5, 19, apply)

    def leftover(i):
        for r in range(3):
            x_ref[r, i] = KEEP * q0_ref[r, i] + pull(y_ref, i, r, level)

    loop(8, 16, leftover)
    g_ref[...] = pool_own(lambda f, i: x_ref[f, i], 3, big_ref).reshape(3, 4, 8, 128)


def third_kernel(place_ref, load_ref, *refs):
    level, (one_ref, two_ref, three_ref, z0_ref, q0_ref, c_ref, even_ref, odd_ref, mixed_ref) = refs[:7], refs[7:16]
    w_ref, dots_ref, x_ref, out1_ref, wide_ref = refs[16:]
    diag_ref, inv_ref = level[5:]
    rhs1 = [window(place_ref, c_ref, even_ref, odd_ref, mixed_ref, r) for r in range(3)]
    coarse_all((one_ref, two_ref, three_ref), rhs1, out1_ref, 14, 22)
    widen_into(out1_ref, 8, wide_ref)

    def start(i):
        for r in range(3):
            x_ref[r, i] = OMEGA * q0_ref[r, i] * inv_ref[r, i] + widened(wide_ref, r, (i - 4) // 2, 8)

    loop(5, 19, start, 7)

    def smooth(i):
        for r in range(3):
            near = q0_ref[r, i] + pull(x_ref, i, r, level)
            w_ref[r, i] = KEEP * x_ref[r, i] + OMEGA * near * inv_ref[r, i]

    loop(6, 18, smooth, 6)

    def add(t, sums):
        sums = list(sums)
        for i in (8 + 2 * t, 9 + 2 * t):
            for r in range(3):
                image = (diag_ref[r, i] * w_ref[r, i] - pull(w_ref, i, r, level))[:, :128]
                b, z0, q0, w = load_ref[i, :, :128], z0_ref[r, i, :, :128], q0_ref[r, i, :, :128], w_ref[r, i, :, :128]
                for q, term in enumerate((b * z0, z0 * q0, b * w, q0 * w, w * image)):
                    sums[r * 5 + q] = sums[r * 5 + q] + (term[:8] + term[8:])
        return tuple(sums)

    sums = lax.fori_loop(0, 4, add, tuple(jnp.zeros((8, 128), F32) for _ in range(15)))
    lane = iota((1, 128), 1)
    row = jnp.zeros((1, 128), F32)
    for q, v in enumerate(sums):
        row = row + jnp.where(lane == q, jnp.sum(jnp.sum(v, 0, keepdims=True), 1, keepdims=True), 0.0)
    dots_ref[...] = jnp.broadcast_to(row[None], (16, 1, 128))


def sum_kernel(in_ref, out_ref):
    out_ref[...] = jnp.broadcast_to(jnp.sum(in_ref[...], 0, keepdims=True), (16, 1, 128))


def last_kernel(place_ref, f_ref, z0_ref, w_ref, dots_ref, sens_ref, comp_ref, u_ref, comb_ref):
    real = place_ref[2]
    totals = jnp.sum(dots_ref[...], 0)
    lane = iota((1, 128), 1)
    pick = lambda q: jnp.sum(jnp.where(lane == q, totals, 0.0), 1, keepdims=True)
    factors = []
    for r in range(3):
        bz, zq, bw, qw, wa = (pick(r * 5 + q) for q in range(5))
        a0 = bz / zq
        rz1 = bz - a0 * bw - a0 * zq + (a0 * a0) * qw
        grow = 1.0 + rz1 / bz
        a1 = rz1 / ((grow * grow) * zq - 2.0 * (a0 * grow) * qw + (a0 * a0) * wa)
        c0, c1 = a0 + a1 * grow, -(a1 * a0)
        factors.append((c0, c1))
        comp_ref[r] = jnp.sum(c0 * bz + c1 * bw)
    y = iota((16, 1), 0)
    low, high = (y >= 1).astype(F32), (y < 15).astype(F32)

    def state(i):
        for r in range(3):
            u_ref[r, i] = factors[r][0] * z0_ref[r, i] + factors[r][1] * w_ref[r, i]

    loop(6, 18, state)

    def energy(i):
        total = jnp.zeros((16, 256), F32)
        for r in range(3):
            u = u_ref[r, i]
            gaps = (
                u - u_ref[r, i - 1],
                u - u_ref[r, i + 1],
                u - low * rolled(u, 1, 0),
                u - high * rolled(u, -1, 0),
                u - rolled(u, 1, 1),
                u - rolled(u, -1, 1),
            )
            square = gaps[0] * gaps[0]
            for gap in gaps[1:]:
                square = square + gap * gap
            total = total - (0.5 * square) * f_ref[r, i]
        comb_ref[i] = total

    loop(7, 17, energy)

    def spread(i):
        c = comb_ref[i]
        total = 2.0 * c + comb_ref[i + 1] + comb_ref[i - 1]
        total = total + low * rolled(c, 1, 0) + high * rolled(c, -1, 0) + rolled(c, 1, 1) + rolled(c, -1, 1)
        sens_ref[i - 8] = jnp.where(real == 0, total[:8, :128], total[8:, :128])

    loop(8, 16, spread)


def call(body, outs, scratch, *args, place=False, flops=0, out_specs=None, aliases=None):
    if place:
        inner = body

        def body(*refs):
            return inner((lax.axis_index(X_AXES), lax.axis_index(Y_AXES), lax.axis_index("real")), *refs)

    if aliases:
        out_specs = (pl.BlockSpec(memory_space=pltpu.VMEM),) * len(outs)
    return pl.pallas_call(
        body,
        out_shape=outs,
        in_specs=[pl.BlockSpec(memory_space=pltpu.VMEM)] * len(args),
        **({} if out_specs is None else {"out_specs": out_specs}),
        input_output_aliases=aliases or {},
        scratch_shapes=[pltpu.VMEM(dims, F32) for dims in scratch],
        compiler_params=pltpu.CompilerParams(vmem_limit_bytes=VMEM_LIMIT),
        cost_estimate=pl.CostEstimate(flops=flops, bytes_accessed=0, transcendentals=0),
    )(*args)


Z_AXES = ("zh", "zl")
X_AXES = ("zh", "zl", "xc")
Y_AXES = ("yl", "core")
FIELD = (3, 24, 16, 256)
SLICES = (24, 16, 256)


def swap(to_even, to_odd, axes, count):
    got = []
    for first, v in ((0, to_even), (1, to_odd)):
        pairs = [(i, i + 1) for i in range(first, count - 1, 2)]
        got.append(lax.ppermute(v, axes, pairs + [(j, i) for i, j in pairs]))
    return got


def fetch(own, *after):
    even, odd = swap(own, own, Z_AXES, 16)
    mixed = call(mix_kernel, shaped(4, 2, *own.shape), [], own, even, odd, *after, place=True)
    return own, even, odd, lax.all_to_all(mixed, "xc", 0, 0)


def body(design, load, void_mask, solid_mask):
    which = iota((4, 8, 8, 128), 0)
    masks = jnp.where(which == 1, void_mask[None], solid_mask[None]).astype(F32)
    own = jnp.where(which == 0, design[None], jnp.where(which == 3, load[None], masks))
    both = lax.all_gather(own, "real")
    outs = (shaped(4, 8, 16, 256), shaped(*SLICES), shaped(*SLICES))
    halves = call(halve_kernel, (shaped(2, 4, 4, 8, 128),) * 2, [], both, place=True)
    mine, up, down = call(select_kernel, outs, [], both, *swap(*halves, Y_AXES, 4), place=True)
    lo = lax.ppermute(up, X_AXES, [(i, i + 1) for i in range(NBX - 1)])
    hi = lax.ppermute(down, X_AXES, [(i + 1, i) for i in range(NBX - 1)])
    fields = (shaped(*SLICES),) + (shaped(*FIELD),) * 9
    kept = call(inner_kernel, fields, [SLICES] * 3, mine, place=True, flops=10**7)
    g, *kept = call(
        first_kernel,
        (shaped(6, 4, 8, 128),) + fields,
        [SLICES] * 3 + [FIELD, (3, 8, 16, 256), (2, 384, 128)],
        mine, lo, hi, *kept, place=True, aliases={3 + q: 1 + q for q in range(10)},
    )
    wide_load, f, _, *level0 = call(
        wide_kernel,
        fields,
        [SLICES] * 3,
        mine, lo, hi, *kept, place=True, flops=2 * 10**7, aliases={3 + q: q for q in range(10)},
    )
    level0 = (wide_load, *level0)
    levels = tuple(shaped(7, 3, n, 8, 128) for n in (36, 18, 9))
    *levels, z0, q0, g2 = call(
        second_kernel,
        levels + (shaped(*FIELD), shaped(*FIELD), shaped(3, 4, 8, 128)),
        [FIELD, FIELD, (3, 10, 8, 128), (2, 480, 128), (2, 192, 128)],
        *level0, *fetch(g, level0[0]), place=True,
    )
    w, dots = call(
        third_kernel,
        (shaped(*FIELD), shaped(16, 1, 128)),
        [FIELD, (3, 8, 8, 128), (2, 384, 128)],
        *level0, *levels, z0, q0, *fetch(g2), place=True,
    )
    dots = lax.all_to_all(dots, ("xc", "yl", "core"), 0, 0, tiled=True)
    dots = call(sum_kernel, shaped(16, 1, 128), [], dots)
    dots = lax.all_to_all(dots, ("zh", "zl"), 0, 0, tiled=True)
    return call(
        last_kernel,
        (shaped(8, 8, 128), shaped(3)),
        [FIELD, SLICES],
        f, z0, w, dots, place=True,
        out_specs=(pl.BlockSpec(memory_space=pltpu.VMEM), pl.BlockSpec(memory_space=pltpu.SMEM)),
    )


def solution(mesh):
    split = Mesh(mesh.devices.reshape(2, 4, 4, 4, 2, 2), ("real", "zh", "zl", "xc", "yl", "core"))
    spec = P(X_AXES, "real", Y_AXES)
    return jax.shard_map(body, mesh=split, in_specs=(spec,) * 4, out_specs=(spec, P()), check_vma=False)
```

```python
import jax
import jax.numpy as jnp
from jax import lax
from jax.experimental import pallas as pl
from jax.experimental.pallas import tpu as pltpu
from jax.sharding import Mesh
from jax.sharding import PartitionSpec as P

EMIN = 0.01
BETA = 8.0
OMEGA = 0.6
ETAS = (0.7, 0.5, 0.3)
NBX = 64
VMEM_LIMIT = 16 * 1024 * 1024
F32 = jnp.float32
HI = lax.Precision.HIGHEST


GROUP = 8


def loop(first, last, step, group=None):
    group = group or GROUP
    turns = (last - first) // group

    def turn(t, _):
        for j in range(group):
            step(first + t * group + j)
        return 0

    lax.fori_loop(0, turns, turn, 0)
    for i in range(first + turns * group, last):
        step(i)


def shaped(*dims):
    return jax.ShapeDtypeStruct(dims, F32)


def rolled(v, amount, axis):
    return pltpu.roll(v, amount % v.shape[axis], axis)


def iota(shape, axis):
    return lax.broadcasted_iota(jnp.int32, shape, axis)


def pool_matrix():
    return (iota((256, 128), 0) // 2 == iota((256, 128), 1)).astype(F32)


def widen_matrix():
    return (iota((128, 256), 1) // 2 == iota((128, 256), 0)).astype(F32)


def y_edges(rows, stride):
    y = iota((rows, 1), 0)
    low = (y >= stride).astype(F32)
    outer = 0.5 * ((y < stride).astype(F32) + (y >= rows - stride).astype(F32))
    return low, outer


def inverse(e, diag):
    return jnp.where(e > 0.0, 1.0 / jnp.where(e > 0.0, diag, 1.0), 0.0)


def prepare(e_ref, level, first, last, group=None):
    cx_ref, cy_ref, cyp_ref, cz_ref, czp_ref, diag_ref, inv_ref = level
    low, outer = y_edges(16, 1)

    def step(i):
        for r in range(3):
            e = e_ref[r, i]
            h = 0.5 * e
            cx, cxp = h + 0.5 * e_ref[r, i - 1], h + 0.5 * e_ref[r, i + 1]
            cy, cz = low * (h + rolled(h, 1, 0)), h + rolled(h, 1, 1)
            cyp, czp = rolled(cy, -1, 0), rolled(cz, -1, 1)
            diag = (cx + cxp) + (cy + cyp) + (cz + czp) + outer * e
            for ref, v in zip(level, (cx, cy, cyp, cz, czp, diag, inverse(e, diag))):
                ref[r, i] = v

    loop(first, last, step, group)
    for r in range(3):
        cx_ref[r, last] = 0.5 * (e_ref[r, last] + e_ref[r, last - 1])


def pull(u_ref, i, r, level):
    cx_ref, cy_ref, cyp_ref, cz_ref, czp_ref = level[:5]
    u = u_ref[r, i]
    total = cx_ref[r, i] * u_ref[r, i - 1] + cx_ref[r, i + 1] * u_ref[r, i + 1]
    total = total + (cy_ref[r, i] * rolled(u, 1, 0) + cyp_ref[r, i] * rolled(u, -1, 0))
    return total + (cz_ref[r, i] * rolled(u, 1, 1) + czp_ref[r, i] * rolled(u, -1, 1))


KEEP = 1.0 - OMEGA


def pool_own(src_of, many, big_ref):
    for f in range(many):
        for k in range(4):
            at = (f * 4 + k) * 16
            pair = src_of(f, 8 + 2 * k) + src_of(f, 9 + 2 * k)
            for h in range(2):
                big_ref[h, at : at + 16, :] = 0.125 * pair[:, 128 * h : 128 * h + 128]
    rows = many * 32
    halves = [big_ref[h, pl.ds(0, rows, stride=2), :] + big_ref[h, pl.ds(1, rows, stride=2), :] for h in range(2)]
    return jnp.dot(jnp.concatenate(halves, 1), pool_matrix(), precision=HI, preferred_element_type=F32)


def stack_level(e, stride):
    low, outer = y_edges(8, stride)
    h = 0.5 * e
    mid = h[1:-1]
    cx, cxp = mid + h[:-2], mid + h[2:]
    cy, cz = low * (mid + rolled(mid, stride, 1)), mid + rolled(mid, stride, 2)
    cyp, czp = rolled(cy, -stride, 1), rolled(cz, -stride, 2)
    diag = (cx + cxp) + (cy + cyp) + (cz + czp) + outer * e[1:-1]
    return cx, cxp, cy, cyp, cz, czp, inverse(e[1:-1], diag)


def stack_pull(level, u, stride, first, last):
    cx, cxp, cy, cyp, cz, czp = (v[first:last] for v in level[:6])
    mid = u[1:-1]
    total = cx * u[:-2] + cxp * u[2:]
    total = total + (cy * rolled(mid, stride, 1) + cyp * rolled(mid, -stride, 1))
    return total + (cz * rolled(mid, stride, 2) + czp * rolled(mid, -stride, 2))


def stack_pool(v, stride):
    n = v.shape[0] // 2
    v = v.reshape(n, 2, 8, 128)
    v = v[:, 0] + v[:, 1]
    y = iota((1, 8, 1), 1)
    v = v + jnp.where((y // stride) % 2 == 0, rolled(v, -stride, 1), rolled(v, stride, 1))
    z = iota((1, 1, 128), 2)
    v = v + jnp.where((z // stride) % 2 == 0, rolled(v, -stride, 2), rolled(v, stride, 2))
    return 0.125 * v


def twice(v):
    n = v.shape[0]
    return jnp.broadcast_to(v[:, None], (n, 2, 8, 128)).reshape(2 * n, 8, 128)


STRIDES = (1, 2, 4)


def set_levels(e1, level_refs):
    for r in range(3):
        e = e1[r]
        for ref, stride in zip(level_refs, STRIDES):
            for q, v in enumerate(stack_level(e, stride)):
                ref[q, r, 1 : 1 + v.shape[0]] = v
            e = 0.25 * stack_pool(e, stride) if stride < 4 else e


def coarse(levels, rhs1, first, last):
    one, two, three = levels
    x1 = OMEGA * rhs1[1:35] * one[6][1:35]
    rhs2 = stack_pool(KEEP * rhs1[2:34] + stack_pull(one, x1, 1, 2, 34), 1)
    x2 = OMEGA * rhs2 * two[6][1:17]
    rhs3 = stack_pool(KEEP * rhs2[1:15] + stack_pull(two, x2, 2, 2, 16), 2)
    x3 = OMEGA * rhs3 * three[6][1:8]
    x3 = KEEP * x3[1:6] + OMEGA * three[6][2:7] * (rhs3[1:6] + stack_pull(three, x3, 4, 2, 7))
    x2 = x2[3:13] + twice(x3)
    x2 = KEEP * x2[1:9] + OMEGA * two[6][5:13] * (rhs2[4:12] + stack_pull(two, x2, 2, 5, 13))
    x1 = x1[9:25] + twice(x2)
    x1, at = x1[first - 11 : last - 9], slice(first, last)
    return KEEP * x1[1:-1] + OMEGA * one[6][at] * (rhs1[at] + stack_pull(one, x1, 1, first, last))


def coarse_all(level_refs, rhs1, out_ref, first, last):
    for r in range(3):
        levels = [[ref[q, r] for q in range(7)] for ref in level_refs]
        out_ref[r] = coarse(levels, rhs1[r], first, last)


def widen_into(e1_ref, count, wide_ref):
    rows = 3 * count * 8
    src = jnp.concatenate([e1_ref[r, :count].reshape(count * 8, 128) for r in range(3)], 0)
    wide = jnp.dot(src, widen_matrix(), precision=HI, preferred_element_type=F32)
    for h in range(2):
        part = wide[:, 128 * h : 128 * h + 128]
        wide_ref[h, pl.ds(0, rows, stride=2), :] = part
        wide_ref[h, pl.ds(1, rows, stride=2), :] = part


def widened(wide_ref, r, k, count):
    at = pl.multiple_of((r * count + k) * 16, 16)
    return jnp.concatenate([wide_ref[0, pl.ds(at, 16), :], wide_ref[1, pl.ds(at, 16), :]], 1)


REACH = (7, 6, 6, 5)
WIDE = (5, 4, 4, 3)
WIDE_AT = (0, 5, 9, 13)
SENT = (41, 16, 128)


def halve_kernel(place_ref, c_ref, even_ref, odd_ref):
    even = place_ref[1] % 2 == 0
    low = iota((8, 128), 1) < 64
    for f in range(4):
        for i in range(4):
            for h in range(2):
                near, far = c_ref[h, f, i], c_ref[h, f, i + 4]
                begin = jnp.where(low, near, rolled(far, 64, 1))
                end = jnp.where(low, rolled(near, 64, 1), far)
                even_ref[h, f, i] = jnp.where(even, end, begin)
                odd_ref[h, f, i] = jnp.where(even, begin, end)


def select_kernel(place_ref, c_ref, even_ref, odd_ref, own_ref, up_ref, down_ref):
    even = place_ref[1] % 2 == 0
    lane = iota((8, 128), 1)
    low = lane < 64
    for h in range(2):
        rows = slice(8 * h, 8 * h + 8)
        packed = [jnp.zeros((8, 128), F32)] * 2
        for f in range(4):
            halos = [None] * 8
            for i in range(4):
                a, b = even_ref[h, f, i], odd_ref[h, f, i]
                after, before = jnp.where(even, a, b), jnp.where(even, b, a)
                halos[i] = jnp.where(low, after, rolled(before, 64, 1))
                halos[i + 4] = jnp.where(low, rolled(after, 64, 1), before)
            for i in range(8):
                own_ref[f, i, rows, :] = jnp.concatenate([c_ref[h, f, i], halos[i]], 1)
            for depth in range(REACH[f]):
                for side, (i, ref) in enumerate(((7 - depth, up_ref), (depth, down_ref))):
                    if depth < WIDE[f]:
                        at = 2 * (WIDE_AT[f] + depth)
                        ref[at, rows, :] = c_ref[h, f, i]
                        ref[at + 1, rows, :] = halos[i]
                    else:
                        k = 2 * f + depth - WIDE[f]
                        ref[32 + k, rows, :] = c_ref[h, f, i]
                        packed[side] = jnp.where(lane // 16 == k, rolled(halos[i], 16 * k + 8, 1), packed[side])
        up_ref[40, rows, :] = packed[0]
        down_ref[40, rows, :] = packed[1]


def spread_out(own_ref, lo_ref, hi_ref, refs):
    lane = iota((16, 128), 1)
    edge = (lane < 8) | (lane >= 120)
    for f, ref in enumerate(refs):
        ref[8:16] = own_ref[f]
        for depth in range(REACH[f]):
            for i, got in ((7 - depth, lo_ref), (16 + depth, hi_ref)):
                if depth < WIDE[f]:
                    at = 2 * (WIDE_AT[f] + depth)
                    main, halo = got[at], got[at + 1]
                else:
                    k = 2 * f + depth - WIDE[f]
                    main, halo = got[32 + k], jnp.where(edge, rolled(got[40], -(16 * k + 8), 1), 0.0)
                ref[i] = jnp.concatenate([main, halo], 1)


def stiffness(place_ref, d_ref, v_ref, s_ref, e_ref, f_ref, first, last, group=None):
    block, gy = place_ref[0], place_ref[1]
    lane = iota((1, 256), 1)
    z = gy * 128 + jnp.where(lane < 192, lane, lane - 256)
    z_in = ((z >= 0) & (z < 512)).astype(F32)
    z_count = ((z >= 1) & (z < 513)).astype(F32) + ((z >= -1) & (z < 511)).astype(F32)
    y = iota((16, 1), 0)
    low, high = (y >= 1).astype(F32), (y < 15).astype(F32)
    yz_count = (low + high) + z_count
    shifts = []
    for eta in ETAS:
        t0 = jnp.tanh(jnp.full((1, 1), BETA * eta, F32))
        shifts.append((t0, 1.0 / (t0 + jnp.tanh(jnp.full((1, 1), BETA * (1.0 - eta), F32)))))

    def step(i):
        x = 8 * block + i - 8
        inside = lambda at: ((at >= 0) & (at < 8 * NBX)).astype(F32)
        d = d_ref[i]
        total = 2.0 * d + d_ref[i + 1] + d_ref[i - 1]
        total = total + low * rolled(d, 1, 0) + high * rolled(d, -1, 0) + rolled(d, 1, 1) + rolled(d, -1, 1)
        weight = 1.0 / (yz_count + (2.0 + inside(x - 1) + inside(x + 1)))
        here = z_in * inside(x)
        filtered = total * weight
        void, solid = v_ref[i], s_ref[i]
        open_ = 1.0 - void
        scale = here * (open_ * (1.0 - solid)) * weight
        for r, eta in enumerate(ETAS):
            t0, den = shifts[r]
            t = jnp.tanh(BETA * (filtered - eta))
            projected = (t0 + t) * den
            physical = open_ * (solid + (1.0 - solid) * projected)
            square = physical * physical
            e_ref[r, i] = here * (EMIN + (1.0 - EMIN) * (square * physical))
            if f_ref is not None:
                slope = BETA * (1.0 - t * t) * den
                f_ref[r, i] = (3.0 * (1.0 - EMIN)) * square * scale * slope

    loop(first, last, step, group)


def inner_kernel(place_ref, own_ref, load_ref, f_ref, e_ref, *refs):
    level, (d_ref, v_ref, s_ref) = refs[:7], refs[7:]
    for f, ref in enumerate((d_ref, v_ref, s_ref, load_ref)):
        ref[8:16] = own_ref[f]
    stiffness(place_ref, d_ref, v_ref, s_ref, e_ref, f_ref, 9, 15, 3)
    prepare(e_ref, level, 10, 14)


def first_kernel(place_ref, own_ref, lo_ref, hi_ref, *refs):
    g_ref, load_ref, f_ref, e_ref = refs[10:14]
    level, (d_ref, v_ref, s_ref, x_ref, rest_ref, big_ref) = refs[14:21], refs[21:]
    inv_ref = level[6]
    spread_out(own_ref, lo_ref, hi_ref, (d_ref, v_ref, s_ref, load_ref))
    for first in (6, 15):
        stiffness(place_ref, d_ref, v_ref, s_ref, e_ref, f_ref, first, first + 3, 3)
    for first in (7, 14):
        prepare(e_ref, level, first, first + 3, 3)

    def start(i):
        for r in range(3):
            x_ref[r, i] = OMEGA * load_ref[i] * inv_ref[r, i]

    loop(7, 17, start)

    def leftover(i):
        for r in range(3):
            rest_ref[r, i - 8] = KEEP * load_ref[i] + pull(x_ref, i, r, level)

    loop(8, 16, leftover)
    source = lambda f, i: rest_ref[f, i - 8] if f < 3 else 0.25 * e_ref[f - 3, i]
    g_ref[...] = pool_own(source, 6, big_ref).reshape(6, 4, 8, 128)


def wide_kernel(place_ref, own_ref, lo_ref, hi_ref, *refs):
    load_ref, f_ref, e_ref = refs[10:13]
    level, (d_ref, v_ref, s_ref) = refs[13:20], refs[20:]
    spread_out(own_ref, lo_ref, hi_ref, (d_ref, v_ref, s_ref, load_ref))
    for first in (2, 18):
        stiffness(place_ref, d_ref, v_ref, s_ref, e_ref, None, first, first + 4)
    for first in (3, 17):
        prepare(e_ref, level, first, first + 4)


def mix_kernel(place_ref, c_ref, even_ref, odd_ref, *refs):
    out_ref = refs[-1]
    mine, even = place_ref[0] % 4, (place_ref[0] // 4) % 2 == 0
    for to in range(4):
        out_ref[to, 0] = c_ref[...]
        out_ref[to, 1] = jnp.where((mine > to) == even, odd_ref[...], even_ref[...])


def window(place_ref, c_ref, even_ref, odd_ref, mixed_ref, field):
    mine, even = place_ref[0] % 4, (place_ref[0] // 4) % 2 == 0
    pieces = []
    for b in range(9):
        source = mine + (b - 4)
        if b == 0:
            piece = jnp.where(even, odd_ref[field], even_ref[field])
        elif b == 4:
            piece = c_ref[field]
        elif b == 8:
            piece = jnp.where(even, even_ref[field], odd_ref[field])
        else:
            far = ((source < 0) | (source > 3)).astype(jnp.int32)
            piece = mixed_ref[(source + 4) % 4, far, field]
        pieces.append(piece)
    return jnp.concatenate(pieces, 0)


def second_kernel(place_ref, load_ref, *refs):
    level, (c_ref, even_ref, odd_ref, mixed_ref) = refs[:7], refs[7:11]
    one_ref, two_ref, three_ref, z0_ref, q0_ref, g_ref = refs[11:17]
    x_ref, y_ref, out1_ref, wide_ref, big_ref = refs[17:]
    diag_ref, inv_ref = level[5:]
    got = (place_ref, c_ref, even_ref, odd_ref, mixed_ref)
    levels = (one_ref, two_ref, three_ref)
    set_levels([window(*got, 3 + r) for r in range(3)], levels)
    coarse_all(levels, [window(*got, r) for r in range(3)], out1_ref, 13, 23)
    widen_into(out1_ref, 10, wide_ref)

    def start(i):
        for r in range(3):
            x_ref[r, i] = OMEGA * load_ref[i] * inv_ref[r, i] + widened(wide_ref, r, (i - 2) // 2, 10)

    loop(3, 21, start)

    def smooth(i):
        for r in range(3):
            near = load_ref[i] + pull(x_ref, i, r, level)
            z0_ref[r, i] = KEEP * x_ref[r, i] + OMEGA * near * inv_ref[r, i]

    loop(4, 20, smooth)

    def apply(i):
        for r in range(3):
            image = diag_ref[r, i] * z0_ref[r, i] - pull(z0_ref, i, r, level)
            q0_ref[r, i] = image
            y_ref[r, i] = OMEGA * image * inv_ref[r, i]

    loop(5, 19, apply)

    def leftover(i):
        for r in range(3):
            x_ref[r, i] = KEEP * q0_ref[r, i] + pull(y_ref, i, r, level)

    loop(8, 16, leftover)
    g_ref[...] = pool_own(lambda f, i: x_ref[f, i], 3, big_ref).reshape(3, 4, 8, 128)


def third_kernel(place_ref, load_ref, *refs):
    level, (one_ref, two_ref, three_ref, z0_ref, q0_ref, c_ref, even_ref, odd_ref, mixed_ref) = refs[:7], refs[7:16]
    w_ref, dots_ref, x_ref, out1_ref, wide_ref = refs[16:]
    diag_ref, inv_ref = level[5:]
    rhs1 = [window(place_ref, c_ref, even_ref, odd_ref, mixed_ref, r) for r in range(3)]
    coarse_all((one_ref, two_ref, three_ref), rhs1, out1_ref, 14, 22)
    widen_into(out1_ref, 8, wide_ref)

    def start(i):
        for r in range(3):
            x_ref[r, i] = OMEGA * q0_ref[r, i] * inv_ref[r, i] + widened(wide_ref, r, (i - 4) // 2, 8)

    loop(5, 19, start, 7)

    def smooth(i):
        for r in range(3):
            near = q0_ref[r, i] + pull(x_ref, i, r, level)
            w_ref[r, i] = KEEP * x_ref[r, i] + OMEGA * near * inv_ref[r, i]

    loop(6, 18, smooth, 6)

    def add(t, sums):
        sums = list(sums)
        for i in (8 + 2 * t, 9 + 2 * t):
            for r in range(3):
                image = (diag_ref[r, i] * w_ref[r, i] - pull(w_ref, i, r, level))[:, :128]
                b, z0, q0, w = load_ref[i, :, :128], z0_ref[r, i, :, :128], q0_ref[r, i, :, :128], w_ref[r, i, :, :128]
                for q, term in enumerate((b * z0, z0 * q0, b * w, q0 * w, w * image)):
                    sums[r * 5 + q] = sums[r * 5 + q] + (term[:8] + term[8:])
        return tuple(sums)

    sums = lax.fori_loop(0, 4, add, tuple(jnp.zeros((8, 128), F32) for _ in range(15)))
    lane = iota((1, 128), 1)
    row = jnp.zeros((1, 128), F32)
    for q, v in enumerate(sums):
        row = row + jnp.where(lane == q, jnp.sum(jnp.sum(v, 0, keepdims=True), 1, keepdims=True), 0.0)
    dots_ref[...] = jnp.broadcast_to(row[None], (16, 1, 128))


def sum_kernel(in_ref, out_ref):
    out_ref[...] = jnp.broadcast_to(jnp.sum(in_ref[...], 0, keepdims=True), (16, 1, 128))


def last_kernel(place_ref, f_ref, z0_ref, w_ref, dots_ref, sens_ref, comp_ref, u_ref, comb_ref):
    real = place_ref[2]
    totals = jnp.sum(dots_ref[...], 0)
    lane = iota((1, 128), 1)
    pick = lambda q: jnp.sum(jnp.where(lane == q, totals, 0.0), 1, keepdims=True)
    factors = []
    for r in range(3):
        bz, zq, bw, qw, wa = (pick(r * 5 + q) for q in range(5))
        a0 = bz / zq
        rz1 = bz - a0 * bw - a0 * zq + (a0 * a0) * qw
        grow = 1.0 + rz1 / bz
        a1 = rz1 / ((grow * grow) * zq - 2.0 * (a0 * grow) * qw + (a0 * a0) * wa)
        c0, c1 = a0 + a1 * grow, -(a1 * a0)
        factors.append((c0, c1))
        comp_ref[r] = jnp.sum(c0 * bz + c1 * bw)
    y = iota((16, 1), 0)
    low, high = (y >= 1).astype(F32), (y < 15).astype(F32)

    def state(i):
        for r in range(3):
            u_ref[r, i] = factors[r][0] * z0_ref[r, i] + factors[r][1] * w_ref[r, i]

    loop(6, 18, state)

    def energy(i):
        total = jnp.zeros((16, 256), F32)
        for r in range(3):
            u = u_ref[r, i]
            gaps = (
                u - u_ref[r, i - 1],
                u - u_ref[r, i + 1],
                u - low * rolled(u, 1, 0),
                u - high * rolled(u, -1, 0),
                u - rolled(u, 1, 1),
                u - rolled(u, -1, 1),
            )
            square = gaps[0] * gaps[0]
            for gap in gaps[1:]:
                square = square + gap * gap
            total = total - (0.5 * square) * f_ref[r, i]
        comb_ref[i] = total

    loop(7, 17, energy)

    def spread(i):
        c = comb_ref[i]
        total = 2.0 * c + comb_ref[i + 1] + comb_ref[i - 1]
        total = total + low * rolled(c, 1, 0) + high * rolled(c, -1, 0) + rolled(c, 1, 1) + rolled(c, -1, 1)
        sens_ref[i - 8] = jnp.where(real == 0, total[:8, :128], total[8:, :128])

    loop(8, 16, spread)


def call(body, outs, scratch, *args, place=False, flops=0, out_specs=None, aliases=None):
    if place:
        inner = body

        def body(*refs):
            return inner((lax.axis_index(X_AXES), lax.axis_index(Y_AXES), lax.axis_index("real")), *refs)

    if aliases:
        out_specs = (pl.BlockSpec(memory_space=pltpu.VMEM),) * len(outs)
    return pl.pallas_call(
        body,
        out_shape=outs,
        in_specs=[pl.BlockSpec(memory_space=pltpu.VMEM)] * len(args),
        **({} if out_specs is None else {"out_specs": out_specs}),
        input_output_aliases=aliases or {},
        scratch_shapes=[pltpu.VMEM(dims, F32) for dims in scratch],
        compiler_params=pltpu.CompilerParams(vmem_limit_bytes=VMEM_LIMIT),
        cost_estimate=pl.CostEstimate(flops=flops, bytes_accessed=0, transcendentals=0),
    )(*args)


Z_AXES = ("zh", "zl")
X_AXES = ("zh", "zl", "xc")
Y_AXES = ("yl", "core")
FIELD = (3, 24, 16, 256)
SLICES = (24, 16, 256)


def swap(to_even, to_odd, axes, count):
    got = []
    for first, v in ((0, to_even), (1, to_odd)):
        pairs = [(i, i + 1) for i in range(first, count - 1, 2)]
        got.append(lax.ppermute(v, axes, pairs + [(j, i) for i, j in pairs]))
    return got


def fetch(own, *after):
    even, odd = swap(own, own, Z_AXES, 16)
    mixed = call(mix_kernel, shaped(4, 2, *own.shape), [], own, even, odd, *after, place=True)
    return own, even, odd, lax.all_to_all(mixed, "xc", 0, 0)


def body(design, load, void_mask, solid_mask):
    which = iota((4, 8, 8, 128), 0)
    masks = jnp.where(which == 1, void_mask[None], solid_mask[None]).astype(F32)
    own = jnp.where(which == 0, design[None], jnp.where(which == 3, load[None], masks))
    both = lax.all_gather(own, "real")
    outs = (shaped(4, 8, 16, 256), shaped(*SENT), shaped(*SENT))
    halves = call(halve_kernel, (shaped(2, 4, 4, 8, 128),) * 2, [], both, place=True)
    mine, up, down = call(select_kernel, outs, [], both, *swap(*halves, Y_AXES, 4), place=True)
    lo = lax.ppermute(up, X_AXES, [(i, i + 1) for i in range(NBX - 1)])
    hi = lax.ppermute(down, X_AXES, [(i + 1, i) for i in range(NBX - 1)])
    fields = (shaped(*SLICES),) + (shaped(*FIELD),) * 9
    kept = call(inner_kernel, fields, [SLICES] * 3, mine, place=True, flops=10**7)
    g, *kept = call(
        first_kernel,
        (shaped(6, 4, 8, 128),) + fields,
        [SLICES] * 3 + [FIELD, (3, 8, 16, 256), (2, 384, 128)],
        mine, lo, hi, *kept, place=True, aliases={3 + q: 1 + q for q in range(10)},
    )
    wide_load, f, _, *level0 = call(
        wide_kernel,
        fields,
        [SLICES] * 3,
        mine, lo, hi, *kept, place=True, flops=2 * 10**7, aliases={3 + q: q for q in range(10)},
    )
    level0 = (wide_load, *level0)
    levels = tuple(shaped(7, 3, n, 8, 128) for n in (36, 18, 9))
    *levels, z0, q0, g2 = call(
        second_kernel,
        levels + (shaped(*FIELD), shaped(*FIELD), shaped(3, 4, 8, 128)),
        [FIELD, FIELD, (3, 10, 8, 128), (2, 480, 128), (2, 192, 128)],
        *level0, *fetch(g, level0[0]), place=True,
    )
    w, dots = call(
        third_kernel,
        (shaped(*FIELD), shaped(16, 1, 128)),
        [FIELD, (3, 8, 8, 128), (2, 384, 128)],
        *level0, *levels, z0, q0, *fetch(g2), place=True,
    )
    dots = lax.all_to_all(dots, ("xc", "yl", "core"), 0, 0, tiled=True)
    dots = call(sum_kernel, shaped(16, 1, 128), [], dots)
    dots = lax.all_to_all(dots, ("zh", "zl"), 0, 0, tiled=True)
    return call(
        last_kernel,
        (shaped(8, 8, 128), shaped(3)),
        [FIELD, SLICES],
        f, z0, w, dots, place=True,
        out_specs=(pl.BlockSpec(memory_space=pltpu.VMEM), pl.BlockSpec(memory_space=pltpu.SMEM)),
    )


def solution(mesh):
    split = Mesh(mesh.devices.reshape(2, 4, 4, 4, 2, 2), ("real", "zh", "zl", "xc", "yl", "core"))
    spec = P(X_AXES, "real", Y_AXES)
    return jax.shard_map(body, mesh=split, in_specs=(spec,) * 4, out_specs=(spec, P()), check_vma=False)
```
